32 devices in a mesh: section: 4 (over y, core), batch: 8 (over z, x).
Axes of the slice: x: 2, y: 2, z: 4, core: 2. Of those that a mesh axis runs over, the one named last changes fastest.
Arguments:
- inputs: bfloat16 [16, 256, 1024], P('batch'), may hold values from -6 to 6
- segments: int32 [16, 256], P('batch'), may hold values from 0 to 5, never falling along the last dimension, each value on 1 to 128 neighbouring positions
- timestep: int32 [16], P('batch'), may hold values from 0 to 4999
- weight_in: bfloat16 [4, 1024, 4096], P('section', 'batch'), as said below
- weight_out: bfloat16 [4, 4096, 1024], P('section', 'batch'), may hold values from -0.125 to 0.125
- vectors: bfloat16 [4, 7, 1024], P('section', None, 'batch'), as said below
- cotangent: bfloat16 [16, 256, 1024], P('batch'), may hold values from -6 to 6
Outputs:
- output: bfloat16 [16, 256, 1024], P('batch', 'section')
- input_grad: float32 [16, 256, 1024], P('batch', 'section')
- weight_in_grad: float32 [4, 1024, 4096], P('section', 'batch')
- weight_out_grad: float32 [4, 4096, 1024], P('section', 'batch')
- vectors_grad: float32 [4, 7, 1024], P('section', None, 'batch')
The draws below stay inside these ranges and needn't reach their ends.
Inputs may be any that keep to these rules, and one draw needn't show every extreme that they name: `segments`: segment numbers never fall along a sequence; a token attends only to tokens of its own sequence with the same segment number. `weight_in`: entries lie within 16 / sqrt(1024) of zero. `vectors`: entries lie within -4 and 4.
All inputs are finite; a program needn't handle non-finite values.
Results may differ from the reference program's by a relative error of at most 0.025.
Values may be sent and summed in bfloat16 or wider, within the bound.
No kernel may reach another device: no remote copies, remote signals or barrier semaphores. Data moves between devices by JAX's collectives and lax.ppermute only.
A program may use at most 192 MiB of HBM per device.

```python
import math
import jax
import jax.numpy as jnp
import numpy as np
from jax import lax

D = 1024
FF = 4096
HEADS = 16
HEAD_DIM = 64
LENGTH = 256
STEPS = 5000
SECTIONS = 4
SEQS = 16
N_SECTION = 4


def draw_weight_in(key, part):
    key = jax.random.fold_in(key, 11)
    standard = jax.random.truncated_normal(key, -4.0, 4.0, (SECTIONS, D, FF), jnp.float32)
    column_block = jnp.arange(FF) // D
    attention_factor = jnp.where(column_block == 3, 4.0, jnp.where(column_block == 2, 1.0, 1.2))
    section_kind = jnp.arange(SECTIONS) % 2
    factor = jnp.where(section_kind[:, None, None] == 0, attention_factor[None, None, :], 1.0)
    return (standard * factor / math.sqrt(D)).astype(jnp.bfloat16)


def draw_vectors(key, part):
    key = jax.random.fold_in(key, 23)
    standard = jax.random.truncated_normal(key, -4.0, 4.0, (SECTIONS, 7, D), jnp.float32)
    spread = jax.random.uniform(jax.random.fold_in(key, 5), (SECTIONS, 7, D), jnp.float32, -0.3, 0.3)
    row_index = jnp.arange(7)[None, :, None]
    section_kind = (jnp.arange(SECTIONS) % 2)[:, None, None]
    attention_rows = jnp.where(row_index == 2, 1.0, jnp.where(row_index == 4, 0.3, jnp.where(row_index == 6, 0.3, 0.5)))
    factor = jnp.where((section_kind == 1) & (row_index < 4), 0.5, attention_rows)
    return jnp.where(row_index == 5, 1.0 + spread, standard * factor).astype(jnp.bfloat16)


def set_ends(drawn, rng, low, largest):
    spot = [jax.random.randint(jax.random.fold_in(rng, axis), (), 0, length) for axis, length in enumerate(drawn.shape)]
    main_axis = drawn.shape.index(max(drawn.shape))
    neighbour = spot[:main_axis] + [(spot[main_axis] + 1) % drawn.shape[main_axis]] + spot[main_axis + 1:]
    return drawn.at[tuple(spot)].set(low).at[tuple(neighbour)].set(largest)


def block_scale(key, dims, pieces, smallest, largest):
    factor_of, own = 1.0, jax.random.fold_in(key, 6)
    for axis_at, parts in pieces:
        steps = jnp.exp(jax.random.uniform(jax.random.fold_in(own, axis_at), (parts,), jnp.float32, smallest / len(pieces), largest / len(pieces)))
        factor_of = factor_of * jnp.repeat(steps, dims[axis_at] // parts).reshape([-1 if axis == axis_at else 1 for axis in range(len(dims))])
    return factor_of


def split_up(count, total, bound, slope):
    weights = [(1 << 20) // math.isqrt(standing ** slope) + 1 for standing in range(2, count + 1)]
    surplus, given = total - bound - (count - 1), [1] * (count - 1)
    while surplus > 0:
        free = [i for i in range(count - 1) if given[i] < bound]
        mass, budget = sum([weights[i] for i in free]), surplus
        for i in free:
            extra = min(bound - given[i], max(1, budget * weights[i] // mass), surplus)
            given[i] = given[i] + extra
            surplus = surplus - extra
    return np.array([bound] + given)


def uneven(key, count, total, reach, skew):
    if count == 2:
        one = jax.random.randint(key, (), max(1, total - reach), min(reach, total - 1) + 1)
        return jnp.stack([one, total - one])
    sizes = jnp.asarray(split_up(count, total, reach, skew), jnp.int32)
    couples = (count - 1) // 2
    donor, sink = sizes[1:1 + 2 * couples:2], sizes[2:2 + 2 * couples:2]
    slack = jnp.minimum(donor - 1, reach - sink)
    moved = jax.random.randint(jax.random.fold_in(key, 1), (couples,), 0, 1 << 20) % (slack + 1)
    sizes = sizes.at[1:1 + 2 * couples:2].set(donor - moved).at[2:2 + 2 * couples:2].set(sink + moved)
    return sizes[jax.random.permutation(jax.random.fold_in(key, 2), count)]


def gaussian(own_key, dims, scale, most, split=(), held_as=jnp.bfloat16):
    values = scale * jax.random.normal(own_key, dims, jnp.float32)
    if split:
        values = values * block_scale(own_key, dims, split, -0.22, 0.18)
    return jnp.clip(values, -most, most).astype(held_as)


def setup_inputs(seed: int = 0) -> dict:
    seeds = jax.random.split(jax.random.key(seed), 8)
    return {
        "inputs": gaussian(seeds[0], (SEQS, LENGTH, D), 1.0, 6.0, ((0, 8),)),
        "segments": jax.vmap(lambda own: jnp.searchsorted(jnp.cumsum(uneven(own, 6, LENGTH, LENGTH // 2, 2)), jnp.arange(LENGTH), side="right"))(jax.random.split(seeds[1], SEQS)).reshape((SEQS, LENGTH)).astype(jnp.int32),
        "timestep": set_ends(jax.random.randint(seeds[2], (SEQS,), 0, STEPS), jax.random.fold_in(seeds[2], 1), 0, STEPS - 1).astype(jnp.int32),
        "weight_in": draw_weight_in(jax.random.fold_in(seeds[7], 71), 0),
        "weight_out": gaussian(seeds[4], (SECTIONS, FF, D), (FF // 2) ** -0.5, 0.125, ((0, 4), (1, 8))),
        "vectors": draw_vectors(jax.random.fold_in(seeds[7], 71), 0),
        "cotangent": gaussian(seeds[6], (SEQS, LENGTH, D), 1.0, 6.0, ((0, 8),)),
    }


@jax.custom_vjp
def low(v):
    return lax.optimization_barrier(v.astype(jnp.bfloat16)).astype(jnp.float32)

@jax.custom_vjp
def low_back(v):
    return v

def low_keep(v):
    return (low(v), None)

def low_pass(kept, grad):
    return (grad,)

def back_keep(v):
    return (v, None)

def back_low(kept, grad):
    return (low(grad),)
low.defvjp(low_keep, low_pass)
low_back.defvjp(back_keep, back_low)
highest = lax.Precision.HIGHEST
norm_eps = 1e-05
masked_score = -1e+30

def layer_norm(resid, ln_gain, ln_shift):
    average = lax.optimization_barrier(jnp.mean(resid, axis=-1, keepdims=True))
    centred = resid - average
    variance = lax.optimization_barrier(jnp.mean(centred * centred, axis=-1, keepdims=True))
    return centred * lax.rsqrt(variance + norm_eps) * ln_gain + ln_shift

def sequence_context(query, key_rows, value_rows, seg_seq):
    length, width = query.shape
    block_rows = min(512, length)
    key_heads = key_rows.reshape(length, HEADS, HEAD_DIM)
    value_heads = value_rows.reshape(length, HEADS, HEAD_DIM)
    query_blocks = query.reshape(length // block_rows, block_rows, HEADS, HEAD_DIM)
    seg_blocks = seg_seq.reshape(length // block_rows, block_rows)
    factor = 1.0 / math.sqrt(HEAD_DIM)

    def attend_block(items):
        query_block, seg_block = items
        scores = low_back(jnp.einsum('qhe,khe->hqk', query_block, key_heads, precision=highest) * factor)
        allowed = (seg_block[:, None] == seg_seq[None, :])[None]
        scores = jnp.where(allowed, scores, masked_score)
        peaks = lax.optimization_barrier(jnp.max(scores, axis=2, keepdims=True))
        exponent = jnp.exp(scores - peaks)
        weights = low(exponent / lax.optimization_barrier(jnp.sum(exponent, axis=2, keepdims=True)))
        return jnp.einsum('hqk,khe->qhe', weights, value_heads, precision=highest)
    contexts = lax.map(jax.checkpoint(attend_block), (query_blocks, seg_blocks))
    return contexts.reshape(length, width)

def attention_sublayer(hidden, first_matrix, vector_rows, seg_group):
    width = hidden.shape[-1]
    rounded = low(hidden)
    projected = jnp.einsum('gld,df->glf', rounded, first_matrix[:, :3 * width], precision=highest)
    query = low_back(low(projected[..., :width] + vector_rows[0]))
    key_rows = low_back(low(projected[..., width:2 * width]))
    value_rows = low_back(low(projected[..., 2 * width:] + vector_rows[1]))
    contexts = jax.vmap(sequence_context)(query, key_rows, value_rows, seg_group)
    context_low = low_back(low(contexts))
    branch = low_back(jnp.einsum('gld,de->gle', context_low, first_matrix[:, 3 * width:], precision=highest) + vector_rows[4])
    return low_back(low(layer_norm(hidden + branch, vector_rows[5], vector_rows[6])))

def feed_sublayer(hidden, first_matrix, second_matrix, vector_rows):
    width = hidden.shape[-1]
    rounded = low(hidden)
    upper = low_back(jnp.einsum('gld,df->glf', rounded, first_matrix, precision=highest) + vector_rows[0:4].reshape(4 * width))
    active = low(jax.nn.gelu(upper, approximate=False))
    branch = low_back(jnp.einsum('glf,fd->gld', active, second_matrix, precision=highest) + vector_rows[4])
    return low_back(low(layer_norm(hidden + branch, vector_rows[5], vector_rows[6])))

def stack_forward(first_all, second_all, vector_all, hidden_in, seg_group, time_group):
    time_scale = time_group.astype(jnp.float32) / STEPS
    hidden = hidden_in + time_scale[:, None, None] * vector_all[0, 2] + vector_all[0, 3]
    for section_index in range(N_SECTION):
        if section_index % 2 == 0:
            hidden = attention_sublayer(hidden, first_all[section_index], vector_all[section_index], seg_group)
        else:
            hidden = feed_sublayer(hidden, first_all[section_index], second_all[section_index], vector_all[section_index])
    return hidden

def grouped(values_in):
    return values_in.reshape((SEQS // 2, 2) + values_in.shape[1:])

def reference(inputs, segments, timestep, weight_in, weight_out, vectors, cotangent):
    first_all = weight_in.astype(jnp.float32)
    second_all = weight_out.astype(jnp.float32)
    vector_all = vectors.astype(jnp.float32)

    def group_step(carried, items):
        input_group, seg_group, time_group, cot_group = items

        def forward(first_w, second_w, vector_w, hidden_in):
            return stack_forward(first_w, second_w, vector_w, hidden_in, seg_group, time_group)
        result, pullback = jax.vjp(forward, first_all, second_all, vector_all, input_group.astype(jnp.float32))
        grads = pullback(cot_group.astype(jnp.float32))
        summed = (carried[0] + grads[0], carried[1] + grads[1], carried[2] + grads[2])
        return (summed, (result.astype(jnp.bfloat16), grads[3]))
    start = (jnp.zeros_like(first_all), jnp.zeros_like(second_all), jnp.zeros_like(vector_all))
    sums, (outputs, input_grads) = lax.scan(group_step, start, (grouped(inputs), grouped(segments), grouped(timestep), grouped(cotangent)))
    return (outputs.reshape(inputs.shape), input_grads.reshape(inputs.shape), sums[0], sums[1], sums[2])
```

```python
import functools
import math

import jax
import jax.numpy as jnp
from jax import lax
from jax.experimental import pallas as pl
from jax.experimental.pallas import tpu as pltpu
from jax.sharding import PartitionSpec as P

STEPS = 5000
SECTIONS = 4
BLOCKS = 8
LANES = 128
HEAD_DIM = 64

norm_eps = 1e-05
masked_score = -1e30
f32, bf16 = jnp.float32, jnp.bfloat16

VMEM = pl.BlockSpec(memory_space=pltpu.VMEM)
SMEM = pl.BlockSpec(memory_space=pltpu.SMEM)
ANY = pl.BlockSpec(memory_space=pl.ANY)


def dot_nn(a, b):
    return jnp.dot(a, b, preferred_element_type=f32)


def dot_nt(a, b):
    return lax.dot_general(a, b, (((1,), (1,)), ((), ())), preferred_element_type=f32)


def dot_tn(a, b):
    return lax.dot_general(a, b, (((0,), (0,)), ((), ())), preferred_element_type=f32)


def shape_of(dims, dtype):
    return jax.ShapeDtypeStruct(dims, dtype)


def kernel_call(body, in_specs, outs, args, scratch=(), flops=0, moved=0, limit=40):
    return pl.pallas_call(
        body,
        in_specs=in_specs,
        out_specs=[VMEM] * len(outs),
        out_shape=outs,
        scratch_shapes=list(scratch),
        compiler_params=pltpu.CompilerParams(vmem_limit_bytes=limit * 1024 * 1024),
        cost_estimate=pl.CostEstimate(flops=flops, bytes_accessed=moved, transcendentals=0),
    )(*args)


def block_copies(order, shards, first_row, rows, cols, target, sems, last):
    copies = []
    for j in range(BLOCKS - 1):
        copies.append(
            pltpu.make_async_copy(
                shards[j].at[pl.ds(first_row, rows), pl.ds(0, cols)],
                target.at[pl.ds(pl.multiple_of(order[j] * rows, rows), rows), :],
                sems.at[j],
            )
        )
    base = order[BLOCKS - 1] * rows
    at = BLOCKS - 1
    for piece, (offset, count) in last:
        copies.append(
            pltpu.make_async_copy(
                piece.at[pl.ds(0, count), pl.ds(0, cols)],
                target.at[pl.ds(pl.multiple_of(base + offset, count), count), :],
                sems.at[at],
            )
        )
        at += 1
    return copies


def start_all(copies):
    for copy in copies:
        copy.start()


def wait_all(copies):
    for copy in copies:
        copy.wait()


def attention_copies(order, shards, cols, target, sems):
    half = LANES // 2
    last = [(shards[7], (0, half)), (shards[8], (half, half))]
    return block_copies(order, shards, 0, LANES, cols, target, sems, last)


def feed_copies(order, shards, width, up, down, sems):
    first = block_copies(order, shards, 0, LANES, width, up, sems.at[0], [(shards[7], (0, LANES))])
    second = block_copies(
        order, shards, LANES, LANES, width, down, sems.at[1], [(shards[8], (0, LANES))]
    )
    return first, second


def lane_masks(rows):
    lane = lax.broadcasted_iota(jnp.int32, (rows, LANES), 1)
    return lane < HEAD_DIM, lane >= HEAD_DIM


def seq_rows(ref, seq, cols, half):
    top = ref[seq * LANES : (seq + 1) * LANES, cols]
    bottom = ref[half + seq * LANES : half + (seq + 1) * LANES, cols]
    return jnp.concatenate([top, bottom], axis=0)


def put_rows(ref, seq, cols, half, value):
    ref[seq * LANES : (seq + 1) * LANES, cols] = value[:LANES]
    ref[half + seq * LANES : half + (seq + 1) * LANES, cols] = value[LANES:]


def attend_kernel(order, own, peer, seg, bias, *refs):
    shards, (qkv, probs, ctx, x, w, sems) = refs[:9], refs[9:]
    half, width = own.shape
    seqs = half // LANES
    copies = attention_copies(order, shards, 3 * 256, w, sems)
    start_all(copies)
    x[:half] = own[...]
    x[half:] = peer[...]
    wait_all(copies)
    for i in range(3):
        cols = slice(256 * i, 256 * (i + 1))
        qkv[:, cols] = (dot_nn(x[...], w[:, cols]) + bias[:, cols]).astype(bf16)
    factor = 1.0 / math.sqrt(HEAD_DIM)
    masks = lane_masks(2 * LANES)
    for seq in range(seqs):
        key_seg = jnp.broadcast_to(seg[seq : seq + 1, :], (2 * LANES, 2 * LANES))
        allowed = key_seg == key_seg.T
        for group in range(2):
            q, k, v = [
                seq_rows(qkv, seq, slice(256 * i + LANES * group, 256 * i + LANES * (group + 1)), half)
                for i in range(3)
            ]
            parts = []
            for h in range(2):
                scores = dot_nt(jnp.where(masks[h], q, jnp.zeros_like(q)), k) * factor
                scores = jnp.where(allowed, scores, masked_score)
                peaks = jnp.max(scores, axis=1, keepdims=True)
                exponent = jnp.exp(scores - peaks)
                totals = jnp.sum(exponent, axis=1, keepdims=True)
                weights = exponent * (1.0 / totals)
                probs[(seq * 2 + group) * 2 + h] = weights
                parts.append(dot_nn(weights.astype(bf16), v))
            put_rows(
                ctx,
                seq,
                slice(LANES * group, LANES * (group + 1)),
                half,
                jnp.where(masks[0], parts[0], parts[1]).astype(bf16),
            )


def attend(order, own, peer, seg, bias, shards):
    half, width = own.shape
    seqs = half // LANES
    return kernel_call(
        attend_kernel,
        [SMEM] + [VMEM] * 4 + [ANY] * 9,
        [
            shape_of((2 * half, 768), bf16),
            shape_of((4 * seqs, 2 * LANES, 2 * LANES), f32),
            shape_of((2 * half, 256), bf16),
        ],
        (order, own, peer, seg, bias, *shards),
        [
            pltpu.VMEM((2 * half, width), bf16),
            pltpu.VMEM((width, 768), bf16),
            pltpu.SemaphoreType.DMA((9,)),
        ],
        flops=4 * half * width * 768,
        moved=8 << 20,
    )


def out_blocks(s):
    return slice(LANES * s, LANES * (s + 1)), slice(512 + LANES * s, 512 + LANES * (s + 1))


def project_kernel(ctx, wo, p_own, p_send):
    half = p_own.shape[0]
    for s in range(SECTIONS):
        result = dot_nn(ctx[...], wo[s].reshape(2 * LANES, 2 * LANES))
        for g, cols in enumerate(out_blocks(s)):
            part = result[:, LANES * g : LANES * (g + 1)]
            p_own[:, cols] = part[:half]
            p_send[:, cols] = part[half:].astype(bf16)


def project(ctx, wo, width):
    half = ctx.shape[0] // 2
    return kernel_call(
        project_kernel,
        [VMEM] * 2,
        [shape_of((half, width), f32), shape_of((half, width), bf16)],
        (ctx, wo),
        flops=4 * half * 256 * width,
        moved=3 << 20,
    )


def pack_kernel(order, *refs):
    shards, (packed, sems) = refs[:9], refs[9:]
    copies = []
    for j in range(7):
        b = order[j]
        copies.append(
            pltpu.make_async_copy(
                shards[j].at[:, pl.ds(768, 256)], packed.at[b % SECTIONS, b // SECTIONS], sems.at[j]
            )
        )
    b = order[7]
    half = LANES // 2
    for j in range(2):
        copies.append(
            pltpu.make_async_copy(
                shards[7 + j].at[:, pl.ds(768, 256)],
                packed.at[b % SECTIONS, b // SECTIONS, pl.ds(half * j, half)],
                sems.at[7 + j],
            )
        )
    start_all(copies)
    wait_all(copies)


def pack_out(order, shards):
    (packed,) = kernel_call(
        pack_kernel,
        [SMEM] + [ANY] * 9,
        [shape_of((SECTIONS, 2, LANES, 256), bf16)],
        (order, *shards),
        [pltpu.SemaphoreType.DMA((9,))],
        moved=1 << 20,
    )
    return packed


def out_grad_kernel(own, peer, ctx, packed):
    half = own.shape[0]
    for s in range(SECTIONS):
        cols = jnp.concatenate(
            [
                jnp.concatenate([own[:, c], peer[:, c]], axis=0)
                for c in out_blocks(s)
            ],
            axis=1,
        )
        packed[s] = dot_tn(ctx[...], cols).astype(bf16).reshape(2, LANES, 256)


def out_grad(own, peer, ctx):
    half, width = own.shape
    (packed,) = kernel_call(
        out_grad_kernel,
        [VMEM] * 3,
        [shape_of((SECTIONS, 2, LANES, 256), bf16)],
        (own, peer, ctx),
        flops=4 * half * 256 * width,
        moved=2 << 20,
    )
    return packed


def attend_back_kernel(order, own, peer, wo, qkv, probs, *refs):
    shards, (p_own, p_send, grads, sums, w, gctx, sems) = refs[:9], refs[9:]
    half, width = own.shape
    seqs = half // LANES
    copies = attention_copies(order, shards, 3 * 256, w, sems)
    start_all(copies)
    for part, rows in ((own, slice(0, half)), (peer, slice(half, 2 * half))):
        total = None
        for s in range(SECTIONS):
            cols = jnp.concatenate([part[:, c] for c in out_blocks(s)], axis=1)
            term = dot_nt(cols, wo[s].reshape(2 * LANES, 2 * LANES))
            total = term if total is None else total + term
        gctx[rows, :] = total.astype(bf16)
    factor = 1.0 / math.sqrt(HEAD_DIM)
    masks = lane_masks(2 * LANES)
    for seq in range(seqs):
        for group in range(2):
            lanes = slice(LANES * group, LANES * (group + 1))
            q, k, v = [
                seq_rows(qkv, seq, slice(256 * i + LANES * group, 256 * i + LANES * (group + 1)), half)
                for i in range(3)
            ]
            grad = seq_rows(gctx, seq, lanes, half)
            parts = []
            for h in range(2):
                weights = probs[(seq * 2 + group) * 2 + h]
                grad_probs = dot_nt(jnp.where(masks[h], grad, jnp.zeros_like(grad)), v)
                inner = jnp.sum(grad_probs * weights, axis=1, keepdims=True)
                grad_scores = (weights * (grad_probs - inner)).astype(bf16)
                parts.append(
                    (
                        dot_nn(grad_scores, k) * factor,
                        dot_tn(grad_scores, q) * factor,
                        dot_tn(weights.astype(bf16), grad),
                    )
                )
            for i in range(3):
                value = jnp.where(masks[0], parts[0][i], parts[1][i]).astype(bf16)
                put_rows(
                    grads,
                    seq,
                    slice(256 * i + LANES * group, 256 * i + LANES * (group + 1)),
                    half,
                    value,
                )
    sums[0:1, :] = jnp.sum(grads[...].astype(f32), axis=0, keepdims=True)
    wait_all(copies)
    for i in range(width // 256):
        cols = slice(256 * i, 256 * (i + 1))
        result = dot_nt(grads[...], w[cols, :])
        p_own[:, cols] = result[:half]
        p_send[:, cols] = result[half:].astype(bf16)


def attend_back(order, own, peer, wo, qkv, probs, shards):
    half, width = own.shape
    return kernel_call(
        attend_back_kernel,
        [SMEM] + [VMEM] * 5 + [ANY] * 9,
        [
            shape_of((half, width), f32),
            shape_of((half, width), bf16),
            shape_of((2 * half, 768), bf16),
            shape_of((8, 768), f32),
        ],
        (order, own, peer, wo, qkv, probs, *shards),
        [
            pltpu.VMEM((width, 768), bf16),
            pltpu.VMEM((2 * half, 256), bf16),
            pltpu.SemaphoreType.DMA((9,)),
        ],
        flops=4 * half * width * 1024,
        moved=8 << 20,
    )


def split_outputs(outs, j, row, value):
    if j == 4:
        outs[8 if row else 4][...] = value
    else:
        outs[j][row : row + LANES, :] = value


def pair_cols(parts, first, second):
    return jnp.concatenate(
        [
            jnp.concatenate([part[:, pl.ds(pl.multiple_of(b * LANES, LANES), LANES)] for b in (first, second)], axis=1)
            for part in parts
        ],
        axis=0,
    )


def attend_weight_kernel(slots, own, peer, grads, wo_grad, *outs):
    for j in range(0, BLOCKS, 2):
        first, second = slots[j], slots[j + 1]
        result = dot_tn(pair_cols((own, peer), first, second), grads[...]).astype(bf16)
        for i, b in enumerate((first, second)):
            slot = j + i
            rows = result[LANES * i : LANES * (i + 1)]
            tail = wo_grad[b % SECTIONS, b // SECTIONS]
            if slot == 4:
                mid = LANES // 2
                outs[4][:, :768], outs[4][:, 768:] = rows[:mid], tail[:mid]
                outs[8][:, :768], outs[8][:, 768:] = rows[mid:], tail[mid:]
            else:
                outs[slot][:, :768], outs[slot][:, 768:] = rows, tail


def chunk_shapes(rows, width):
    half = rows // 2
    return [shape_of((half if j in (4, 8) else rows, width), bf16) for j in range(9)]


def attend_weight(slots, own, peer, grads, wo_grad):
    half, width = own.shape
    return kernel_call(
        attend_weight_kernel,
        [SMEM] + [VMEM] * 4,
        chunk_shapes(LANES, width),
        (slots, own, peer, grads, wo_grad),
        flops=4 * half * width * 768,
        moved=5 << 20,
    )


def feed_kernel(order, own, peer, bias, *refs):
    shards, (p_own, p_send, active, slope, x, up, down, sems) = refs[:9], refs[9:]
    half, width = own.shape
    first, second = feed_copies(order, shards, width, up, down, sems)
    start_all(first)
    start_all(second)
    x[:half] = own[...]
    x[half:] = peer[...]
    wait_all(first)
    for i in range(width // 256):
        cols = slice(256 * i, 256 * (i + 1))
        upper = dot_nn(x[...], up[:, cols]) + bias[:, cols]
        cumulative = 0.5 * (1.0 + lax.erf(upper * (1.0 / math.sqrt(2.0))))
        density = jnp.exp(-0.5 * upper * upper) * (1.0 / math.sqrt(2.0 * math.pi))
        active[:, cols] = (upper * cumulative).astype(bf16)
        slope[:, cols] = cumulative + upper * density
    wait_all(second)
    for i in range(width // 256):
        cols = slice(256 * i, 256 * (i + 1))
        result = dot_nn(active[...], down[:, cols])
        p_own[:, cols] = result[:half]
        p_send[:, cols] = result[half:].astype(bf16)


def feed(order, own, peer, bias, shards):
    half, width = own.shape
    return kernel_call(
        feed_kernel,
        [SMEM] + [VMEM] * 3 + [ANY] * 9,
        [
            shape_of((half, width), f32),
            shape_of((half, width), bf16),
            shape_of((2 * half, width), bf16),
            shape_of((2 * half, width), f32),
        ],
        (order, own, peer, bias, *shards),
        [
            pltpu.VMEM((2 * half, width), bf16),
            pltpu.VMEM((width, width), bf16),
            pltpu.VMEM((width, width), bf16),
            pltpu.SemaphoreType.DMA((2, 9)),
        ],
        flops=8 * half * width * width,
        moved=10 << 20,
    )


def feed_back_kernel(order, own, peer, slope, *refs):
    shards, (p_own, p_send, grads, sums, g, up, down, sems) = refs[:9], refs[9:]
    half, width = own.shape
    first, second = feed_copies(order, shards, width, up, down, sems)
    start_all(second)
    start_all(first)
    g[:half] = own[...]
    g[half:] = peer[...]
    wait_all(second)
    for i in range(width // 256):
        cols = slice(256 * i, 256 * (i + 1))
        grad = (dot_nt(g[...], down[cols, :]) * slope[:, cols]).astype(bf16)
        grads[:, cols] = grad
        sums[0:1, cols] = jnp.sum(grad.astype(f32), axis=0, keepdims=True)
    wait_all(first)
    for i in range(width // 256):
        cols = slice(256 * i, 256 * (i + 1))
        result = dot_nt(grads[...], up[cols, :])
        p_own[:, cols] = result[:half]
        p_send[:, cols] = result[half:].astype(bf16)


def feed_back(order, own, peer, slope, shards):
    half, width = own.shape
    return kernel_call(
        feed_back_kernel,
        [SMEM] + [VMEM] * 3 + [ANY] * 9,
        [
            shape_of((half, width), f32),
            shape_of((half, width), bf16),
            shape_of((2 * half, width), bf16),
            shape_of((8, width), f32),
        ],
        (order, own, peer, slope, *shards),
        [
            pltpu.VMEM((2 * half, width), bf16),
            pltpu.VMEM((width, width), bf16),
            pltpu.VMEM((width, width), bf16),
            pltpu.SemaphoreType.DMA((2, 9)),
        ],
        flops=8 * half * width * width,
        moved=10 << 20,
    )


def feed_weight_kernel(slots, own, peer, grads, gown, gpeer, active, *outs):
    g = jnp.concatenate([gown[...], gpeer[...]], axis=0)
    for j in range(0, BLOCKS, 2):
        first, second = slots[j], slots[j + 1]
        up = dot_tn(pair_cols((own, peer), first, second), grads[...]).astype(bf16)
        down = dot_tn(pair_cols((active,), first, second), g).astype(bf16)
        for i in range(2):
            rows = slice(LANES * i, LANES * (i + 1))
            split_outputs(outs, j + i, 0, up[rows])
            split_outputs(outs, j + i, LANES, down[rows])


def feed_weight(slots, own, peer, grads, gown, gpeer, active):
    half, width = own.shape
    return kernel_call(
        feed_weight_kernel,
        [SMEM] + [VMEM] * 6,
        chunk_shapes(2 * LANES, width),
        (slots, own, peer, grads, gown, gpeer, active),
        flops=8 * half * width * width,
        moved=8 << 20,
    )


def norm_rows(resid):
    average = jnp.mean(resid, axis=1, keepdims=True)
    centred = resid - average
    variance = jnp.mean(centred * centred, axis=1, keepdims=True)
    inverse = lax.rsqrt(variance + norm_eps)
    return centred * inverse, inverse


def norm_back_rows(grad_out, normed, inverse, gain):
    scaled = grad_out * gain
    return inverse * (
        scaled
        - jnp.mean(scaled, axis=1, keepdims=True)
        - normed * jnp.mean(scaled * normed, axis=1, keepdims=True)
    )


def add_sums(sums, first, grad_branch, grad_out, normed):
    terms = [grad_branch.astype(f32), grad_out * normed, grad_out]
    for row, term in enumerate(terms):
        total = jnp.sum(term, axis=0, keepdims=True)
        sums[row : row + 1, :] = total if first else sums[row : row + 1, :] + total


def norm_kernel(prev, mine, theirs, tail, out, normed, inverse):
    step = LANES
    for r in range(prev.shape[0] // step):
        rows = slice(step * r, step * (r + 1))
        branch = mine[rows].astype(f32) + theirs[rows].astype(f32) + tail[0:1]
        value, inv = norm_rows(prev[rows].astype(f32) + branch)
        normed[rows] = value
        inverse[rows] = jnp.broadcast_to(inv, (step, LANES))
        out[rows] = (value * tail[1:2] + tail[2:3]).astype(bf16)


def norm(prev, mine, theirs, tail):
    half, width = prev.shape
    return kernel_call(
        norm_kernel,
        [VMEM] * 4,
        [shape_of((half, width), bf16), shape_of((half, width), f32), shape_of((half, LANES), f32)],
        (prev, mine, theirs, tail),
        flops=20 * half * width,
        moved=4 << 20,
    )


def turn_kernel(prev, mine, theirs, tail, cot, out, grad_resid, grad_branch, sums):
    step = LANES
    for r in range(prev.shape[0] // step):
        rows = slice(step * r, step * (r + 1))
        branch = mine[rows].astype(f32) + theirs[rows].astype(f32) + tail[0:1]
        value, inv = norm_rows(prev[rows].astype(f32) + branch)
        out[rows] = (value * tail[1:2] + tail[2:3]).astype(bf16)
        grad_out = cot[rows].astype(f32)
        grad = norm_back_rows(grad_out, value, inv, tail[1:2])
        low = grad.astype(bf16)
        grad_resid[rows] = grad
        grad_branch[rows] = low
        add_sums(sums, r == 0, low, grad_out, value)


def turn(prev, mine, theirs, tail, cot):
    half, width = prev.shape
    return kernel_call(
        turn_kernel,
        [VMEM] * 5,
        [
            shape_of((half, width), bf16),
            shape_of((half, width), f32),
            shape_of((half, width), bf16),
            shape_of((8, width), f32),
        ],
        (prev, mine, theirs, tail, cot),
        flops=40 * half * width,
        moved=5 << 20,
    )


def norm_back_kernel(above, mine, theirs, normed, inverse, tail, grad_resid, grad_branch, sums):
    step = LANES
    for r in range(above.shape[0] // step):
        rows = slice(step * r, step * (r + 1))
        grad_in = above[rows] + (mine[rows].astype(f32) + theirs[rows].astype(f32))
        grad_out = grad_in.astype(bf16).astype(f32)
        value = normed[rows]
        grad = norm_back_rows(grad_out, value, inverse[rows, 0:1], tail[1:2])
        low = grad.astype(bf16)
        grad_resid[rows] = grad
        grad_branch[rows] = low
        add_sums(sums, r == 0, low, grad_out, value)


def norm_back(above, mine, theirs, normed, inverse, tail):
    half, width = above.shape
    return kernel_call(
        norm_back_kernel,
        [VMEM] * 6,
        [shape_of((half, width), f32), shape_of((half, width), bf16), shape_of((8, width), f32)],
        (above, mine, theirs, normed, inverse, tail),
        flops=30 * half * width,
        moved=5 << 20,
    )


def over_section(value, r, sources=range(SECTIONS), targets=range(SECTIONS)):
    route = [(i, i ^ r) for i in range(SECTIONS) if i in sources and (i ^ r) in targets]
    return lax.ppermute(value, "section", route)


def ring_of(n):
    return list(range(0, n, 2)) + list(range(n - 1, 0, -2))


def around(value, way):
    ring = ring_of(lax.axis_size("batch"))
    n = len(ring)
    return lax.ppermute(value, "batch", [(ring[i], ring[(i + way) % n]) for i in range(n)])


def ring_gather(shard):
    out, right, left = [shard], shard, shard
    for _ in range(3):
        right, left = around(right, 1), around(left, -1)
        out += [right, left]
    mid = shard.shape[0] // 2
    return out + [around(right[:mid], 1), around(left[mid:], -1)]


def ring_reduce(chunks):
    mid = chunks[4].shape[0]
    right, left = around(chunks[4], 1), around(chunks[8], -1)
    right = jnp.concatenate([chunks[3][:mid] + right, chunks[3][mid:]], axis=0)
    left = jnp.concatenate([chunks[5][:mid], chunks[5][mid:] + left], axis=0)
    for i in range(2):
        right = around(right, 1) + chunks[2 - i]
        left = around(left, -1) + chunks[6 + i]
    right, left = around(right, 1), around(left, -1)
    return chunks[0].astype(f32) + right.astype(f32) + left.astype(f32)


def ring_tables():
    ring = ring_of(BLOCKS)
    place = [ring.index(b) for b in range(BLOCKS)]
    steps = [0, -1, 1, -2, 2, -3, 3, 4]
    order = [[ring[(place[b] + k) % BLOCKS] for k in steps] for b in range(BLOCKS)]
    slots = [[ring[(place[b] + j) % BLOCKS] for j in range(BLOCKS)] for b in range(BLOCKS)]
    return order, slots


def double_gather(value, axis, dim):
    size, index = lax.axis_size(axis), lax.axis_index(axis)
    step = 1
    while step < size:
        other = lax.ppermute(value, axis, [(i, i ^ step) for i in range(size)])
        lower = (index // step) % 2 == 0
        value = jnp.where(
            lower,
            jnp.concatenate([value, other], axis=dim),
            jnp.concatenate([other, value], axis=dim),
        )
        step *= 2
    return value


def halve_reduce(value, axis, dim):
    size, index = lax.axis_size(axis), lax.axis_index(axis)
    step = size // 2
    while step >= 1:
        low, high = jnp.split(value, 2, axis=dim)
        lower = (index // step) % 2 == 0
        send, keep = jnp.where(lower, high, low), jnp.where(lower, low, high)
        value = keep + lax.ppermute(send, axis, [(i, i ^ step) for i in range(size)])
        step //= 2
    return value


def spread(parts, section_id, first):
    stacked = parts
    sources = (first, first + 2)
    pieces = [lax.dynamic_index_in_dim(stacked, section_id, 0, keepdims=False)]
    for r in (1, 2, 3):
        piece = lax.dynamic_index_in_dim(stacked, section_id ^ r, 0, keepdims=False)
        pieces.append(over_section(piece, r, sources=sources))
    return [lax.select_n(section_id ^ k, *pieces) for k in sources]


def collect(values, section_id, targets):
    def pick(k):
        result = values[targets[0]]
        for t in targets[1:]:
            result = jnp.where(k == t, values[t], result)
        return result

    pieces = [pick(section_id)]
    for r in (1, 2, 3):
        pieces.append(over_section(pick(section_id ^ r), r, targets=targets))
    return [lax.select_n(section_id ^ s, *pieces) for s in range(SECTIONS)]


def local(inputs, segments, timestep, weight_in, weight_out, vectors, cotangent):
    section_id = lax.axis_index("section")
    batch_id = lax.axis_index("batch")
    batch = lax.axis_size("batch")
    ringed = batch == BLOCKS
    core_id = section_id % 2
    seqs, length, width = inputs.shape
    half = seqs * length // 2
    hidden_width = weight_in.shape[2]
    unit = hidden_width // batch // SECTIONS

    if ringed:
        order_table, slot_table = ring_tables()
        order = jnp.asarray(order_table, jnp.int32)[batch_id]
        slots = jnp.asarray(slot_table, jnp.int32)[batch_id]
    else:
        order = slots = jnp.arange(BLOCKS, dtype=jnp.int32)

    def halves(value):
        rest = value.shape[2:]
        split = value.reshape((seqs, 2, 2, length // 4) + rest)
        split = jnp.moveaxis(split, 2, 0)
        return split.reshape((2, seqs, length // 2) + rest)

    def own_half(value):
        return lax.dynamic_index_in_dim(value, core_id, 0, keepdims=False)

    def peer_half(value):
        return lax.dynamic_index_in_dim(value, 1 - core_id, 0, keepdims=False)

    rows = weight_in.shape[1]
    by_head = weight_in[0].reshape(rows, -1, SECTIONS, LANES).transpose(2, 0, 1, 3)
    by_head = by_head.reshape(SECTIONS, rows, width)
    if unit == LANES:
        by_unit = by_head
    else:
        by_unit = weight_in[0].reshape(rows, -1, SECTIONS, unit).transpose(2, 0, 1, 3)
        by_unit = by_unit.reshape(SECTIONS, rows, width)
    down_parts = weight_out[0].reshape(SECTIONS, unit, width)
    attn_shards = spread(by_head, section_id, 0)
    feed_shards = spread(jnp.concatenate([by_unit, down_parts], axis=1), section_id, 1)

    vector_full = double_gather(double_gather(vectors, "section", 0), "batch", 2).astype(f32)

    def gather_attn(shard):
        if ringed:
            return ring_gather(shard)
        full = lax.all_gather(shard, "batch", axis=0, tiled=True)
        blocks = list(full.reshape(BLOCKS, LANES, width))
        return blocks[:7] + [blocks[7][: LANES // 2], blocks[7][LANES // 2 :]]

    def gather_feed(shard):
        if ringed:
            return ring_gather(shard)
        up = lax.all_gather(shard[:rows], "batch", axis=0, tiled=True).reshape(BLOCKS, LANES, width)
        down = lax.all_gather(shard[rows:], "batch", axis=0, tiled=True).reshape(BLOCKS, LANES, width)
        blocks = [jnp.concatenate([up[j], down[j]], axis=0) for j in range(7)]
        return blocks + [up[7], down[7]]

    weights = [
        gather_attn(attn_shards[0]),
        gather_feed(feed_shards[0]),
        gather_attn(attn_shards[1]),
        gather_feed(feed_shards[1]),
    ]

    def head_slice(row):
        split = row.reshape(2, SECTIONS, LANES)
        return lax.dynamic_index_in_dim(split, section_id, 1, keepdims=False).reshape(1, 256)

    def unit_slice(four):
        split = four.reshape(-1, SECTIONS, unit)
        return lax.dynamic_index_in_dim(split, section_id, 1, keepdims=False).reshape(1, width)

    biases, tails = [], []
    for k in range(SECTIONS):
        v = vector_full[k]
        if k % 2 == 0:
            biases.append(
                jnp.concatenate([head_slice(v[0]), jnp.zeros((1, 256), f32), head_slice(v[1])], axis=1)
            )
        else:
            biases.append(unit_slice(v[0:4]))
        tails.append(jnp.concatenate([v[4:7], jnp.zeros((5, width), f32)], axis=0))

    scale = timestep.astype(f32) / STEPS
    split_inputs = halves(inputs)
    embedding = scale[:, None, None] * vector_full[0, 2] + vector_full[0, 3]
    hidden = (own_half(split_inputs).astype(f32) + embedding).reshape(half, width)
    own = hidden.astype(bf16)
    peer = (peer_half(split_inputs).astype(f32) + embedding).astype(bf16).reshape(half, width)
    split_segments = halves(segments)
    seg = jnp.concatenate([own_half(split_segments), peer_half(split_segments)], axis=1).astype(f32)
    cot = own_half(halves(cotangent)).reshape(half, width)

    def exchange(p_own, p_send):
        mine = (p_own + over_section(p_send, 1).astype(f32)).astype(bf16)
        return mine, over_section(mine, 2)

    def to_all(packed):
        return lax.all_to_all(packed, "section", 0, 0)

    saved = []
    prev = hidden
    for k in range(SECTIONS):
        if k % 2 == 0:
            wo = to_all(pack_out(order, weights[k]))
            qkv, probs, ctx = attend(order, own, peer, seg, biases[k], weights[k])
            p_own, p_send = project(ctx, wo, width)
            kept = (own, peer, wo, qkv, probs, ctx)
        else:
            p_own, p_send, active, slope = feed(order, own, peer, biases[k], weights[k])
            kept = (own, peer, active, slope)
        mine, theirs = exchange(p_own, p_send)
        if k < SECTIONS - 1:
            out, normed, inverse = norm(prev, mine, theirs, tails[k])
            saved.append((kept, normed, inverse))
            prev, own, peer = out, out, over_section(out, 1)
        else:
            out, grad_resid, grad_own, tail_sums = turn(prev, mine, theirs, tails[k], cot)
            saved.append((kept, None, None))

    pick_rows = lax.dynamic_index_in_dim(
        out.reshape(seqs, 2, length // 4, width), section_id // 2, 1, keepdims=False
    )

    shards, vector_terms = [None] * SECTIONS, [None] * SECTIONS
    for k in range(SECTIONS - 1, -1, -1):
        kept, _, _ = saved[k]
        grad_peer = over_section(grad_own, 1)
        if k % 2 == 0:
            own, peer, wo, qkv, probs, ctx = kept
            wo_grad = to_all(out_grad(grad_own, grad_peer, ctx))
            p_own, p_send, grads, sums = attend_back(
                order, grad_own, grad_peer, wo, qkv, probs, weights[k]
            )
            chunks = attend_weight(slots, own, peer, grads, wo_grad)

            def placed(piece):
                empty = jnp.zeros((2, SECTIONS, LANES), f32)
                piece = piece.reshape(2, 1, LANES)
                return lax.dynamic_update_slice_in_dim(empty, piece, section_id, 1).reshape(1, width)

            head = [placed(sums[0, :256]), placed(sums[0, 512:])]
        else:
            own, peer, active, slope = kept
            p_own, p_send, grads, sums = feed_back(order, grad_own, grad_peer, slope, weights[k])
            chunks = feed_weight(slots, own, peer, grads, grad_own, grad_peer, active)
            empty = jnp.zeros((width // unit, SECTIONS, unit), f32)
            piece = sums[0].reshape(width // unit, 1, unit)
            head = [lax.dynamic_update_slice_in_dim(empty, piece, section_id, 1).reshape(4, width)]
        shards[k] = chunks
        tail = 0.5 * tail_sums[:3]
        mine, theirs = exchange(p_own, p_send)
        if k > 0:
            _, normed, inverse = saved[k - 1]
            above = grad_resid
            grad_resid, grad_own, tail_sums = norm_back(
                above, mine, theirs, normed, inverse, tails[k - 1]
            )
            middle = [jnp.zeros((2, width), f32)] if k == 2 else []
        else:
            input_grad = grad_resid + (mine.astype(f32) + theirs.astype(f32))
            per_sequence = jnp.sum(input_grad.reshape(seqs, length // 2, width), axis=1)
            middle = [
                0.5 * jnp.sum(scale[:, None] * per_sequence, axis=0, keepdims=True),
                0.5 * jnp.sum(per_sequence, axis=0, keepdims=True),
            ]
        vector_terms[k] = jnp.concatenate(head + middle + [tail], axis=0)

    input_part = lax.dynamic_index_in_dim(
        input_grad.reshape(seqs, 2, length // 4, width), section_id // 2, 1, keepdims=False
    )

    def reduce_chunks(k):
        chunks = list(shards[k])
        if ringed:
            total = ring_reduce(chunks).astype(bf16)
            return (total, None) if k % 2 == 0 else (total[:rows], total[rows:])

        def scatter(parts):
            return lax.psum_scatter(
                jnp.concatenate(parts, axis=0), "batch", scatter_dimension=0, tiled=True
            )

        if k % 2 == 0:
            blocks = chunks[:4] + [chunks[4], chunks[8]] + chunks[5:8]
            return scatter(blocks), None
        up = [c[:LANES] for c in chunks[:4]] + [chunks[4]] + [c[:LANES] for c in chunks[5:8]]
        down = [c[LANES:] for c in chunks[:4]] + [chunks[8]] + [c[LANES:] for c in chunks[5:8]]
        return scatter(up), scatter(down)

    reduced = [None] * SECTIONS
    for k in range(SECTIONS - 1, -1, -1):
        reduced[k] = reduce_chunks(k)

    slices = collect([r[0] for r in reduced], section_id, list(range(SECTIONS)))
    first = jnp.stack([p.reshape(rows, -1, LANES) for p in slices], axis=2)
    first = first.reshape(rows, hidden_width)
    if unit != LANES:
        other = jnp.stack([p.reshape(rows, -1, unit) for p in slices], axis=2)
        first = jnp.where(section_id % 2 == 1, other.reshape(rows, hidden_width), first)
    second = jnp.stack(collect([r[1] for r in reduced], section_id, [1, 3]), axis=0)
    second = second.reshape(SECTIONS * unit, width).astype(f32)
    second = jnp.where(section_id % 2 == 1, second, 0.0)

    terms = jnp.stack(vector_terms)
    terms = halve_reduce(halve_reduce(terms, "section", 0), "batch", 2)
    return (pick_rows, input_part, first.astype(f32)[None], second[None], terms)


def solution(mesh):
    return jax.shard_map(
        local,
        mesh=mesh,
        in_specs=(
            P("batch", None, None),
            P("batch", None),
            P("batch"),
            P("section", "batch", None),
            P("section", "batch", None),
            P("section", None, "batch"),
            P("batch", None, None),
        ),
        out_specs=(
            P("batch", "section", None),
            P("batch", "section", None),
            P("section", "batch", None),
            P("section", "batch", None),
            P("section", None, "batch"),
        ),
        check_vma=False,
    )
```

```python
import functools
import math

import jax
import jax.numpy as jnp
from jax import lax
from jax.experimental import pallas as pl
from jax.experimental.pallas import tpu as pltpu
from jax.sharding import PartitionSpec as P

STEPS = 5000
SECTIONS = 4
BLOCKS = 8
LANES = 128
HEAD_DIM = 64

norm_eps = 1e-05
masked_score = -1e30
f32, bf16 = jnp.float32, jnp.bfloat16

VMEM = pl.BlockSpec(memory_space=pltpu.VMEM)
SMEM = pl.BlockSpec(memory_space=pltpu.SMEM)
ANY = pl.BlockSpec(memory_space=pl.ANY)
HBM = pl.BlockSpec(memory_space=pltpu.HBM)
KEEP = pl.BlockSpec()


def dot_nn(a, b):
    return jnp.dot(a, b, preferred_element_type=f32)


def dot_nt(a, b):
    return lax.dot_general(a, b, (((1,), (1,)), ((), ())), preferred_element_type=f32)


def dot_tn(a, b):
    return lax.dot_general(a, b, (((0,), (0,)), ((), ())), preferred_element_type=f32)


def shape_of(dims, dtype):
    return jax.ShapeDtypeStruct(dims, dtype)


def kept(dims, dtype):
    return pltpu.HBM(dims, dtype)


def kernel_call(body, in_specs, outs, args, scratch=(), limit=16, after=()):
    known, late = len(args), len(after)

    def run(*refs):
        body(*refs[:known], *refs[known + late :])

    args = [
        pltpu.with_memory_space_constraint(x, pltpu.HBM) if spec in (HBM, KEEP, SMEM) else x
        for x, spec in zip(args, in_specs)
    ]
    return pl.pallas_call(
        run,
        in_specs=[ANY if spec is HBM else spec for spec in in_specs] + [ANY] * late,
        out_specs=[VMEM if isinstance(o, jax.ShapeDtypeStruct) else KEEP for o in outs],
        out_shape=outs,
        scratch_shapes=list(scratch),
        compiler_params=pltpu.CompilerParams(vmem_limit_bytes=limit * 1024 * 1024),
        cost_estimate=pl.CostEstimate(flops=0, bytes_accessed=0, transcendentals=0),
        name=getattr(body, "func", body).__name__,
    )(*args, *after)


def block_copies(order, shards, first_row, rows, cols, target, sems, last):
    copies = []
    for j in range(BLOCKS - 1):
        copies.append(
            pltpu.make_async_copy(
                shards[j].at[pl.ds(first_row, rows), pl.ds(0, cols)],
                target.at[pl.ds(pl.multiple_of(order[j] * rows, rows), rows), :],
                sems.at[j],
            )
        )
    base = order[BLOCKS - 1] * rows
    at = BLOCKS - 1
    for piece, (offset, count) in last:
        copies.append(
            pltpu.make_async_copy(
                piece.at[pl.ds(0, count), pl.ds(0, cols)],
                target.at[pl.ds(pl.multiple_of(base + offset, count), count), :],
                sems.at[at],
            )
        )
        at += 1
    return copies


def start_all(copies):
    for copy in copies:
        copy.start()


def wait_all(copies):
    for copy in copies:
        copy.wait()


def attention_copies(order, shards, cols, target, sems):
    half = LANES // 2
    last = [(shards[7], (0, half)), (shards[8], (half, half))]
    return block_copies(order, shards, 0, LANES, cols, target, sems, last)


def feed_copies(order, shards, width, up, down, sems):
    first = block_copies(order, shards, 0, LANES, width, up, sems.at[0], [(shards[7], (0, LANES))])
    second = block_copies(
        order, shards, LANES, LANES, width, down, sems.at[1], [(shards[8], (0, LANES))]
    )
    return first, second


def lane_masks(rows):
    lane = lax.broadcasted_iota(jnp.int32, (rows, LANES), 1)
    return lane < HEAD_DIM, lane >= HEAD_DIM


def seq_rows(ref, seq, cols, half):
    top = ref[seq * LANES : (seq + 1) * LANES, cols]
    bottom = ref[half + seq * LANES : half + (seq + 1) * LANES, cols]
    return jnp.concatenate([top, bottom], axis=0)


def put_rows(ref, seq, cols, half, value):
    ref[seq * LANES : (seq + 1) * LANES, cols] = value[:LANES]
    ref[half + seq * LANES : half + (seq + 1) * LANES, cols] = value[LANES:]


def attend_kernel(k, order, own, peer, seg, bias, *refs):
    shards, (qkv, probs, ctx, ctx_kept, x, w, sems) = refs[:9], refs[9:]
    half, width = own.shape
    seqs = half // LANES
    copies = attention_copies(order, shards, 3 * 256, w, sems)
    start_all(copies)
    x[:half] = own[...]
    x[half:] = peer[...]
    wait_all(copies)
    for i in range(3):
        cols = slice(256 * i, 256 * (i + 1))
        qkv[:, cols] = (dot_nn(x[...], w[:, cols]) + bias[k : k + 1, cols]).astype(bf16)
    factor = 1.0 / math.sqrt(HEAD_DIM)
    masks = lane_masks(2 * LANES)
    for seq in range(seqs):
        key_seg = jnp.broadcast_to(seg[seq : seq + 1, :], (2 * LANES, 2 * LANES))
        allowed = key_seg == key_seg.T
        for group in range(2):
            q, k, v = [
                seq_rows(qkv, seq, slice(256 * i + LANES * group, 256 * i + LANES * (group + 1)), half)
                for i in range(3)
            ]
            parts = []
            for h in range(2):
                scores = dot_nt(jnp.where(masks[h], q, jnp.zeros_like(q)), k) * factor
                scores = jnp.where(allowed, scores, masked_score)
                peaks = jnp.max(scores, axis=1, keepdims=True)
                exponent = jnp.exp(scores - peaks)
                totals = jnp.sum(exponent, axis=1, keepdims=True)
                weights = exponent * (1.0 / totals)
                probs[(seq * 2 + group) * 2 + h] = weights
                parts.append(dot_nn(weights.astype(bf16), v))
            put_rows(
                ctx,
                seq,
                slice(LANES * group, LANES * (group + 1)),
                half,
                jnp.where(masks[0], parts[0], parts[1]).astype(bf16),
            )
    ctx_kept[...] = ctx[...]


def attend(k, order, own, peer, seg, bias, shards, after):
    half, width = own.shape
    seqs = half // LANES
    return kernel_call(
        functools.partial(attend_kernel, k),
        [SMEM] + [VMEM] * 2 + [KEEP] * 2 + [HBM] * 9,
        [
            kept((2 * half, 768), bf16),
            kept((4 * seqs, 2 * LANES, 2 * LANES), f32),
            shape_of((2 * half, 256), bf16),
            kept((2 * half, 256), bf16),
            kept((2 * half, width), bf16),
        ],
        (order, own, peer, seg, bias, *shards),
        [pltpu.VMEM((width, 768), bf16), pltpu.SemaphoreType.DMA((9,))],
        after=after,
    )


def out_blocks(s):
    return slice(LANES * s, LANES * (s + 1)), slice(512 + LANES * s, 512 + LANES * (s + 1))


def project_kernel(ctx, wo, p_own, p_send):
    half = p_own.shape[0]
    for s in range(SECTIONS):
        result = dot_nn(ctx[...], wo[s].reshape(2 * LANES, 2 * LANES))
        for g, cols in enumerate(out_blocks(s)):
            part = result[:, LANES * g : LANES * (g + 1)]
            p_own[:, cols] = part[:half]
            p_send[:, cols] = part[half:].astype(bf16)


def project(ctx, wo, width, after):
    half = ctx.shape[0] // 2
    return kernel_call(
        project_kernel,
        [VMEM, KEEP],
        [shape_of((half, width), f32), shape_of((half, width), bf16)],
        (ctx, wo),
        after=after,
    )


def pack_kernel(order, *refs):
    shards, (packed, sems) = refs[:9], refs[9:]
    copies = []
    for j in range(7):
        b = order[j]
        copies.append(
            pltpu.make_async_copy(
                shards[j].at[pl.ds(0, LANES), pl.ds(768, 256)], packed.at[b % SECTIONS, b // SECTIONS], sems.at[j]
            )
        )
    b = order[7]
    half = LANES // 2
    for j in range(2):
        copies.append(
            pltpu.make_async_copy(
                shards[7 + j].at[pl.ds(0, half), pl.ds(768, 256)],
                packed.at[b % SECTIONS, b // SECTIONS, pl.ds(half * j, half)],
                sems.at[7 + j],
            )
        )
    start_all(copies)
    wait_all(copies)


def pack_out(order, shards, after):
    (packed,) = kernel_call(
        pack_kernel,
        [SMEM] + [HBM] * 9,
        [shape_of((SECTIONS, 2, LANES, 256), bf16)],
        (order, *shards),
        [pltpu.SemaphoreType.DMA((9,))],
        after=after,
    )
    return packed


def out_grad_kernel(own, peer, ctx, packed):
    half = own.shape[0]
    for s in range(SECTIONS):
        cols = jnp.concatenate(
            [
                jnp.concatenate([own[:, c], peer[:, c]], axis=0)
                for c in out_blocks(s)
            ],
            axis=1,
        )
        packed[s] = dot_tn(ctx[...], cols).astype(bf16).reshape(2, LANES, 256)


def out_grad(own, peer, ctx, after):
    half, width = own.shape
    (packed,) = kernel_call(
        out_grad_kernel,
        [VMEM, VMEM, KEEP],
        [shape_of((SECTIONS, 2, LANES, 256), bf16)],
        (own, peer, ctx),
        after=after,
    )
    return packed


def attend_back_kernel(order, own, peer, wo, qkv, probs, *refs):
    shards, (p_own, p_send, grads, sums, w, gctx, sems) = refs[:9], refs[9:]
    half, width = own.shape
    seqs = half // LANES
    copies = attention_copies(order, shards, 3 * 256, w, sems)
    start_all(copies)
    for part, rows in ((own, slice(0, half)), (peer, slice(half, 2 * half))):
        total = None
        for s in range(SECTIONS):
            cols = jnp.concatenate([part[:, c] for c in out_blocks(s)], axis=1)
            term = dot_nt(cols, wo[s].reshape(2 * LANES, 2 * LANES))
            total = term if total is None else total + term
        gctx[rows, :] = total.astype(bf16)
    factor = 1.0 / math.sqrt(HEAD_DIM)
    masks = lane_masks(2 * LANES)
    for seq in range(seqs):
        for group in range(2):
            lanes = slice(LANES * group, LANES * (group + 1))
            q, k, v = [
                seq_rows(qkv, seq, slice(256 * i + LANES * group, 256 * i + LANES * (group + 1)), half)
                for i in range(3)
            ]
            grad = seq_rows(gctx, seq, lanes, half)
            parts = []
            for h in range(2):
                weights = probs[(seq * 2 + group) * 2 + h]
                grad_probs = dot_nt(jnp.where(masks[h], grad, jnp.zeros_like(grad)), v)
                inner = jnp.sum(grad_probs * weights, axis=1, keepdims=True)
                grad_scores = (weights * (grad_probs - inner)).astype(bf16)
                parts.append(
                    (
                        dot_nn(grad_scores, k) * factor,
                        dot_tn(grad_scores, q) * factor,
                        dot_tn(weights.astype(bf16), grad),
                    )
                )
            for i in range(3):
                value = jnp.where(masks[0], parts[0][i], parts[1][i]).astype(bf16)
                put_rows(
                    grads,
                    seq,
                    slice(256 * i + LANES * group, 256 * i + LANES * (group + 1)),
                    half,
                    value,
                )
    sums[0:1, :] = jnp.sum(grads[...].astype(f32), axis=0, keepdims=True)
    wait_all(copies)
    for i in range(width // 256):
        cols = slice(256 * i, 256 * (i + 1))
        result = dot_nt(grads[...], w[cols, :])
        p_own[:, cols] = result[:half]
        p_send[:, cols] = result[half:].astype(bf16)


def attend_back(order, own, peer, wo, qkv, probs, shards, after):
    half, width = own.shape
    return kernel_call(
        attend_back_kernel,
        [SMEM] + [VMEM] * 2 + [KEEP] * 3 + [HBM] * 9,
        [
            shape_of((half, width), f32),
            shape_of((half, width), bf16),
            shape_of((2 * half, 768), bf16),
            kept((8, 768), f32),
        ],
        (order, own, peer, wo, qkv, probs, *shards),
        [
            pltpu.VMEM((width, 768), bf16),
            pltpu.VMEM((2 * half, 256), bf16),
            pltpu.SemaphoreType.DMA((9,)),
        ],
        after=after,
    )


def split_outputs(outs, j, row, value):
    if j == 4:
        outs[8 if row else 4][...] = value
    else:
        outs[j][row : row + LANES, :] = value


def pair_cols(x, first, second):
    blocks = [x[:, pl.ds(pl.multiple_of(b * LANES, LANES), LANES)] for b in (first, second)]
    return jnp.concatenate(blocks, axis=1)


def attend_weight_kernel(joined, slots, x, grads, *refs):
    outs = refs[1:] if joined else refs
    mid = LANES // 2
    for j in range(0, BLOCKS, 2):
        first, second = slots[j], slots[j + 1]
        result = dot_tn(pair_cols(x, first, second), grads[...]).astype(bf16)
        for i, b in enumerate((first, second)):
            slot = j + i
            rows = result[LANES * i : LANES * (i + 1)]
            if slot == 4:
                outs[4][:, :768] = rows[:mid]
                outs[8][:, :768] = rows[mid:]
            else:
                outs[slot][:, :768] = rows
            if joined:
                tail = refs[0][b % SECTIONS, b // SECTIONS]
                if slot == 4:
                    outs[4][:, 768:] = tail[:mid]
                    outs[8][:, 768:] = tail[mid:]
                else:
                    outs[slot][:, 768:] = tail


def chunk_shapes(rows, width):
    half = rows // 2
    return [kept((half if j in (4, 8) else rows, width), bf16) for j in range(9)]


def attend_weight(slots, x, grads, wo_grad, after):
    return kernel_call(
        functools.partial(attend_weight_kernel, True),
        [SMEM, KEEP, VMEM, KEEP],
        chunk_shapes(LANES, x.shape[1]),
        (slots, x, grads, wo_grad),
        after=after,
    )


def feed_kernel(k, order, own, peer, bias, *refs):
    shards, (p_own, p_send, active, slope, x, up, down, sems) = refs[:9], refs[9:]
    half, width = own.shape
    first, second = feed_copies(order, shards, width, up, down, sems)
    start_all(first)
    start_all(second)
    x[:half] = own[...]
    x[half:] = peer[...]
    wait_all(first)
    for i in range(width // 256):
        cols = slice(256 * i, 256 * (i + 1))
        upper = dot_nn(x[...], up[:, cols]) + bias[k : k + 1, cols]
        cumulative = 0.5 * (1.0 + lax.erf(upper * (1.0 / math.sqrt(2.0))))
        density = jnp.exp(-0.5 * upper * upper) * (1.0 / math.sqrt(2.0 * math.pi))
        active[:, cols] = (upper * cumulative).astype(bf16)
        slope[:, cols] = cumulative + upper * density
    wait_all(second)
    for i in range(width // 256):
        cols = slice(256 * i, 256 * (i + 1))
        result = dot_nn(active[...], down[:, cols])
        p_own[:, cols] = result[:half]
        p_send[:, cols] = result[half:].astype(bf16)


def feed(k, order, own, peer, bias, shards, after):
    half, width = own.shape
    return kernel_call(
        functools.partial(feed_kernel, k),
        [SMEM] + [VMEM] * 2 + [KEEP] + [HBM] * 9,
        [
            shape_of((half, width), f32),
            shape_of((half, width), bf16),
            kept((2 * half, width), bf16),
            kept((2 * half, width), f32),
            kept((2 * half, width), bf16),
        ],
        (order, own, peer, bias, *shards),
        [
            pltpu.VMEM((width, width), bf16),
            pltpu.VMEM((width, width), bf16),
            pltpu.SemaphoreType.DMA((2, 9)),
        ],
        after=after,
    )


def feed_back_kernel(order, own, peer, slope, *refs):
    shards, (p_own, p_send, grads, sums, g, up, down, sems) = refs[:9], refs[9:]
    half, width = own.shape
    first, second = feed_copies(order, shards, width, up, down, sems)
    start_all(second)
    start_all(first)
    g[:half] = own[...]
    g[half:] = peer[...]
    wait_all(second)
    for i in range(width // 256):
        cols = slice(256 * i, 256 * (i + 1))
        grad = (dot_nt(g[...], down[cols, :]) * slope[:, cols]).astype(bf16)
        grads[:, cols] = grad
        sums[0:1, cols] = jnp.sum(grad.astype(f32), axis=0, keepdims=True)
    wait_all(first)
    for i in range(width // 256):
        cols = slice(256 * i, 256 * (i + 1))
        result = dot_nt(grads[...], up[cols, :])
        p_own[:, cols] = result[:half]
        p_send[:, cols] = result[half:].astype(bf16)


def feed_back(order, own, peer, slope, shards, after):
    half, width = own.shape
    return kernel_call(
        feed_back_kernel,
        [SMEM] + [VMEM] * 2 + [KEEP] + [HBM] * 9,
        [
            shape_of((half, width), f32),
            shape_of((half, width), bf16),
            shape_of((2 * half, width), bf16),
            kept((8, width), f32),
        ],
        (order, own, peer, slope, *shards),
        [
            pltpu.VMEM((2 * half, width), bf16),
            pltpu.VMEM((width, width), bf16),
            pltpu.VMEM((width, width), bf16),
            pltpu.SemaphoreType.DMA((2, 9)),
        ],
        after=after,
    )


def feed_weight_kernel(slots, x, grads, gown, gpeer, active, *outs):
    g = jnp.concatenate([gown[...], gpeer[...]], axis=0)
    for j in range(0, BLOCKS, 2):
        first, second = slots[j], slots[j + 1]
        up = dot_tn(pair_cols(x, first, second), grads[...]).astype(bf16)
        down = dot_tn(pair_cols(active, first, second), g).astype(bf16)
        for i in range(2):
            rows = slice(LANES * i, LANES * (i + 1))
            split_outputs(outs, j + i, 0, up[rows])
            split_outputs(outs, j + i, LANES, down[rows])


def feed_weight(slots, x, grads, gown, gpeer, active, after):
    return kernel_call(
        feed_weight_kernel,
        [SMEM, KEEP, VMEM, VMEM, VMEM, KEEP],
        chunk_shapes(2 * LANES, x.shape[1]),
        (slots, x, grads, gown, gpeer, active),
        after=after,
        limit=20,
    )


def norm_rows(resid):
    average = jnp.mean(resid, axis=1, keepdims=True)
    centred = resid - average
    variance = jnp.mean(centred * centred, axis=1, keepdims=True)
    inverse = lax.rsqrt(variance + norm_eps)
    return centred * inverse, inverse


def norm_back_rows(grad_out, normed, inverse, gain):
    scaled = grad_out * gain
    return inverse * (
        scaled
        - jnp.mean(scaled, axis=1, keepdims=True)
        - normed * jnp.mean(scaled * normed, axis=1, keepdims=True)
    )


def add_sums(sums, first, grad_branch, grad_out, normed):
    terms = [grad_branch.astype(f32), grad_out * normed, grad_out]
    for row, term in enumerate(terms):
        total = jnp.sum(term, axis=0, keepdims=True)
        sums[row : row + 1, :] = total if first else sums[row : row + 1, :] + total


def norm_kernel(k, prev, mine, theirs, tails, out, normed, inverse):
    step = LANES
    tail = tails[k]
    for r in range(mine.shape[0] // step):
        rows = slice(step * r, step * (r + 1))
        branch = mine[rows].astype(f32) + theirs[rows].astype(f32) + tail[0:1]
        value, inv = norm_rows(prev[rows].astype(f32) + branch)
        normed[rows] = value
        inverse[rows] = jnp.broadcast_to(inv, (step, LANES))
        out[rows] = (value * tail[1:2] + tail[2:3]).astype(bf16)


def norm(k, prev, mine, theirs, tails, after):
    half, width = mine.shape
    return kernel_call(
        functools.partial(norm_kernel, k),
        [KEEP, VMEM, VMEM, KEEP],
        [shape_of((half, width), bf16), kept((half, width), f32), kept((half, LANES), f32)],
        (prev, mine, theirs, tails),
        after=after,
    )


def turn_kernel(k, ids, prev, mine, theirs, tails, cot, picked, grad_resid, grad_branch, sums, out):
    step = LANES
    tail = tails[k]
    for r in range(mine.shape[0] // step):
        rows = slice(step * r, step * (r + 1))
        branch = mine[rows].astype(f32) + theirs[rows].astype(f32) + tail[0:1]
        value, inv = norm_rows(prev[rows].astype(f32) + branch)
        out[rows] = (value * tail[1:2] + tail[2:3]).astype(bf16)
        grad_out = cot[rows].astype(f32)
        grad = norm_back_rows(grad_out, value, inv, tail[1:2])
        low = grad.astype(bf16)
        grad_resid[rows] = grad
        grad_branch[rows] = low
        add_sums(sums, r == 0, low, grad_out, value)
    pick_rows(ids, out, picked)


def pick_rows(ids, value, picked):
    count = picked.shape[1]
    for seq in range(picked.shape[0]):
        start = pl.multiple_of(2 * count * seq + count * (ids[0] // 2), count)
        picked[seq] = value[pl.ds(start, count), :]


def turn(k, ids, prev, mine, theirs, tails, cot, seqs, after):
    half, width = mine.shape
    return kernel_call(
        functools.partial(turn_kernel, k),
        [SMEM, KEEP, VMEM, VMEM, KEEP, KEEP],
        [
            kept((seqs, half // seqs // 2, width), bf16),
            kept((half, width), f32),
            shape_of((half, width), bf16),
            kept((8, width), f32),
        ],
        (ids, prev, mine, theirs, tails, cot),
        [pltpu.VMEM((half, width), bf16)],
        after=after,
    )


def norm_back_kernel(k, above, mine, theirs, normed, inverse, tails, grad_resid, grad_branch, sums):
    step = LANES
    tail = tails[k]
    for r in range(above.shape[0] // step):
        rows = slice(step * r, step * (r + 1))
        grad_in = above[rows] + (mine[rows].astype(f32) + theirs[rows].astype(f32))
        grad_out = grad_in.astype(bf16).astype(f32)
        value = normed[rows]
        grad = norm_back_rows(grad_out, value, inverse[rows, 0:1], tail[1:2])
        low = grad.astype(bf16)
        grad_resid[rows] = grad
        grad_branch[rows] = low
        add_sums(sums, r == 0, low, grad_out, value)


def norm_back(k, above, mine, theirs, normed, inverse, tails, after):
    half, width = above.shape
    return kernel_call(
        functools.partial(norm_back_kernel, k),
        [KEEP, VMEM, VMEM, KEEP, KEEP, KEEP],
        [kept((half, width), f32), shape_of((half, width), bf16), kept((8, width), f32)],
        (above, mine, theirs, normed, inverse, tails),
        after=after,
    )


def finish_kernel(ids, scale, above, mine, theirs, picked, sums, grad_in):
    count = picked.shape[0]
    rows_each = above.shape[0] // count
    total, scaled = None, None
    for seq in range(count):
        rows = slice(rows_each * seq, rows_each * (seq + 1))
        value = above[rows] + (mine[rows].astype(f32) + theirs[rows].astype(f32))
        grad_in[rows] = value
        part = jnp.sum(value, axis=0, keepdims=True)
        total = part if total is None else total + part
        scaled = part * scale[seq] if scaled is None else scaled + part * scale[seq]
    sums[0:1] = scaled
    sums[1:2] = total
    pick_rows(ids, grad_in, picked)


def finish(ids, scale, above, mine, theirs):
    half, width = above.shape
    seqs = scale.shape[0]
    return kernel_call(
        finish_kernel,
        [SMEM] * 2 + [KEEP, VMEM, VMEM],
        [kept((seqs, half // seqs // 2, width), f32), kept((8, width), f32)],
        (ids, scale, above, mine, theirs),
        [pltpu.VMEM((half, width), f32)],
    )


def join_kernel(own, other, out):
    out[...] = (own[...] + other[...].astype(f32)).astype(bf16)


def join(own, other, after):
    (out,) = kernel_call(
        join_kernel, [VMEM] * 2, [shape_of(own.shape, bf16)], (own, other), after=after
    )
    return out


def prepare_kernel(ids, scale, inputs, cot, vec, hidden, own, peer, cot_own, tails, bias):
    section = ids[0]
    core = section % 2
    seqs, length, width = inputs.shape
    quarter = length // 4
    mul, add = vec[0, 2:3, :], vec[0, 3:4, :]
    for seq in range(seqs):
        embedding = scale[seq] * mul + add
        for y in range(2):
            at = slice((2 * seq + y) * quarter, (2 * seq + y + 1) * quarter)
            mine = pl.ds(pl.multiple_of((2 * y + core) * quarter, quarter), quarter)
            other = pl.ds(pl.multiple_of((2 * y + 1 - core) * quarter, quarter), quarter)
            value = inputs[seq, mine, :].astype(f32) + embedding
            hidden[at] = value
            own[at] = value.astype(bf16)
            peer[at] = (inputs[seq, other, :].astype(f32) + embedding).astype(bf16)
            cot_own[at] = cot[seq, mine, :]
    for k in range(SECTIONS):
        tails[k, 0:3, :] = vec[k, 4:7, :]
        if k % 2 == 0:
            bias[k : k + 1, :] = jnp.zeros((1, width), f32)
            for g in range(2):
                cols = pl.ds(pl.multiple_of(512 * g + LANES * section, LANES), LANES)
                for i in range(2):
                    at = 512 * i + LANES * g
                    bias[k : k + 1, at : at + LANES] = vec[k, i : i + 1, cols]
        else:
            for g in range(8):
                cols = pl.ds(pl.multiple_of(512 * (g % 2) + LANES * section, LANES), LANES)
                bias[k : k + 1, LANES * g : LANES * (g + 1)] = vec[k, g // 2 : g // 2 + 1, cols]


def prepare(ids, scale, inputs, cot, vec, after):
    seqs, length, width = inputs.shape
    half = seqs * length // 2
    return kernel_call(
        prepare_kernel,
        [SMEM] * 2 + [KEEP] * 3,
        [
            kept((half, width), f32),
            shape_of((half, width), bf16),
            shape_of((half, width), bf16),
            kept((half, width), bf16),
            kept((SECTIONS, 8, width), f32),
            kept((SECTIONS, width), f32),
        ],
        (ids, scale, inputs, cot, vec),
        after=after,
    )


def open_kernel(order, *refs):
    shards, (vec, parts, sems) = refs[:8], refs[8:]
    copies = []
    for j in range(BLOCKS):
        first = LANES if j < BLOCKS - 1 else LANES // 2
        copies.append(
            pltpu.make_async_copy(shards[j].at[pl.ds(first, 16), :], parts.at[j], sems.at[j])
        )
    start_all(copies)
    wait_all(copies)
    for j in range(BLOCKS):
        value = parts[j].astype(f32)
        cols = pl.ds(pl.multiple_of(order[j] * LANES, LANES), LANES)
        for k in range(SECTIONS):
            for i in range(7):
                vec[k, i : i + 1, cols] = value[k : k + 1, LANES * i : LANES * (i + 1)]


def open_vectors(order, shards, after):
    width = shards[0].shape[1]
    (vec,) = kernel_call(
        open_kernel,
        [SMEM] + [HBM] * 8,
        [kept((SECTIONS, 8, width), f32)],
        (order, *shards[:7], shards[8]),
        [pltpu.VMEM((BLOCKS, 16, width), bf16), pltpu.SemaphoreType.DMA((BLOCKS,))],
        after=after,
    )
    return vec


def terms_kernel(ids, time_sums, *refs):
    heads, tails, terms = refs[:4], refs[4:8], refs[8]
    section = ids[0]
    terms[...] = jnp.zeros_like(terms)
    for k in range(SECTIONS):
        if k % 2 == 0:
            for g in range(2):
                cols = pl.ds(pl.multiple_of(512 * g + LANES * section, LANES), LANES)
                for i in range(2):
                    at = 512 * i + LANES * g
                    terms[k, i : i + 1, cols] = heads[k][0:1, at : at + LANES]
        else:
            for g in range(8):
                cols = pl.ds(pl.multiple_of(512 * (g % 2) + LANES * section, LANES), LANES)
                row = g // 2
                terms[k, row : row + 1, cols] = heads[k][0:1, LANES * g : LANES * (g + 1)]
        terms[k, 4:7, :] = 0.5 * tails[k][0:3, :]
    terms[0, 2:4, :] = 0.5 * time_sums[0:2, :]


def vector_terms(ids, time_sums, heads, tails):
    width = time_sums.shape[1]
    (terms,) = kernel_call(
        terms_kernel,
        [SMEM] + [KEEP] * 9,
        [shape_of((SECTIONS, 7, width), f32)],
        (ids, time_sums, *heads, *tails),
    )
    return terms


def cut_kernel(kind, ids, first, second, *outs):
    sems = outs[4]
    section = ids[0]
    rows = first.shape[0]

    @pl.when(section % 2 == kind)
    def _():
        copies = []
        for r in range(SECTIONS):
            at = section ^ r
            for g in range(8):
                cols = pl.ds(pl.multiple_of(512 * g + LANES * at, LANES), LANES)
                copies.append(
                    pltpu.make_async_copy(
                        first.at[:, cols],
                        outs[r].at[pl.ds(0, rows), pl.ds(LANES * g, LANES)],
                        sems.at[r, g],
                    )
                )
            if kind:
                piece = pl.ds(pl.multiple_of(LANES * at, LANES), LANES)
                copies.append(
                    pltpu.make_async_copy(
                        second.at[piece, :], outs[r].at[pl.ds(rows, LANES), :], sems.at[r, 8]
                    )
                )
        start_all(copies)
        wait_all(copies)


def cut(kind, ids, first, second, after):
    rows, width = first.shape[0], second.shape[1]
    return kernel_call(
        functools.partial(cut_kernel, kind),
        [SMEM] + [HBM] * 2,
        [shape_of((rows + LANES * kind, width), bf16)] * 4,
        (ids, first, second),
        [pltpu.SemaphoreType.DMA((SECTIONS, 9))],
        after=after,
    )


def choose_kernel(base, joined, ids, *refs):
    pieces, refs = refs[:4], refs[4:]
    vectors, refs = (refs[0], refs[1:]) if joined else (None, refs)
    outs, sems = refs[:2], refs[2]
    rows = pieces[0].shape[0]
    for i in range(2):
        at = ids[0] ^ (base + 2 * i)
        for r in range(SECTIONS):

            @pl.when(at == r)
            def _():
                target = outs[i].at[pl.ds(0, rows), :]
                pltpu.make_async_copy(pieces[r], target, sems.at[i]).start()

    if joined:
        width = outs[0].shape[1]
        value = vectors[...].astype(f32)
        lines = [
            jnp.concatenate(
                [value[k, i : i + 1, :] for i in range(7)] + [jnp.zeros((1, width - 7 * LANES), f32)],
                axis=1,
            )
            for k in range(SECTIONS)
        ]
        lines.append(jnp.zeros((16 - SECTIONS, width), f32))
        outs[0][rows:, :] = jnp.concatenate(lines, axis=0).astype(bf16)

    for i in range(2):
        target = outs[i].at[pl.ds(0, rows), :]
        pltpu.make_async_copy(pieces[0], target, sems.at[i]).wait()


def choose(ids, base, pieces, vectors, after):
    rows, width = pieces[0].shape
    joined = vectors is not None
    return kernel_call(
        functools.partial(choose_kernel, base, joined),
        [SMEM] + [ANY] * 4 + [VMEM] * joined,
        [shape_of((rows + 16 * joined, width), bf16), shape_of((rows, width), bf16)],
        (ids, *pieces) + ((vectors,) if joined else ()),
        [pltpu.SemaphoreType.DMA((2,))],
        after=after,
    )


def step_kernel(kind, right, left, ahead, behind, *outs):
    if kind == "last":
        total = ahead[...].astype(f32) + right[...].astype(f32) + left[...].astype(f32)
        outs[0][...] = total.astype(bf16)
    elif kind == "first":
        mid = right.shape[0]
        outs[0][:mid] = ahead[:mid] + right[...]
        outs[0][mid:] = ahead[mid:]
        outs[1][:mid] = behind[:mid]
        outs[1][mid:] = behind[mid:] + left[...]
    else:
        outs[0][...] = ahead[...] + right[...]
        outs[1][...] = behind[...] + left[...]


def ring_step(kind, right, left, ahead, behind, after):
    count = 1 if kind == "last" else 2
    return kernel_call(
        functools.partial(step_kernel, kind),
        [VMEM, VMEM, KEEP, KEEP],
        [shape_of(ahead.shape, bf16)] * count,
        (right, left, ahead, behind),
        after=after,
    )


def over_section(value, r, sources=range(SECTIONS), targets=range(SECTIONS)):
    route = [(i, i ^ r) for i in range(SECTIONS) if i in sources and (i ^ r) in targets]
    return lax.ppermute(value, "section", route)


def ring_of(n):
    return list(range(0, n, 2)) + list(range(n - 1, 0, -2))


def around(value, way):
    ring = ring_of(lax.axis_size("batch"))
    n = len(ring)
    return lax.ppermute(value, "batch", [(ring[i], ring[(i + way) % n]) for i in range(n)])


def ring_gather(shard, name):
    with jax.named_scope(name):
        return ring_gather_steps(shard)


def ring_gather_steps(shard):
    out, right, left = [shard], shard, shard
    for _ in range(3):
        right, left = around(right, 1), around(left, -1)
        out += [right, left]
    mid = shard.shape[0] // 32 * 16
    return out + [around(right[:mid], 1), around(left[mid:], -1)]


class Reduction:
    def __init__(self, chunks, name):
        self.chunks, self.name, self.at = chunks, name, 0
        self.sending = (chunks[4], chunks[8])

    def step(self, after):
        chunks, at = self.chunks, self.at
        with jax.named_scope(self.name):
            right, left = around(self.sending[0], 1), around(self.sending[1], -1)
            kind = ("first", "middle", "middle", "last")[at]
            ahead, behind = ((3, 5), (2, 6), (1, 7), (0, 0))[at]
            self.sending = tuple(
                ring_step(kind, right, left, chunks[ahead], chunks[behind], tuple(after))
            )
        self.at += 1
        return self.sending


def ring_tables():
    ring = ring_of(BLOCKS)
    place = [ring.index(b) for b in range(BLOCKS)]
    steps = [0, -1, 1, -2, 2, -3, 3, 4]
    order = [[ring[(place[b] + k) % BLOCKS] for k in steps] for b in range(BLOCKS)]
    slots = [[ring[(place[b] + j) % BLOCKS] for j in range(BLOCKS)] for b in range(BLOCKS)]
    return order, slots


def double_gather(value, axis, dim):
    size, index = lax.axis_size(axis), lax.axis_index(axis)
    step = 1
    while step < size:
        other = lax.ppermute(value, axis, [(i, i ^ step) for i in range(size)])
        lower = (index // step) % 2 == 0
        value = jnp.where(
            lower,
            jnp.concatenate([value, other], axis=dim),
            jnp.concatenate([other, value], axis=dim),
        )
        step *= 2
    return value


def halve_reduce(value, axis, dim):
    size, index = lax.axis_size(axis), lax.axis_index(axis)
    step = size // 2
    while step >= 1:
        low, high = jnp.split(value, 2, axis=dim)
        lower = (index // step) % 2 == 0
        send, keep = jnp.where(lower, high, low), jnp.where(lower, low, high)
        value = keep + lax.ppermute(send, axis, [(i, i ^ step) for i in range(size)])
        step //= 2
    return value


def spread(parts, section_id, first):
    stacked = parts
    sources = (first, first + 2)
    pieces = [lax.dynamic_index_in_dim(stacked, section_id, 0, keepdims=False)]
    for r in (1, 2, 3):
        piece = lax.dynamic_index_in_dim(stacked, section_id ^ r, 0, keepdims=False)
        pieces.append(over_section(piece, r, sources=sources))
    return [lax.select_n(section_id ^ k, *pieces) for k in sources]


def local(inputs, segments, timestep, weight_in, weight_out, vectors, cotangent):
    section_id = lax.axis_index("section")
    batch_id = lax.axis_index("batch")
    batch = lax.axis_size("batch")
    ringed = batch == BLOCKS
    core_id = section_id % 2
    seqs, length, width = inputs.shape
    half = seqs * length // 2
    hidden_width = weight_in.shape[2]
    rows = weight_in.shape[1]
    unit = hidden_width // batch // SECTIONS
    ids = jnp.stack([section_id, batch_id]).astype(jnp.int32)
    scale = timestep.astype(f32) / STEPS

    if ringed:
        order_table, slot_table = ring_tables()
        order = jnp.asarray(order_table, jnp.int32)[batch_id]
        slots = jnp.asarray(slot_table, jnp.int32)[batch_id]
    else:
        order = slots = jnp.arange(BLOCKS, dtype=jnp.int32)

    if ringed:

        def sent(group, sources):
            with jax.named_scope(f"spread_{sources[0]}"):
                return [group[0]] + [over_section(group[r], r, sources=sources) for r in (1, 2, 3)]

        with jax.named_scope("vectors"):
            section_vectors = double_gather(vectors, "section", 0)
        attn_pieces = sent(cut(0, ids, weight_in[0], weight_out[0], ()), (0, 2))
        attn_shards = choose(ids, 0, attn_pieces, section_vectors, ())
        first_weights = ring_gather(attn_shards[0], "gather_0")
        feed_pieces = sent(cut(1, ids, weight_in[0], weight_out[0], (attn_shards[1],)), (1, 3))
        feed_shards = choose(ids, 1, feed_pieces, None, (first_weights[7], first_weights[8]))
    else:
        by_head = weight_in[0].reshape(rows, -1, SECTIONS, LANES).transpose(2, 0, 1, 3)
        by_head = by_head.reshape(SECTIONS, rows, width)
        by_unit = weight_in[0].reshape(rows, -1, SECTIONS, unit).transpose(2, 0, 1, 3)
        by_unit = by_unit.reshape(SECTIONS, rows, width)
        down_parts = weight_out[0].reshape(SECTIONS, unit, width)
        attn_shards = spread(by_head, section_id, 0)
        feed_shards = spread(jnp.concatenate([by_unit, down_parts], axis=1), section_id, 1)

    def gather_attn(shard, k):
        if ringed:
            return ring_gather(shard, f"gather_{k}")
        full = lax.all_gather(shard, "batch", axis=0, tiled=True)
        blocks = list(full.reshape(BLOCKS, LANES, width))
        return blocks[:7] + [blocks[7][: LANES // 2], blocks[7][LANES // 2 :]]

    def gather_feed(shard, k):
        if ringed:
            return ring_gather(shard, f"gather_{k}")
        up = lax.all_gather(shard[:rows], "batch", axis=0, tiled=True).reshape(BLOCKS, LANES, width)
        down = lax.all_gather(shard[rows:], "batch", axis=0, tiled=True).reshape(BLOCKS, LANES, width)
        blocks = [jnp.concatenate([up[j], down[j]], axis=0) for j in range(7)]
        return blocks + [up[7], down[7]]

    weights = [
        first_weights if ringed else gather_attn(attn_shards[0], 0),
        gather_feed(feed_shards[0], 1),
        gather_attn(attn_shards[1], 2),
        gather_feed(feed_shards[1], 3),
    ]

    def step_of(k, *steps):
        if not ringed:
            return ()
        return tuple(weights[k][2 * i - 1 + j] for i in steps for j in range(2))

    if ringed:
        vec = open_vectors(order, first_weights, ())
    else:
        vec = double_gather(double_gather(vectors, "section", 0), "batch", 2).astype(f32)
        vec = jnp.pad(vec, ((0, 0), (0, 1), (0, 0)))
    hidden, own, peer, cot, tails, bias = prepare(ids, scale, inputs, cotangent, vec, ())
    if unit != LANES:
        rest = [
            lax.dynamic_index_in_dim(
                vec[k, 0:4].reshape(-1, SECTIONS, unit), section_id, 1, keepdims=False
            ).reshape(width)
            for k in (1, 3)
        ]
        bias = jnp.stack([bias[0], rest[0], bias[2], rest[1]])

    quarters = jnp.moveaxis(segments.reshape(seqs, 2, 2, length // 4), 2, 0)
    quarters = quarters.reshape(2, seqs, length // 2).astype(f32)
    seg = jnp.where(
        core_id == 0,
        jnp.concatenate([quarters[0], quarters[1]], axis=1),
        jnp.concatenate([quarters[1], quarters[0]], axis=1),
    )

    def exchange(p_own, p_send, after):
        with jax.named_scope("sum_cores"):
            mine = join(p_own, over_section(p_send, 1), after)
        with jax.named_scope("sum_chips"):
            return mine, over_section(mine, 2)

    def to_all(packed):
        return lax.all_to_all(packed, "section", 0, 0)

    saved = []
    prev = hidden
    for k in range(SECTIONS):
        if k % 2 == 0:
            wo = to_all(pack_out(order, weights[k], (own,) if k == 0 else ()))
            qkv, probs, ctx, ctx_kept, x = attend(
                k, order, own, peer, seg, bias, weights[k], step_of(1, 1) if k == 0 else ()
            )
            p_own, p_send = project(ctx, wo, width, ())
            held = (x, wo, qkv, probs, ctx_kept)
        else:
            p_own, p_send, active, slope, x = feed(k, order, own, peer, bias, weights[k], ())
            held = (x, active, slope)
        mine, theirs = exchange(
            p_own, p_send, (step_of(1, 2), step_of(2, 2), step_of(3, 2), ())[k]
        )
        prev = hidden if k == 0 else x
        if k < SECTIONS - 1:
            late = (step_of(1, 3) + step_of(2, 1), step_of(2, 3) + step_of(3, 1), step_of(3, 3))[k]
            own, normed, inverse = norm(k, prev, mine, theirs, tails, late)
            saved.append((held, normed, inverse))
            with jax.named_scope("other_half"):
                peer = over_section(own, 1)
        else:
            output_part, grad_resid, grad_own, tail_sums = turn(
                k, ids, prev, mine, theirs, tails, cot, seqs, ()
            )
            saved.append((held, None, None))

    def scatter(parts):
        return lax.psum_scatter(
            jnp.concatenate(parts, axis=0), "batch", scatter_dimension=0, tiled=True
        )

    def whole_reduce(k, chunks):
        chunks = list(chunks)
        if k % 2 == 0:
            return scatter(chunks[:4] + [chunks[4], chunks[8]] + chunks[5:8])
        up = [c[:LANES] for c in chunks[:4]] + [chunks[4]] + [c[:LANES] for c in chunks[5:8]]
        down = [c[LANES:] for c in chunks[:4]] + [chunks[8]] + [c[LANES:] for c in chunks[5:8]]
        return jnp.concatenate([scatter(up), scatter(down)], axis=0)

    rings, reduced = [None] * 4, [None] * 4
    heads, tail_list = [None] * 4, [None] * 4

    def steps(numbers, after):
        if not ringed:
            return ()
        found = []
        for k in numbers:
            found += rings[k].step(after)
        return tuple(found)

    def weight_ring(k, chunks):
        if ringed:
            rings[k] = Reduction(chunks, f"reduce_{k}")
        else:
            reduced[k] = whole_reduce(k, chunks)

    for k in range(SECTIONS - 1, -1, -1):
        held, _, _ = saved[k]
        tail_list[k] = tail_sums
        with jax.named_scope("other_half"):
            grad_peer = over_section(grad_own, 1)
        before_join, before_norm = (((2, 1), (1,)), ((3, 2), (2, 1)), ((3,), (3, 2)), ((), (3,)))[k]
        if k == 0:
            before_norm = ()
        if k % 2 == 0:
            x, wo, qkv, probs, ctx = held
            wo_grad = to_all(out_grad(grad_own, grad_peer, ctx, ()))
            p_own, p_send, grads, sums = attend_back(
                order, grad_own, grad_peer, wo, qkv, probs, weights[k], ()
            )
            late = steps(before_join, (p_send,))
            mine, theirs = exchange(p_own, p_send, late)
            weight_ring(k, attend_weight(slots, x, grads, wo_grad, (mine,)))
        else:
            x, active, slope = held
            p_own, p_send, grads, sums = feed_back(
                order, grad_own, grad_peer, slope, weights[k], ()
            )
            late = steps(before_join, (p_send,))
            mine, theirs = exchange(p_own, p_send, late)
            weight_ring(k, feed_weight(slots, x, grads, grad_own, grad_peer, active, (mine,)))
        heads[k] = sums
        late = steps(before_norm, (mine,))
        if k > 0:
            _, normed, inverse = saved[k - 1]
            grad_resid, grad_own, tail_sums = norm_back(
                k - 1, grad_resid, mine, theirs, normed, inverse, tails, late
            )
        else:
            input_part, time_sums = finish(ids, scale, grad_resid, mine, theirs)
    if ringed:
        for k in (1, 0):
            while rings[k].at < 4:
                steps((k,), ())
        reduced = [r.sending[0] for r in rings]

    def to_owner(k, r):
        return jnp.where((section_id ^ r) == k, reduced[k], reduced[k + 2])

    def pieces_of(k):
        found = [to_owner(k, 0)]
        return found + [over_section(to_owner(k, r), r, targets=(k, k + 2)) for r in (1, 2, 3)]

    with jax.named_scope("collect"):
        feed_pieces, attn_pieces = pieces_of(1), pieces_of(0)
    odd = section_id % 2 == 1
    first_pieces = [jnp.where(odd, f[:rows], a) for f, a in zip(feed_pieces, attn_pieces)]
    slices = [lax.select_n(section_id ^ s, *first_pieces) for s in range(SECTIONS)]
    first = jnp.stack([p.reshape(rows, -1, LANES) for p in slices], axis=2)
    first = first.reshape(rows, hidden_width)
    if unit != LANES:
        other = jnp.stack([p.reshape(rows, -1, unit) for p in slices], axis=2)
        first = jnp.where(odd, other.reshape(rows, hidden_width), first)
    second = jnp.stack(
        [lax.select_n(section_id ^ s, *[f[rows:] for f in feed_pieces]) for s in range(SECTIONS)]
    )
    second = jnp.where(odd, second.reshape(SECTIONS * unit, width).astype(f32), 0.0)

    if unit == LANES:
        terms = vector_terms(ids, time_sums, heads, tail_list)
    else:
        empty_row = jnp.zeros((2, width), f32)
        terms = []
        for k in range(SECTIONS):
            if k % 2 == 0:
                def placed(piece):
                    empty = jnp.zeros((2, SECTIONS, LANES), f32)
                    piece = piece.reshape(2, 1, LANES)
                    return lax.dynamic_update_slice_in_dim(empty, piece, section_id, 1).reshape(1, width)

                head = [placed(heads[k][0, :256]), placed(heads[k][0, 512:])]
                head.append(0.5 * time_sums[:2] if k == 0 else empty_row)
            else:
                empty = jnp.zeros((width // unit, SECTIONS, unit), f32)
                piece = heads[k][0].reshape(width // unit, 1, unit)
                head = [lax.dynamic_update_slice_in_dim(empty, piece, section_id, 1).reshape(4, width)]
            terms.append(jnp.concatenate(head + [0.5 * tail_list[k][:3]], axis=0))
        terms = jnp.stack(terms)
    with jax.named_scope("vectors_back"):
        terms = halve_reduce(halve_reduce(terms, "section", 0), "batch", 2)
    return (output_part, input_part, first.astype(f32)[None], second[None], terms)


def solution(mesh):
    return jax.shard_map(
        local,
        mesh=mesh,
        in_specs=(
            P("batch", None, None),
            P("batch", None),
            P("batch"),
            P("section", "batch", None),
            P("section", "batch", None),
            P("section", None, "batch"),
            P("batch", None, None),
        ),
        out_specs=(
            P("batch", "section", None),
            P("batch", "section", None),
            P("section", "batch", None),
            P("section", "batch", None),
            P("section", None, "batch"),
        ),
        check_vma=False,
    )
```

```python
import functools
import math

import jax
import jax.numpy as jnp
from jax import lax
from jax.experimental import pallas as pl
from jax.experimental.pallas import tpu as pltpu
from jax.sharding import PartitionSpec as P

STEPS = 5000
SECTIONS = 4
BLOCKS = 8
LANES = 128
HEAD_DIM = 64

norm_eps = 1e-05
masked_score = -1e30
f32, bf16 = jnp.float32, jnp.bfloat16

VMEM = pl.BlockSpec(memory_space=pltpu.VMEM)
SMEM = pl.BlockSpec(memory_space=pltpu.SMEM)
ANY = pl.BlockSpec(memory_space=pl.ANY)
HBM = pl.BlockSpec(memory_space=pltpu.HBM)
KEEP = pl.BlockSpec()


def dot_nn(a, b):
    return jnp.dot(a, b, preferred_element_type=f32)


def dot_nt(a, b):
    return lax.dot_general(a, b, (((1,), (1,)), ((), ())), preferred_element_type=f32)


def dot_tn(a, b):
    return lax.dot_general(a, b, (((0,), (0,)), ((), ())), preferred_element_type=f32)


def shape_of(dims, dtype):
    return jax.ShapeDtypeStruct(dims, dtype)


def kept(dims, dtype):
    return pltpu.HBM(dims, dtype)


class Stored:
    def __init__(self, dims, dtype):
        self.ref = pltpu.HBM(dims, dtype)


def kernel_call(body, in_specs, outs, args, scratch=(), limit=16, after=()):
    known, late = len(args), len(after)

    def run(*refs):
        body(*refs[:known], *refs[known + late :])

    args = [
        pltpu.with_memory_space_constraint(x, pltpu.HBM) if spec in (HBM, KEEP, SMEM) else x
        for x, spec in zip(args, in_specs)
    ]
    return pl.pallas_call(
        run,
        in_specs=[ANY if spec is HBM else spec for spec in in_specs] + [ANY] * late,
        out_specs=[
            VMEM if isinstance(o, jax.ShapeDtypeStruct) else ANY if isinstance(o, Stored) else KEEP
            for o in outs
        ],
        out_shape=[o.ref if isinstance(o, Stored) else o for o in outs],
        scratch_shapes=list(scratch),
        compiler_params=pltpu.CompilerParams(vmem_limit_bytes=limit * 1024 * 1024),
        cost_estimate=pl.CostEstimate(flops=0, bytes_accessed=0, transcendentals=0),
        name=getattr(body, "func", body).__name__,
    )(*args, *after)


def block_copies(order, shards, first_row, rows, cols, target, sems, last):
    copies = []
    for j in range(BLOCKS - 1):
        copies.append(
            pltpu.make_async_copy(
                shards[j].at[pl.ds(first_row, rows), pl.ds(0, cols)],
                target.at[pl.ds(pl.multiple_of(order[j] * rows, rows), rows), :],
                sems.at[j],
            )
        )
    base = order[BLOCKS - 1] * rows
    at = BLOCKS - 1
    for piece, (offset, count) in last:
        copies.append(
            pltpu.make_async_copy(
                piece.at[pl.ds(0, count), pl.ds(0, cols)],
                target.at[pl.ds(pl.multiple_of(base + offset, count), count), :],
                sems.at[at],
            )
        )
        at += 1
    return copies


def begin(source, target, sem):
    copy = pltpu.make_async_copy(source, target, sem)
    copy.start()
    return copy


def gate_kernel(*refs):
    pass


def gate(arrays, after):
    count = len(arrays)
    return pl.pallas_call(
        gate_kernel,
        in_specs=[ANY] * (count + len(after)),
        out_specs=[ANY] * count,
        out_shape=[pltpu.HBM(a.shape, a.dtype) for a in arrays],
        input_output_aliases={i: i for i in range(count)},
        cost_estimate=pl.CostEstimate(flops=0, bytes_accessed=0, transcendentals=0),
        name="gate_kernel",
    )(*[pltpu.with_memory_space_constraint(a, pltpu.HBM) for a in arrays], *after)


def start_all(copies):
    for copy in copies:
        copy.start()


def wait_all(copies):
    for copy in copies:
        copy.wait()


def attention_copies(order, shards, cols, target, sems):
    half = LANES // 2
    last = [(shards[7], (0, half)), (shards[8], (half, half))]
    return block_copies(order, shards, 0, LANES, cols, target, sems, last)


def feed_copies(order, shards, width, up, down, sems):
    first = block_copies(order, shards, 0, LANES, width, up, sems.at[0], [(shards[7], (0, LANES))])
    second = block_copies(
        order, shards, LANES, LANES, width, down, sems.at[1], [(shards[8], (0, LANES))]
    )
    return first, second


def lane_masks(rows):
    lane = lax.broadcasted_iota(jnp.int32, (rows, LANES), 1)
    return lane < HEAD_DIM, lane >= HEAD_DIM


def seq_rows(ref, seq, cols, half):
    top = ref[seq * LANES : (seq + 1) * LANES, cols]
    bottom = ref[half + seq * LANES : half + (seq + 1) * LANES, cols]
    return jnp.concatenate([top, bottom], axis=0)


def put_rows(ref, seq, cols, half, value):
    ref[seq * LANES : (seq + 1) * LANES, cols] = value[:LANES]
    ref[half + seq * LANES : half + (seq + 1) * LANES, cols] = value[LANES:]


def attend_kernel(k, order, own, peer, seg, bias, *refs):
    shards, outs, refs = refs[:9], refs[9:14], refs[14:]
    qkv_out, probs_out, ctx, ctx_out, x_out = outs
    qkv, probs, x, w, sems, out_sems = refs
    half, width = own.shape
    seqs = half // LANES
    copies = attention_copies(order, shards, 3 * 256, w, sems)
    start_all(copies)
    x[:half] = own[...]
    x[half:] = peer[...]
    leaving = [begin(x, x_out, out_sems.at[0])]
    wait_all(copies)
    for i in range(3):
        cols = slice(256 * i, 256 * (i + 1))
        qkv[:, cols] = (dot_nn(x[...], w[:, cols]) + bias[k : k + 1, cols]).astype(bf16)
    leaving.append(begin(qkv, qkv_out, out_sems.at[1]))
    factor = 1.0 / math.sqrt(HEAD_DIM)
    masks = lane_masks(2 * LANES)
    for seq in range(seqs):
        key_seg = jnp.broadcast_to(seg[seq : seq + 1, :], (2 * LANES, 2 * LANES))
        allowed = key_seg == key_seg.T
        for group in range(2):
            q, k, v = [
                seq_rows(qkv, seq, slice(256 * i + LANES * group, 256 * i + LANES * (group + 1)), half)
                for i in range(3)
            ]
            parts = []
            for h in range(2):
                scores = dot_nt(jnp.where(masks[h], q, jnp.zeros_like(q)), k) * factor
                scores = jnp.where(allowed, scores, masked_score)
                peaks = jnp.max(scores, axis=1, keepdims=True)
                exponent = jnp.exp(scores - peaks)
                totals = jnp.sum(exponent, axis=1, keepdims=True)
                weights = exponent * (1.0 / totals)
                at = (seq * 2 + group) * 2 + h
                weights = weights.astype(bf16)
                probs[at] = weights
                leaving.append(begin(probs.at[at], probs_out.at[at], out_sems.at[3 + at]))
                parts.append(dot_nn(weights, v))
            put_rows(
                ctx,
                seq,
                slice(LANES * group, LANES * (group + 1)),
                half,
                jnp.where(masks[0], parts[0], parts[1]).astype(bf16),
            )
    leaving.append(begin(ctx, ctx_out, out_sems.at[2]))
    wait_all(leaving)


def attend(k, order, own, peer, seg, bias, shards, after):
    half, width = own.shape
    seqs = half // LANES
    return kernel_call(
        functools.partial(attend_kernel, k),
        [SMEM] + [VMEM] * 2 + [KEEP] * 2 + [HBM] * 9,
        [
            Stored((2 * half, 768), bf16),
            Stored((4 * seqs, 2 * LANES, 2 * LANES), bf16),
            shape_of((2 * half, 256), bf16),
            Stored((2 * half, 256), bf16),
            Stored((2 * half, width), bf16),
        ],
        (order, own, peer, seg, bias, *shards),
        [
            pltpu.VMEM((2 * half, 768), bf16),
            pltpu.VMEM((4 * seqs, 2 * LANES, 2 * LANES), bf16),
            pltpu.VMEM((2 * half, width), bf16),
            pltpu.VMEM((width, 768), bf16),
            pltpu.SemaphoreType.DMA((9,)),
            pltpu.SemaphoreType.DMA((3 + 4 * seqs,)),
        ],
        after=after,
    )


def out_blocks(s):
    return slice(LANES * s, LANES * (s + 1)), slice(512 + LANES * s, 512 + LANES * (s + 1))


def gather_parts(ids, parts, target, sems):
    return [
        begin(parts[r], target.at[ids[0] ^ r], sems.at[r]) for r in range(SECTIONS)
    ]


def project_kernel(ids, ctx, *refs):
    parts, (p_own, p_send, wo, sems) = refs[:4], refs[4:]
    half = p_own.shape[0]
    wait_all(gather_parts(ids, parts, wo, sems))
    for s in range(SECTIONS):
        result = dot_nn(ctx[...], wo[s].reshape(2 * LANES, 2 * LANES))
        for g, cols in enumerate(out_blocks(s)):
            part = result[:, LANES * g : LANES * (g + 1)]
            p_own[:, cols] = part[:half]
            p_send[:, cols] = part[half:].astype(bf16)


def project(ids, ctx, wo, width, after):
    half = ctx.shape[0] // 2
    return kernel_call(
        project_kernel,
        [SMEM, VMEM] + [HBM] * 4,
        [shape_of((half, width), f32), shape_of((half, width), bf16)],
        (ids, ctx, *wo),
        [
            pltpu.VMEM((SECTIONS, 2, LANES, 256), bf16),
            pltpu.SemaphoreType.DMA((SECTIONS,)),
        ],
        after=after,
    )


def pack_kernel(ids, order, *refs):
    shards, outs, (packed, sems) = refs[:9], refs[9:13], refs[13:]
    half = LANES // 2
    copies = []
    for j in range(9):
        b = order[min(j, 7)]
        first, count = ((0, LANES) if j < 7 else (half * (j - 7), half))
        copies.append(
            pltpu.make_async_copy(
                shards[j].at[pl.ds(0, count), pl.ds(768, 256)],
                packed.at[b % SECTIONS, b // SECTIONS, pl.ds(first, count)],
                sems.at[j],
            )
        )
    start_all(copies)
    wait_all(copies)
    for r in range(SECTIONS):
        outs[r][...] = packed[ids[0] ^ r]


def pack_out(ids, order, shards, after):
    return kernel_call(
        pack_kernel,
        [SMEM] * 2 + [HBM] * 9,
        [shape_of((2, LANES, 256), bf16)] * SECTIONS,
        (ids, order, *shards),
        [
            pltpu.VMEM((SECTIONS, 2, LANES, 256), bf16),
            pltpu.SemaphoreType.DMA((9,)),
        ],
        after=after,
    )


def out_grad_kernel(ids, own, peer, ctx, *outs):
    for r in range(SECTIONS):
        cols = jnp.concatenate(
            [
                jnp.concatenate(
                    [
                        part[:, pl.ds(pl.multiple_of(512 * g + LANES * (ids[0] ^ r), LANES), LANES)]
                        for part in (own, peer)
                    ],
                    axis=0,
                )
                for g in range(2)
            ],
            axis=1,
        )
        outs[r][...] = dot_tn(ctx[...], cols).astype(bf16).reshape(2, LANES, 256)


def out_grad(ids, own, peer, ctx, after):
    return kernel_call(
        out_grad_kernel,
        [SMEM, VMEM, VMEM, KEEP],
        [shape_of((2, LANES, 256), bf16)] * SECTIONS,
        (ids, own, peer, ctx),
        after=after,
    )


def attend_back_kernel(timed, ids, order, own, peer, qkv_in, probs_in, *refs):
    parts, shards, refs = refs[:4], refs[4:13], refs[13:]
    scale, refs = (refs[0], refs[1:]) if timed else (None, refs)
    p_own, p_send, grads, sums, wo, qkv, probs, w, gctx, sems, in_sems = refs
    half, width = own.shape
    seqs = half // LANES
    first = gather_parts(ids, parts, wo, in_sems)
    arriving = [begin(qkv_in, qkv, in_sems.at[4]), begin(probs_in, probs, in_sems.at[5])]
    copies = attention_copies(order, shards, 3 * 256, w, sems)
    start_all(copies)
    wait_all(first)
    for part, rows in ((own, slice(0, half)), (peer, slice(half, 2 * half))):
        total = None
        for s in range(SECTIONS):
            cols = jnp.concatenate([part[:, c] for c in out_blocks(s)], axis=1)
            term = dot_nt(cols, wo[s].reshape(2 * LANES, 2 * LANES))
            total = term if total is None else total + term
        gctx[rows, :] = total.astype(bf16)
    wait_all(arriving)
    factor = 1.0 / math.sqrt(HEAD_DIM)
    masks = lane_masks(2 * LANES)
    for seq in range(seqs):
        for group in range(2):
            lanes = slice(LANES * group, LANES * (group + 1))
            q, k, v = [
                seq_rows(qkv, seq, slice(256 * i + LANES * group, 256 * i + LANES * (group + 1)), half)
                for i in range(3)
            ]
            grad = seq_rows(gctx, seq, lanes, half)
            parts = []
            for h in range(2):
                low = probs[(seq * 2 + group) * 2 + h]
                weights = low.astype(f32)
                grad_probs = dot_nt(jnp.where(masks[h], grad, jnp.zeros_like(grad)), v)
                inner = jnp.sum(grad_probs * weights, axis=1, keepdims=True)
                grad_scores = (weights * (grad_probs - inner)).astype(bf16)
                parts.append(
                    (
                        dot_nn(grad_scores, k) * factor,
                        dot_tn(grad_scores, q) * factor,
                        dot_tn(low, grad),
                    )
                )
            for i in range(3):
                value = jnp.where(masks[0], parts[0][i], parts[1][i]).astype(bf16)
                put_rows(
                    grads,
                    seq,
                    slice(256 * i + LANES * group, 256 * i + LANES * (group + 1)),
                    half,
                    value,
                )
    sums[0:1, :768] = jnp.sum(grads[...].astype(f32), axis=0, keepdims=True)
    wait_all(copies)
    for i in range(width // 256):
        cols = slice(256 * i, 256 * (i + 1))
        result = dot_nt(grads[...], w[cols, :])
        if timed:
            plain, scaled = None, None
            for seq in range(seqs):
                rows = slice(seq * LANES, (seq + 1) * LANES)
                part = jnp.sum(result[:half][rows] + result[half:][rows], axis=0, keepdims=True)
                plain = part if plain is None else plain + part
                scaled = part * scale[seq] if scaled is None else scaled + part * scale[seq]
            sums[1:2, cols] = scaled
            sums[2:3, cols] = plain
        p_own[:, cols] = result[:half]
        p_send[:, cols] = result[half:].astype(bf16)


def attend_back(ids, order, own, peer, wo, qkv, probs, shards, scale, after):
    half, width = own.shape
    timed = scale is not None
    return kernel_call(
        functools.partial(attend_back_kernel, timed),
        [SMEM] * 2 + [VMEM] * 2 + [HBM] * 15 + [SMEM] * timed,
        [
            shape_of((half, width), f32),
            shape_of((half, width), bf16),
            shape_of((2 * half, 768), bf16),
            kept((8, width), f32),
        ],
        (ids, order, own, peer, qkv, probs, *wo, *shards) + ((scale,) if timed else ()),
        [
            pltpu.VMEM((SECTIONS, 2, LANES, 256), bf16),
            pltpu.VMEM(qkv.shape, bf16),
            pltpu.VMEM(probs.shape, bf16),
            pltpu.VMEM((width, 768), bf16),
            pltpu.VMEM((2 * half, 256), bf16),
            pltpu.SemaphoreType.DMA((9,)),
            pltpu.SemaphoreType.DMA((6,)),
        ],
        after=after,
    )


def pair_cols(x, first, second):
    blocks = [x[:, pl.ds(pl.multiple_of(b * LANES, LANES), LANES)] for b in (first, second)]
    return jnp.concatenate(blocks, axis=1)


def weight_kernel(pairs, parts, slots, *refs):
    sources = []
    for part in parts:
        count = {"feed": 5, "attend": 7}.get(part, 1 + 2 * len(part))
        sources.append(refs[:count])
        refs = refs[count:]
    refs, (wo_grad, terms) = refs[:-2], refs[-2:]
    targets, buffers, sems = refs[: len(refs) // 2], refs[len(refs) // 2 : -1], refs[-1]
    for part, source in zip(parts, sources):
        if part == "attend":
            for r in range(SECTIONS):
                wo_grad[source[2][0] ^ r] = source[3 + r][...]
        if isinstance(part, tuple):
            for n, k in enumerate(part):
                fill_terms(source[0][0], k, source[1 + 2 * n], source[2 + 2 * n], terms.at[n])
    outs, places, at, leaving = {}, {}, 0, []
    for pair in pairs:
        for slot in (pair, pair + 1):
            count = 2 if slot == 4 else 1
            outs[slot] = buffers[at : at + count]
            places[slot] = range(at, at + count)
            at += count

    def put(slot, row, cols, value):
        start = 0
        for out in outs[slot]:
            stop = start + out.shape[0]
            low, high = max(row, start), min(row + value.shape[0], stop)
            if low < high:
                out[low - start : high - start, cols] = value[low - row : high - row]
            start = stop

    whole = [
        jnp.concatenate([source[2][...], source[3][...]], axis=0) if part == "feed" else None
        for part, source in zip(parts, sources)
    ]
    for pair in pairs:
        blocks = slots[pair], slots[pair + 1]
        row = 0
        for part, source, g in zip(parts, sources, whole):
            width = terms.shape[2]
            if isinstance(part, tuple):
                for i, b in enumerate(blocks):
                    cols = pl.ds(pl.multiple_of(b * LANES, LANES), LANES)
                    lines = [
                        jnp.concatenate(
                            [terms[n, j : j + 1, cols] for j in range(7)]
                            + [jnp.zeros((1, width - 7 * LANES), f32)],
                            axis=1,
                        )
                        for n in range(len(part))
                    ]
                    lines.append(jnp.zeros((16 - len(part), width), f32))
                    lines = jnp.concatenate(lines, axis=0).astype(bf16)
                    put(pair + i, row, slice(0, width), lines)
                row += 16
                continue
            x, grads = source[:2]
            first = dot_tn(pair_cols(x, *blocks), grads[...]).astype(bf16)
            if part == "feed":
                second = dot_tn(pair_cols(source[4], *blocks), g).astype(bf16)
            for i, b in enumerate(blocks):
                rows = slice(LANES * i, LANES * (i + 1))
                if part == "feed":
                    put(pair + i, row, slice(0, width), first[rows])
                    put(pair + i, row + LANES, slice(0, width), second[rows])
                else:
                    put(pair + i, row, slice(0, 768), first[rows])
                    put(pair + i, row, slice(768, width), wo_grad[b % SECTIONS, b // SECTIONS])
            row += 2 * LANES if part == "feed" else LANES
        for n in (*places[pair], *places[pair + 1]):
            leaving.append(begin(buffers[n], targets[n], sems.at[n]))
    wait_all(leaving)


def weight_grads(slots, work, after, split):
    parts = tuple(part for part, _ in work)
    rows = sum({"feed": 2 * LANES, "attend": LANES}.get(part, 16) for part in parts)
    first = rows // 32 * 16
    width = [group[0].shape[1] for part, group in work if isinstance(part, str)][0]
    args = [a for _, group in work for a in group]
    specs = []
    for part in parts:
        if part == "feed":
            specs += [KEEP, VMEM, VMEM, VMEM, KEEP]
        elif part == "attend":
            specs += [KEEP, KEEP, SMEM] + [KEEP] * 4
        else:
            specs += [SMEM] + [KEEP] * (2 * len(part))
    found = [None] * 9
    for pairs in ((4,), (0, 2, 6)) if split else ((4, 0, 2, 6),):
        shapes, names = [], []
        for pair in pairs:
            for slot in (pair, pair + 1):
                names += [4, 8] if slot == 4 else [slot]
                shapes += [(first, width), (rows - first, width)] if slot == 4 else [(rows, width)]
        made = kernel_call(
            functools.partial(weight_kernel, pairs, parts),
            [SMEM] + specs,
            [Stored(dims, bf16) for dims in shapes],
            (slots, *args),
            [pltpu.VMEM(dims, bf16) for dims in shapes]
            + [
                pltpu.SemaphoreType.DMA((len(shapes),)),
                pltpu.VMEM((SECTIONS, 2, LANES, 256), bf16),
                pltpu.VMEM((3, 8, width), f32),
            ],
            limit=24,
            after=after if found[5] is None else (found[5],),
        )
        for name, value in zip(names, made):
            found[name] = value
    return found


def feed_kernel(k, order, own, peer, bias, *refs):
    shards, outs, refs = refs[:9], refs[9:14], refs[14:]
    p_own, p_send, active_out, slope_out, x_out = outs
    active, slope, x, up, down, sems, out_sems = refs
    half, width = own.shape
    first, second = feed_copies(order, shards, width, up, down, sems)
    start_all(first)
    start_all(second)
    x[:half] = own[...]
    x[half:] = peer[...]
    leaving = [begin(x, x_out, out_sems.at[8])]
    wait_all(first)
    for i in range(width // 256):
        cols = slice(256 * i, 256 * (i + 1))
        upper = dot_nn(x[...], up[:, cols]) + bias[k : k + 1, cols]
        cumulative = 0.5 * (1.0 + lax.erf(upper * (1.0 / math.sqrt(2.0))))
        density = jnp.exp(-0.5 * upper * upper) * (1.0 / math.sqrt(2.0 * math.pi))
        active[:, cols] = (upper * cumulative).astype(bf16)
        slope[:, cols] = (cumulative + upper * density).astype(bf16)
        for j, (part, out) in enumerate(((active, active_out), (slope, slope_out))):
            leaving.append(begin(part.at[:, cols], out.at[:, cols], out_sems.at[4 * j + i]))
    wait_all(second)
    for i in range(width // 256):
        cols = slice(256 * i, 256 * (i + 1))
        result = dot_nn(active[...], down[:, cols])
        p_own[:, cols] = result[:half]
        p_send[:, cols] = result[half:].astype(bf16)
    wait_all(leaving)


def feed(k, order, own, peer, bias, shards, after):
    half, width = own.shape
    return kernel_call(
        functools.partial(feed_kernel, k),
        [SMEM] + [VMEM] * 2 + [KEEP] + [HBM] * 9,
        [
            shape_of((half, width), f32),
            shape_of((half, width), bf16),
            Stored((2 * half, width), bf16),
            Stored((2 * half, width), bf16),
            Stored((2 * half, width), bf16),
        ],
        (order, own, peer, bias, *shards),
        [
            pltpu.VMEM((2 * half, width), bf16),
            pltpu.VMEM((2 * half, width), bf16),
            pltpu.VMEM((2 * half, width), bf16),
            pltpu.VMEM((width, width), bf16),
            pltpu.VMEM((width, width), bf16),
            pltpu.SemaphoreType.DMA((2, 9)),
            pltpu.SemaphoreType.DMA((9,)),
        ],
        after=after,
    )


def feed_back_kernel(order, own, peer, slope_in, *refs):
    shards, (p_own, p_send, grads, sums, slope, g, up, down, sems, slope_sem) = refs[:9], refs[9:]
    half, width = own.shape
    first, second = feed_copies(order, shards, width, up, down, sems)
    start_all(second[:2])
    arriving = begin(slope_in, slope, slope_sem.at[0])
    start_all(second[2:])
    start_all(first)
    g[:half] = own[...]
    g[half:] = peer[...]
    for j in range(0, BLOCKS, 2):
        wait_all(second[j : j + 2])
        if j == 0:
            arriving.wait()
        places = [pl.ds(pl.multiple_of(order[j + i] * LANES, LANES), LANES) for i in range(2)]
        rows = jnp.concatenate([down[p, :] for p in places], axis=0)
        slopes = jnp.concatenate([slope[:, p] for p in places], axis=1)
        grad = (dot_nt(g[...], rows) * slopes.astype(f32)).astype(bf16)
        total = jnp.sum(grad.astype(f32), axis=0, keepdims=True)
        for i, p in enumerate(places):
            grads[:, p] = grad[:, LANES * i : LANES * (i + 1)]
            sums[0:1, p] = total[:, LANES * i : LANES * (i + 1)]
    wait_all(first)
    for i in range(width // 256):
        cols = slice(256 * i, 256 * (i + 1))
        result = dot_nt(grads[...], up[cols, :])
        p_own[:, cols] = result[:half]
        p_send[:, cols] = result[half:].astype(bf16)


def feed_back(order, own, peer, slope, shards, after):
    half, width = own.shape
    return kernel_call(
        feed_back_kernel,
        [SMEM] + [VMEM] * 2 + [HBM] * 10,
        [
            shape_of((half, width), f32),
            shape_of((half, width), bf16),
            shape_of((2 * half, width), bf16),
            kept((8, width), f32),
        ],
        (order, own, peer, slope, *shards),
        [
            pltpu.VMEM((2 * half, width), bf16),
            pltpu.VMEM((2 * half, width), bf16),
            pltpu.VMEM((width, width), bf16),
            pltpu.VMEM((width, width), bf16),
            pltpu.SemaphoreType.DMA((2, 9)),
            pltpu.SemaphoreType.DMA((4,)),
        ],
        after=after,
    )


def norm_rows(resid):
    average = jnp.mean(resid, axis=1, keepdims=True)
    centred = resid - average
    variance = jnp.mean(centred * centred, axis=1, keepdims=True)
    inverse = lax.rsqrt(variance + norm_eps)
    return centred * inverse, inverse


def norm_back_rows(grad_out, normed, inverse, gain):
    scaled = grad_out * gain
    return inverse * (
        scaled
        - jnp.mean(scaled, axis=1, keepdims=True)
        - normed * jnp.mean(scaled * normed, axis=1, keepdims=True)
    )


def add_sums(sums, first, grad_branch, grad_out, normed):
    terms = [grad_branch.astype(f32), grad_out * normed, grad_out]
    for row, term in enumerate(terms):
        total = jnp.sum(term, axis=0, keepdims=True)
        sums[row : row + 1, :] = total if first else sums[row : row + 1, :] + total


def fetch_kernel(k, with_cot, prev, tails, *refs):
    base, tail = refs[with_cot : with_cot + 2]
    tail[...] = tails[k]
    base[...] = prev[: base.shape[0]].astype(f32) + tails[k, 0:1, :]
    if with_cot:
        refs[3][...] = refs[0][...]


def fetch(k, prev, tails, cot, half, after):
    width = prev.shape[1]
    with_cot = cot is not None
    outs = [shape_of((half, width), f32), shape_of((8, width), f32)]
    return kernel_call(
        functools.partial(fetch_kernel, k, int(with_cot)),
        [KEEP] * (2 + with_cot),
        outs + [shape_of((half, width), bf16)] * with_cot,
        (prev, tails) + ((cot,) if with_cot else ()),
        after=after,
    )


def norm_kernel(base, tail, mine, theirs, out, normed_out, inverse_out, normed, inverse, sems):
    step = LANES
    leaving = []
    for r in range(mine.shape[0] // step):
        rows = slice(step * r, step * (r + 1))
        branch = mine[rows].astype(f32) + theirs[rows].astype(f32)
        value, inv = norm_rows(base[rows] + branch)
        normed[rows] = value.astype(bf16)
        inverse[rows] = jnp.broadcast_to(inv, (step, LANES))
        leaving.append(begin(normed.at[rows], normed_out.at[rows], sems.at[0, r]))
        leaving.append(begin(inverse.at[rows], inverse_out.at[rows], sems.at[1, r]))
        out[rows] = (value * tail[1:2] + tail[2:3]).astype(bf16)
    wait_all(leaving)


def norm(base, tail, mine, theirs, after):
    half, width = mine.shape
    return kernel_call(
        norm_kernel,
        [VMEM] * 4,
        [shape_of((half, width), bf16), Stored((half, width), bf16), Stored((half, LANES), f32)],
        (base, tail, mine, theirs),
        [
            pltpu.VMEM((half, width), bf16),
            pltpu.VMEM((half, LANES), f32),
            pltpu.SemaphoreType.DMA((2, half // LANES)),
        ],
        after=after,
    )


def turn_kernel(ids, base, tail, cot, mine, theirs, picked, grad_out_resid, grad_branch, sums, *scratch):
    out, grad_resid, sems = scratch
    step = LANES
    leaving = []
    for r in range(mine.shape[0] // step):
        rows = slice(step * r, step * (r + 1))
        branch = mine[rows].astype(f32) + theirs[rows].astype(f32)
        value, inv = norm_rows(base[rows] + branch)
        out[rows] = (value * tail[1:2] + tail[2:3]).astype(bf16)
        grad_out = cot[rows].astype(f32)
        grad = norm_back_rows(grad_out, value, inv, tail[1:2])
        low = grad.astype(bf16)
        grad_resid[rows] = grad
        leaving.append(begin(grad_resid.at[rows], grad_out_resid.at[rows], sems.at[r]))
        grad_branch[rows] = low
        add_sums(sums, r == 0, low, grad_out, value)
    pick_rows(ids, out, picked)
    wait_all(leaving)


def pick_rows(ids, value, picked):
    count = picked.shape[1]
    for seq in range(picked.shape[0]):
        start = pl.multiple_of(2 * count * seq + count * (ids[0] // 2), count)
        picked[seq] = value[pl.ds(start, count), :]


def turn(ids, base, tail, cot, mine, theirs, seqs, after):
    half, width = mine.shape
    return kernel_call(
        turn_kernel,
        [SMEM] + [VMEM] * 5,
        [
            kept((seqs, half // seqs // 2, width), bf16),
            Stored((half, width), f32),
            shape_of((half, width), bf16),
            kept((8, width), f32),
        ],
        (ids, base, tail, cot, mine, theirs),
        [
            pltpu.VMEM((half, width), bf16),
            pltpu.VMEM((half, width), f32),
            pltpu.SemaphoreType.DMA((half // LANES,)),
        ],
        after=after,
    )


def fetch_back_kernel(k, above_in, normed_in, inverse_in, tails, above, normed, inverse, tail):
    above[...] = above_in[...]
    normed[...] = normed_in[...]
    inverse[...] = inverse_in[...]
    tail[...] = tails[k]


def fetch_back(k, above, normed, inverse, tails, after):
    half, width = above.shape
    return kernel_call(
        functools.partial(fetch_back_kernel, k),
        [KEEP] * 4,
        [
            shape_of((half, width), f32),
            shape_of((half, width), bf16),
            shape_of((half, LANES), f32),
            shape_of((8, width), f32),
        ],
        (above, normed, inverse, tails),
        after=after,
    )


def norm_back_kernel(timed, above, normed, inverse, tail, mine, theirs, *refs):
    scale, refs = (refs[0], refs[1:]) if timed else (None, refs)
    resid_out, grad_branch, sums, grad_resid, sems = refs
    step = LANES
    leaving = []
    for r in range(above.shape[0] // step):
        rows = slice(step * r, step * (r + 1))
        grad_in = above[rows] + (mine[rows].astype(f32) + theirs[rows].astype(f32))
        grad_out = grad_in.astype(bf16).astype(f32)
        value = normed[rows].astype(f32)
        grad = norm_back_rows(grad_out, value, inverse[rows, 0:1], tail[1:2])
        low = grad.astype(bf16)
        grad_resid[rows] = grad
        leaving.append(begin(grad_resid.at[rows], resid_out.at[rows], sems.at[r]))
        grad_branch[rows] = low
        add_sums(sums, r == 0, low, grad_out, value)
        if timed:
            part = jnp.sum(grad, axis=0, keepdims=True)
            for row, term in ((3, part * scale[r]), (4, part)):
                sums[row : row + 1, :] = term if r == 0 else sums[row : row + 1, :] + term
    wait_all(leaving)


def norm_back(above, normed, inverse, tail, mine, theirs, scale, after):
    half, width = above.shape
    timed = scale is not None
    return kernel_call(
        functools.partial(norm_back_kernel, timed),
        [VMEM] * 6 + [SMEM] * timed,
        [Stored((half, width), f32), shape_of((half, width), bf16), kept((8, width), f32)],
        (above, normed, inverse, tail, mine, theirs) + ((scale,) if timed else ()),
        [pltpu.VMEM((half, width), f32), pltpu.SemaphoreType.DMA((half // LANES,))],
        after=after,
    )


def finish_kernel(ids, above, mine, theirs, picked, grad_in):
    grad_in[...] = above[...] + (mine[...].astype(f32) + theirs[...].astype(f32))
    pick_rows(ids, grad_in, picked)


def finish(ids, above, mine, theirs, seqs, after):
    half, width = above.shape
    (picked,) = kernel_call(
        finish_kernel,
        [SMEM, KEEP, VMEM, VMEM],
        [kept((seqs, half // seqs // 2, width), f32)],
        (ids, above, mine, theirs),
        [pltpu.VMEM((half, width), f32)],
        after=after,
    )
    return picked


def join_kernel(own, other, out):
    out[...] = (own[...] + other[...].astype(f32)).astype(bf16)


def join(own, other, after):
    (out,) = kernel_call(
        join_kernel, [VMEM] * 2, [shape_of(own.shape, bf16)], (own, other), after=after
    )
    return out


def prepare_kernel(ids, scale, inputs, cot, vec, hidden, own, peer, cot_own, tails, bias):
    section = ids[0]
    core = section % 2
    seqs, length, width = inputs.shape
    quarter = length // 4
    mul, add = vec[0, 2:3, :], vec[0, 3:4, :]
    for seq in range(seqs):
        embedding = scale[seq] * mul + add
        for y in range(2):
            at = slice((2 * seq + y) * quarter, (2 * seq + y + 1) * quarter)
            mine = pl.ds(pl.multiple_of((2 * y + core) * quarter, quarter), quarter)
            other = pl.ds(pl.multiple_of((2 * y + 1 - core) * quarter, quarter), quarter)
            value = inputs[seq, mine, :].astype(f32) + embedding
            hidden[at] = value
            own[at] = value.astype(bf16)
            peer[at] = (inputs[seq, other, :].astype(f32) + embedding).astype(bf16)
            cot_own[at] = cot[seq, mine, :]
    for k in range(SECTIONS):
        tails[k, 0:3, :] = vec[k, 4:7, :]
        if k % 2 == 0:
            bias[k : k + 1, :] = jnp.zeros((1, width), f32)
            for g in range(2):
                cols = pl.ds(pl.multiple_of(512 * g + LANES * section, LANES), LANES)
                for i in range(2):
                    at = 512 * i + LANES * g
                    bias[k : k + 1, at : at + LANES] = vec[k, i : i + 1, cols]
        else:
            for g in range(8):
                cols = pl.ds(pl.multiple_of(512 * (g % 2) + LANES * section, LANES), LANES)
                bias[k : k + 1, LANES * g : LANES * (g + 1)] = vec[k, g // 2 : g // 2 + 1, cols]


def prepare(ids, scale, inputs, cot, vec, after):
    seqs, length, width = inputs.shape
    half = seqs * length // 2
    return kernel_call(
        prepare_kernel,
        [SMEM] * 2 + [KEEP] * 3,
        [
            kept((half, width), f32),
            shape_of((half, width), bf16),
            shape_of((half, width), bf16),
            kept((half, width), bf16),
            kept((SECTIONS, 8, width), f32),
            kept((SECTIONS, width), f32),
        ],
        (ids, scale, inputs, cot, vec),
        after=after,
    )


def open_kernel(order, *refs):
    shards, (vec, parts, sems) = refs[:8], refs[8:]
    copies = []
    for j in range(BLOCKS):
        first = LANES if j < BLOCKS - 1 else LANES // 2
        copies.append(
            pltpu.make_async_copy(shards[j].at[pl.ds(first, 16), :], parts.at[j], sems.at[j])
        )
    start_all(copies)
    wait_all(copies)
    for j in range(BLOCKS):
        value = parts[j].astype(f32)
        cols = pl.ds(pl.multiple_of(order[j] * LANES, LANES), LANES)
        for k in range(SECTIONS):
            for i in range(7):
                vec[k, i : i + 1, cols] = value[k : k + 1, LANES * i : LANES * (i + 1)]


def open_vectors(order, shards, after):
    width = shards[0].shape[1]
    (vec,) = kernel_call(
        open_kernel,
        [SMEM] + [HBM] * 8,
        [kept((SECTIONS, 8, width), f32)],
        (order, *shards[:7], shards[8]),
        [pltpu.VMEM((BLOCKS, 16, width), bf16), pltpu.SemaphoreType.DMA((BLOCKS,))],
        after=after,
    )
    return vec


def fill_terms(section, k, head, tail, terms):
    terms[...] = jnp.zeros_like(terms)
    if k % 2 == 0:
        for g in range(2):
            cols = pl.ds(pl.multiple_of(512 * g + LANES * section, LANES), LANES)
            for i in range(2):
                at = 512 * i + LANES * g
                terms[i : i + 1, cols] = head[0:1, at : at + LANES]
        if k == 0:
            terms[2:4, :] = head[1:3, :] + 0.5 * tail[3:5, :]
    else:
        for g in range(8):
            cols = pl.ds(pl.multiple_of(512 * (g % 2) + LANES * section, LANES), LANES)
            terms[g // 2 : g // 2 + 1, cols] = head[0:1, LANES * g : LANES * (g + 1)]
    terms[4:7, :] = 0.5 * tail[0:3, :]


def cut_kernel(kind, ids, first, second, *outs):
    sems = outs[4]
    section = ids[0]
    rows = first.shape[0]

    @pl.when(section % 2 == kind)
    def _():
        copies = []
        for r in range(SECTIONS):
            at = section ^ r
            for g in range(8):
                cols = pl.ds(pl.multiple_of(512 * g + LANES * at, LANES), LANES)
                copies.append(
                    pltpu.make_async_copy(
                        first.at[:, cols],
                        outs[r].at[pl.ds(0, rows), pl.ds(LANES * g, LANES)],
                        sems.at[r, g],
                    )
                )
            if kind:
                piece = pl.ds(pl.multiple_of(LANES * at, LANES), LANES)
                copies.append(
                    pltpu.make_async_copy(
                        second.at[piece, :], outs[r].at[pl.ds(rows, LANES), :], sems.at[r, 8]
                    )
                )
        start_all(copies)
        wait_all(copies)


def cut(kind, ids, first, second, after):
    rows, width = first.shape[0], second.shape[1]
    return kernel_call(
        functools.partial(cut_kernel, kind),
        [SMEM] + [HBM] * 2,
        [shape_of((rows + LANES * kind, width), bf16)] * 4,
        (ids, first, second),
        [pltpu.SemaphoreType.DMA((SECTIONS, 9))],
        after=after,
    )


def choose_kernel(base, joined, ids, *refs):
    pieces, refs = refs[:4], refs[4:]
    vectors, refs = (refs[0], refs[1:]) if joined else (None, refs)
    outs, sems = refs[:2], refs[2]
    rows = pieces[0].shape[0]
    for i in range(2):
        at = ids[0] ^ (base + 2 * i)
        for r in range(SECTIONS):

            @pl.when(at == r)
            def _():
                target = outs[i].at[pl.ds(0, rows), :]
                pltpu.make_async_copy(pieces[r], target, sems.at[i]).start()

    if joined:
        width = outs[0].shape[1]
        value = vectors[...].astype(f32)
        lines = [
            jnp.concatenate(
                [value[k, i : i + 1, :] for i in range(7)] + [jnp.zeros((1, width - 7 * LANES), f32)],
                axis=1,
            )
            for k in range(SECTIONS)
        ]
        lines.append(jnp.zeros((16 - SECTIONS, width), f32))
        outs[0][rows:, :] = jnp.concatenate(lines, axis=0).astype(bf16)

    for i in range(2):
        target = outs[i].at[pl.ds(0, rows), :]
        pltpu.make_async_copy(pieces[0], target, sems.at[i]).wait()


def choose(ids, base, pieces, vectors, after):
    rows, width = pieces[0].shape
    joined = vectors is not None
    return kernel_call(
        functools.partial(choose_kernel, base, joined),
        [SMEM] + [ANY] * 4 + [VMEM] * joined,
        [shape_of((rows + 16 * joined, width), bf16), shape_of((rows, width), bf16)],
        (ids, *pieces) + ((vectors,) if joined else ()),
        [pltpu.SemaphoreType.DMA((2,))],
        after=after,
    )


def step_kernel(kind, right, left, ahead, behind, *outs):
    if kind == "last":
        total = ahead[...].astype(f32) + right[...].astype(f32) + left[...].astype(f32)
        outs[0][...] = total.astype(bf16)
    elif kind == "first":
        mid = right.shape[0]
        outs[0][:mid] = ahead[:mid] + right[...]
        outs[0][mid:] = ahead[mid:]
        outs[1][:mid] = behind[:mid]
        outs[1][mid:] = behind[mid:] + left[...]
    else:
        outs[0][...] = ahead[...] + right[...]
        outs[1][...] = behind[...] + left[...]


def ring_step(kind, right, left, ahead, behind, after):
    count = 1 if kind == "last" else 2
    return kernel_call(
        functools.partial(step_kernel, kind),
        [VMEM, VMEM, KEEP, KEEP],
        [shape_of(ahead.shape, bf16)] * count,
        (right, left, ahead, behind),
        after=after,
    )


def place_kernel(ids, *refs):
    feed_pieces, attn_pieces, (first, second, vec) = refs[:4], refs[4:8], refs[8:]
    section = ids[0]
    rows, width = first.shape[0], second.shape[1]

    def columns(r, piece, start):
        at = section ^ r
        for g in range(8):
            cols = pl.ds(pl.multiple_of(512 * g + LANES * at, LANES), LANES)
            first[:, cols] = piece[start : start + rows, LANES * g : LANES * (g + 1)].astype(f32)

    def vector_rows(pieces, start, low, high, pick_high):
        total = None
        for piece in pieces:
            extra = piece[start : start + 16, :].astype(f32)
            total = extra if total is None else total + extra
        line = jnp.where(pick_high, total[high : high + 1, :], total[low : low + 1, :])
        for j in range(7):
            vec[j : j + 1, :] = line[:, LANES * j : LANES * (j + 1)]

    @pl.when(section % 2 == 1)
    def _():
        for r in range(SECTIONS):
            columns(r, feed_pieces[r], 0)
            at = pl.ds(pl.multiple_of((section ^ r) * LANES, LANES), LANES)
            second[at, :] = feed_pieces[r][rows : rows + LANES, :].astype(f32)
        vector_rows(feed_pieces, rows + LANES, 0, 2, section == 3)

    @pl.when(section % 2 == 0)
    def _():
        for r in range(SECTIONS):
            columns(r, attn_pieces[r], 16)
        vector_rows(attn_pieces, 0, 0, 1, section == 2)
        second[...] = jnp.zeros_like(second)


def place(ids, feed_pieces, attn_pieces):
    width = attn_pieces[0].shape[1]
    return kernel_call(
        place_kernel,
        [SMEM] + [VMEM] * 8,
        [
            kept((LANES, 4 * width), f32),
            kept((SECTIONS * LANES, width), f32),
            kept((7, LANES), f32),
        ],
        (ids, *feed_pieces, *attn_pieces),
        limit=20,
    )


def over_section(value, r, sources=range(SECTIONS), targets=range(SECTIONS)):
    route = [(i, i ^ r) for i in range(SECTIONS) if i in sources and (i ^ r) in targets]
    return lax.ppermute(value, "section", route)


def ring_of(n):
    return list(range(0, n, 2)) + list(range(n - 1, 0, -2))


def around(value, way):
    ring = ring_of(lax.axis_size("batch"))
    n = len(ring)
    return lax.ppermute(value, "batch", [(ring[i], ring[(i + way) % n]) for i in range(n)])


def ring_gather(shard, name, after=()):
    with jax.named_scope(name):
        return ring_gather_steps(shard, after)


def ring_gather_steps(shard, after):
    out, right, left = [shard], shard, shard
    for i in range(3):
        right, left = around(right, 1), around(left, -1)
        if i == 0 and after:
            right, left = gate((right, left), after)
        out += [right, left]
    mid = shard.shape[0] // 32 * 16
    return out + [around(right[:mid], 1), around(left[mid:], -1)]


class Reduction:
    def __init__(self, chunks, name):
        self.chunks, self.name, self.at = chunks, name, 0
        self.sending = (chunks[4], chunks[8])

    def step(self, after):
        chunks, at = self.chunks, self.at
        with jax.named_scope(self.name):
            right, left = around(self.sending[0], 1), around(self.sending[1], -1)
            kind = ("first", "middle", "middle", "last")[at]
            ahead, behind = ((3, 5), (2, 6), (1, 7), (0, 0))[at]
            self.sending = tuple(
                ring_step(kind, right, left, chunks[ahead], chunks[behind], tuple(after))
            )
        self.at += 1
        return self.sending


class Gathering:
    def __init__(self, shard, name):
        self.name = name
        self.blocks = [shard]
        with jax.named_scope(name):
            right, left = shard, shard
            for _ in range(2):
                right, left = around(right, 1), around(left, -1)
                self.blocks += [right, left]

    def finish(self, after):
        with jax.named_scope(self.name):
            right, left = gate(tuple(self.blocks[3:5]), after)
            self.blocks[3:5] = [right, left]
            right, left = around(right, 1), around(left, -1)
            mid = right.shape[0] // 32 * 16
            self.blocks += [right, left, around(right[:mid], 1), around(left[mid:], -1)]
        return self.blocks


def ring_tables():
    ring = ring_of(BLOCKS)
    place = [ring.index(b) for b in range(BLOCKS)]
    steps = [0, -1, 1, -2, 2, -3, 3, 4]
    order = [[ring[(place[b] + k) % BLOCKS] for k in steps] for b in range(BLOCKS)]
    slots = [[ring[(place[b] + j) % BLOCKS] for j in range(BLOCKS)] for b in range(BLOCKS)]
    return order, slots


def double_gather(value, axis, dim):
    size, index = lax.axis_size(axis), lax.axis_index(axis)
    step = 1
    while step < size:
        other = lax.ppermute(value, axis, [(i, i ^ step) for i in range(size)])
        lower = (index // step) % 2 == 0
        value = jnp.where(
            lower,
            jnp.concatenate([value, other], axis=dim),
            jnp.concatenate([other, value], axis=dim),
        )
        step *= 2
    return value


def halve_reduce(value, axis, dim):
    size, index = lax.axis_size(axis), lax.axis_index(axis)
    step = size // 2
    while step >= 1:
        low, high = jnp.split(value, 2, axis=dim)
        lower = (index // step) % 2 == 0
        send, keep = jnp.where(lower, high, low), jnp.where(lower, low, high)
        value = keep + lax.ppermute(send, axis, [(i, i ^ step) for i in range(size)])
        step //= 2
    return value


def spread(parts, section_id, first):
    stacked = parts
    sources = (first, first + 2)
    pieces = [lax.dynamic_index_in_dim(stacked, section_id, 0, keepdims=False)]
    for r in (1, 2, 3):
        piece = lax.dynamic_index_in_dim(stacked, section_id ^ r, 0, keepdims=False)
        pieces.append(over_section(piece, r, sources=sources))
    return [lax.select_n(section_id ^ k, *pieces) for k in sources]


def local(inputs, segments, timestep, weight_in, weight_out, vectors, cotangent):
    section_id = lax.axis_index("section")
    batch_id = lax.axis_index("batch")
    batch = lax.axis_size("batch")
    ringed = batch == BLOCKS
    core_id = section_id % 2
    seqs, length, width = inputs.shape
    half = seqs * length // 2
    hidden_width = weight_in.shape[2]
    rows = weight_in.shape[1]
    unit = hidden_width // batch // SECTIONS
    ids = jnp.stack([section_id, batch_id]).astype(jnp.int32)
    scale = timestep.astype(f32) / STEPS

    if ringed:
        order_table, slot_table = ring_tables()
        order = jnp.asarray(order_table, jnp.int32)[batch_id]
        slots = jnp.asarray(slot_table, jnp.int32)[batch_id]
    else:
        order = slots = jnp.arange(BLOCKS, dtype=jnp.int32)

    if ringed:

        def sent(group, sources):
            with jax.named_scope(f"spread_{sources[0]}"):
                return [group[0]] + [over_section(group[r], r, sources=sources) for r in (1, 2, 3)]

        with jax.named_scope("vectors"):
            section_vectors = double_gather(vectors, "section", 0)
        attn_pieces = sent(cut(0, ids, weight_in[0], weight_out[0], ()), (0, 2))
        attn_shards = choose(ids, 0, attn_pieces, section_vectors, ())
        first_weights = ring_gather(attn_shards[0], "gather_0")
        feed_pieces = sent(cut(1, ids, weight_in[0], weight_out[0], (attn_shards[1],)), (1, 3))
    else:
        by_head = weight_in[0].reshape(rows, -1, SECTIONS, LANES).transpose(2, 0, 1, 3)
        by_head = by_head.reshape(SECTIONS, rows, width)
        by_unit = weight_in[0].reshape(rows, -1, SECTIONS, unit).transpose(2, 0, 1, 3)
        by_unit = by_unit.reshape(SECTIONS, rows, width)
        down_parts = weight_out[0].reshape(SECTIONS, unit, width)
        attn_shards = spread(by_head, section_id, 0)
        feed_shards = spread(jnp.concatenate([by_unit, down_parts], axis=1), section_id, 1)

    def gather_attn(shard, k):
        if ringed:
            return ring_gather(shard, f"gather_{k}")
        full = lax.all_gather(shard, "batch", axis=0, tiled=True)
        blocks = list(full.reshape(BLOCKS, LANES, width))
        return blocks[:7] + [blocks[7][: LANES // 2], blocks[7][LANES // 2 :]]

    def gather_feed(shard, k, after=()):
        if ringed:
            return ring_gather(shard, f"gather_{k}", after)
        up = lax.all_gather(shard[:rows], "batch", axis=0, tiled=True).reshape(BLOCKS, LANES, width)
        down = lax.all_gather(shard[rows:], "batch", axis=0, tiled=True).reshape(BLOCKS, LANES, width)
        blocks = [jnp.concatenate([up[j], down[j]], axis=0) for j in range(7)]
        return blocks + [up[7], down[7]]

    if ringed:
        vec = open_vectors(order, first_weights, (first_weights[7],))
    else:
        vec = double_gather(double_gather(vectors, "section", 0), "batch", 2).astype(f32)
        vec = jnp.pad(vec, ((0, 0), (0, 1), (0, 0)))
    hidden, own, peer, cot, tails, bias = prepare(ids, scale, inputs, cotangent, vec, ())
    if ringed:
        first_packed = pack_out(ids, order, first_weights, (own,))
        feed_shards = choose(ids, 1, feed_pieces, None, (first_weights[7], first_weights[8]))
    else:
        first_weights = gather_attn(attn_shards[0], 0)
        first_packed = pack_out(ids, order, first_weights, ())

    weights = [
        first_weights,
        gather_feed(feed_shards[0], 1, (first_packed[0],)),
        gather_attn(attn_shards[1], 2),
        None,
    ]
    if ringed:
        last_ring = Gathering(feed_shards[1], "gather_3")
        weights[3] = last_ring.blocks
    else:
        weights[3] = gather_feed(feed_shards[1], 3)

    def step_of(k, *steps):
        if not ringed:
            return ()
        return tuple(weights[k][2 * i - 1 + j] for i in steps for j in range(2))

    if unit != LANES:
        rest = [
            lax.dynamic_index_in_dim(
                vec[k, 0:4].reshape(-1, SECTIONS, unit), section_id, 1, keepdims=False
            ).reshape(width)
            for k in (1, 3)
        ]
        bias = jnp.stack([bias[0], rest[0], bias[2], rest[1]])

    quarters = jnp.moveaxis(segments.reshape(seqs, 2, 2, length // 4), 2, 0)
    quarters = quarters.reshape(2, seqs, length // 2).astype(f32)
    seg = jnp.where(
        core_id == 0,
        jnp.concatenate([quarters[0], quarters[1]], axis=1),
        jnp.concatenate([quarters[1], quarters[0]], axis=1),
    )

    def exchange(p_own, p_send, after):
        with jax.named_scope("sum_cores"):
            mine = join(p_own, over_section(p_send, 1), after)
        with jax.named_scope("sum_chips"):
            return mine, over_section(mine, 2)

    def to_all(parts):
        with jax.named_scope("turn_out_slices"):
            return (parts[0],) + tuple(over_section(parts[r], r) for r in (1, 2, 3))

    saved = []
    prev = hidden
    for k in range(SECTIONS):
        if k % 2 == 0:
            packed = first_packed if k == 0 else pack_out(ids, order, weights[k], ())
            if k == 2 and ringed:
                weights[3] = last_ring.finish((packed[0],))
            wo = to_all(packed)
            qkv, probs, ctx, ctx_kept, x = attend(
                k, order, own, peer, seg, bias, weights[k], ()
            )
            p_own, p_send = project(ids, ctx, wo, width, step_of(1, 2) if k == 0 else step_of(3, 3))
            held = (x, wo, qkv, probs, ctx_kept)
        else:
            p_own, p_send, active, slope, x = feed(
                k, order, own, peer, bias, weights[k], step_of(2, 2) if k == 1 else ()
            )
            held = (x, active, slope)
        mine, theirs = exchange(p_own, p_send, step_of(3, 1) if k == 1 else ())
        prev = hidden if k == 0 else x
        ahead = fetch(k, prev, tails, cot if k == 3 else None, half, (mine,))
        if k < SECTIONS - 1:
            numbers = (((1, 3), (2, 1)), ((2, 3), (3, 2)), ((3, 4),))[k]
            late = sum((step_of(*n) for n in numbers), ())
            own, normed, inverse = norm(*ahead, mine, theirs, late)
            saved.append((held, normed, inverse))
            with jax.named_scope("other_half"):
                peer = over_section(own, 1)
        else:
            output_part, grad_resid, grad_own, tail_sums = turn(
                ids, *ahead, mine, theirs, seqs, ()
            )
            saved.append((held, None, None))

    def scatter(parts):
        return lax.psum_scatter(
            jnp.concatenate(parts, axis=0), "batch", scatter_dimension=0, tiled=True
        )

    def whole_reduce(k, chunks):
        chunks = list(chunks)
        if k % 2 == 0:
            return scatter(chunks[:4] + [chunks[4], chunks[8]] + chunks[5:8])
        up = [c[:LANES] for c in chunks[:4]] + [chunks[4]] + [c[:LANES] for c in chunks[5:8]]
        down = [c[LANES:] for c in chunks[:4]] + [chunks[8]] + [c[LANES:] for c in chunks[5:8]]
        return jnp.concatenate([scatter(up), scatter(down)], axis=0)

    rings, reduced = [None] * 4, [None] * 4
    heads, tail_list = [None] * 4, [None] * 4

    def steps(numbers, after):
        if not ringed:
            return ()
        found = []
        for k in numbers:
            found += rings[k].step(after)
        return tuple(found)

    def weight_ring(k, chunks):
        if ringed:
            rings[k] = Reduction(chunks, f"reduce_{k}")
        else:
            reduced[k] = whole_reduce(k, chunks)

    waiting = []
    for k in range(SECTIONS - 1, -1, -1):
        held, _, _ = saved[k]
        tail_list[k] = tail_sums
        with jax.named_scope("other_half"):
            grad_peer = over_section(grad_own, 1)
        before_join, before_norm = (((1,), (1,)), ((3,), (3,)), ((), (3,)), ((), (3,)))[k]
        early = steps((1,), (grad_own,)) if k == 0 else ()
        if k % 2 == 0:
            x, wo, qkv, probs, ctx = held
            if k == 0:
                packed = out_grad(ids, grad_own, grad_peer, ctx, ())
                wo_grad = to_all(packed)
            p_own, p_send, grads, sums = attend_back(
                ids,
                order,
                grad_own,
                grad_peer,
                wo,
                qkv,
                probs,
                weights[k],
                scale if k == 0 else None,
                (packed[0], *early) if k == 0 else (),
            )
            late = steps(before_join, (p_send,))
            if k == 0:
                late = (*late, *wo_grad[1:])
            mine, theirs = exchange(p_own, p_send, late)
            if k != 0:
                packed = out_grad(ids, grad_own, grad_peer, ctx, (mine,))
                wo_grad = to_all(packed)
            work = [("attend", (x, grads, ids, *wo_grad))]
        else:
            x, active, slope = held
            p_own, p_send, grads, sums = feed_back(
                order, grad_own, grad_peer, slope, weights[k], wo_grad[1:] if k == 1 else ()
            )
            late = steps(before_join, (p_send,))
            mine, theirs = exchange(p_own, p_send, late)
            work = [("feed", (x, grads, grad_own, grad_peer, active))]
        heads[k] = sums

        def shares(numbers):
            if not ringed:
                return []
            return [(numbers, (ids, *[a for n in numbers for a in (heads[n], tail_list[n])]))]

        fence = (mine,)
        if k == 2 and ringed:
            waiting = work
        else:
            if k == 1:
                work = work + shares((1, 2, 3))
            elif k == 0:
                work = shares((0,)) + work
            chunks = weight_grads(slots, work + waiting, (mine,), k != 1)
            weight_ring(k, chunks)
            waiting = []
            if k == 0:
                fence = (mine, chunks[0])
        if k == 0:
            first_step = steps((0,), fence)
            fence = (mine, *first_step[:1])
        late = steps(before_norm, fence)
        if k == 2:
            late = (*late, packed[0])
        if k > 0:
            _, normed, inverse = saved[k - 1]
            ahead = fetch_back(k - 1, grad_resid, normed, inverse, tails, (mine,))
            grad_resid, grad_own, tail_sums = norm_back(
                *ahead, mine, theirs, scale if k == 1 else None, late
            )
        else:
            input_part = finish(ids, grad_resid, mine, theirs, seqs, late)
    if ringed:
        last = (input_part,)
        for k in (1, 0, 0, 0):
            last = steps((k,), (last[0],))
        both = rings[1].sending[0]
        cut_at = 2 * rows + 16
        upper = jnp.concatenate([rings[3].sending[0], both[2 * rows : cut_at]], axis=0)
        reduced = [rings[0].sending[0], both[:cut_at], both[2 * rows :], upper]

    def to_owner(k, r):
        return jnp.where((section_id ^ r) == k, reduced[k], reduced[k + 2])

    def pieces_of(k):
        found = [to_owner(k, 0)]
        return found + [over_section(to_owner(k, r), r, targets=(k, k + 2)) for r in (1, 2, 3)]

    with jax.named_scope("collect"):
        feed_pieces, attn_pieces = pieces_of(1), pieces_of(0)
    if unit == LANES:
        first, second, terms = place(ids, feed_pieces, attn_pieces)
    else:
        odd = section_id % 2 == 1
        first_pieces = [jnp.where(odd, f[:rows], a) for f, a in zip(feed_pieces, attn_pieces)]
        slices = [lax.select_n(section_id ^ s, *first_pieces) for s in range(SECTIONS)]
        first = jnp.stack([p.reshape(rows, -1, LANES) for p in slices], axis=2)
        first = first.reshape(rows, hidden_width)
        if unit != LANES:
            other = jnp.stack([p.reshape(rows, -1, unit) for p in slices], axis=2)
            first = jnp.where(odd, other.reshape(rows, hidden_width), first)
        second = jnp.stack(
            [lax.select_n(section_id ^ s, *[f[rows:] for f in feed_pieces]) for s in range(SECTIONS)]
        )
        second = jnp.where(odd, second.reshape(SECTIONS * unit, width).astype(f32), 0.0)

    if unit != LANES:
        empty_row = jnp.zeros((2, width), f32)
        time_sums = heads[0][1:3] + 0.5 * tail_list[0][3:5]
        terms = []
        for k in range(SECTIONS):
            if k % 2 == 0:

                def placed(piece):
                    empty = jnp.zeros((2, SECTIONS, LANES), f32)
                    piece = piece.reshape(2, 1, LANES)
                    full = lax.dynamic_update_slice_in_dim(empty, piece, section_id, 1)
                    return full.reshape(1, width)

                head = [placed(heads[k][0, :256]), placed(heads[k][0, 512:768])]
                head.append(time_sums if k == 0 else empty_row)
            else:
                empty = jnp.zeros((width // unit, SECTIONS, unit), f32)
                piece = heads[k][0].reshape(width // unit, 1, unit)
                full = lax.dynamic_update_slice_in_dim(empty, piece, section_id, 1)
                head = [full.reshape(4, width)]
            terms.append(jnp.concatenate(head + [0.5 * tail_list[k][:3]], axis=0))
        with jax.named_scope("vectors_back"):
            terms = halve_reduce(halve_reduce(jnp.stack(terms), "section", 0), "batch", 2)[0]
    return (output_part, input_part, first.astype(f32)[None], second[None], terms[None])


def solution(mesh):
    return jax.shard_map(
        local,
        mesh=mesh,
        in_specs=(
            P("batch", None, None),
            P("batch", None),
            P("batch"),
            P("section", "batch", None),
            P("section", "batch", None),
            P("section", None, "batch"),
            P("batch", None, None),
        ),
        out_specs=(
            P("batch", "section", None),
            P("batch", "section", None),
            P("section", "batch", None),
            P("section", "batch", None),
            P("section", None, "batch"),
        ),
        check_vma=False,
    )
```

```python
import functools
import math

import jax
import jax.numpy as jnp
from jax import lax
from jax.experimental import pallas as pl
from jax.experimental.pallas import tpu as pltpu
from jax.sharding import PartitionSpec as P

STEPS = 5000
SECTIONS = 4
BLOCKS = 8
LANES = 128
HEAD_DIM = 64

norm_eps = 1e-05
masked_score = -1e30
f32, bf16 = jnp.float32, jnp.bfloat16

VMEM = pl.BlockSpec(memory_space=pltpu.VMEM)
SMEM = pl.BlockSpec(memory_space=pltpu.SMEM)
ANY = pl.BlockSpec(memory_space=pl.ANY)
HBM = pl.BlockSpec(memory_space=pltpu.HBM)
KEEP = pl.BlockSpec()


def dot_nn(a, b):
    return jnp.dot(a, b, preferred_element_type=f32)


def dot_nt(a, b):
    return lax.dot_general(a, b, (((1,), (1,)), ((), ())), preferred_element_type=f32)


def dot_tn(a, b):
    return lax.dot_general(a, b, (((0,), (0,)), ((), ())), preferred_element_type=f32)


def shape_of(dims, dtype):
    return jax.ShapeDtypeStruct(dims, dtype)


def kept(dims, dtype):
    return pltpu.HBM(dims, dtype)


class Stored:
    def __init__(self, dims, dtype):
        self.ref = pltpu.HBM(dims, dtype)


def kernel_call(body, in_specs, outs, args, scratch=(), limit=16, after=()):
    known, late = len(args), len(after)

    def run(*refs):
        body(*refs[:known], *refs[known + late :])

    args = [
        pltpu.with_memory_space_constraint(x, pltpu.HBM) if spec in (HBM, KEEP, SMEM) else x
        for x, spec in zip(args, in_specs)
    ]
    return pl.pallas_call(
        run,
        in_specs=[ANY if spec is HBM else spec for spec in in_specs] + [ANY] * late,
        out_specs=[
            VMEM if isinstance(o, jax.ShapeDtypeStruct) else ANY if isinstance(o, Stored) else KEEP
            for o in outs
        ],
        out_shape=[o.ref if isinstance(o, Stored) else o for o in outs],
        scratch_shapes=list(scratch),
        compiler_params=pltpu.CompilerParams(vmem_limit_bytes=limit * 1024 * 1024),
        cost_estimate=pl.CostEstimate(flops=0, bytes_accessed=0, transcendentals=0),
        name=getattr(body, "func", body).__name__,
    )(*args, *after)


def block_copies(order, shards, first_row, rows, cols, target, sems, last):
    copies = []
    for j in range(BLOCKS - 1):
        copies.append(
            pltpu.make_async_copy(
                shards[j].at[pl.ds(first_row, rows), pl.ds(0, cols)],
                target.at[pl.ds(pl.multiple_of(order[j] * rows, rows), rows), :],
                sems.at[j],
            )
        )
    base = order[BLOCKS - 1] * rows
    at = BLOCKS - 1
    for piece, (offset, count) in last:
        copies.append(
            pltpu.make_async_copy(
                piece.at[pl.ds(0, count), pl.ds(0, cols)],
                target.at[pl.ds(pl.multiple_of(base + offset, count), count), :],
                sems.at[at],
            )
        )
        at += 1
    return copies


def begin(source, target, sem):
    copy = pltpu.make_async_copy(source, target, sem)
    copy.start()
    return copy


def gate_kernel(*refs):
    pass


def gate(arrays, after):
    count = len(arrays)
    return pl.pallas_call(
        gate_kernel,
        in_specs=[ANY] * (count + len(after)),
        out_specs=[ANY] * count,
        out_shape=[pltpu.HBM(a.shape, a.dtype) for a in arrays],
        input_output_aliases={i: i for i in range(count)},
        cost_estimate=pl.CostEstimate(flops=0, bytes_accessed=0, transcendentals=0),
        name="gate_kernel",
    )(*[pltpu.with_memory_space_constraint(a, pltpu.HBM) for a in arrays], *after)


def start_all(copies):
    for copy in copies:
        copy.start()


def wait_all(copies):
    for copy in copies:
        copy.wait()


def attention_copies(order, shards, cols, target, sems):
    half = LANES // 2
    last = [(shards[7], (0, half)), (shards[8], (half, half))]
    return block_copies(order, shards, 0, LANES, cols, target, sems, last)


def feed_copies(order, shards, width, up, down, sems):
    first = block_copies(order, shards, 0, LANES, width, up, sems.at[0], [(shards[7], (0, LANES))])
    second = block_copies(
        order, shards, LANES, LANES, width, down, sems.at[1], [(shards[8], (0, LANES))]
    )
    return first, second


def lane_masks(rows):
    lane = lax.broadcasted_iota(jnp.int32, (rows, LANES), 1)
    return lane < HEAD_DIM, lane >= HEAD_DIM


def seq_rows(ref, seq, cols, half):
    top = ref[seq * LANES : (seq + 1) * LANES, cols]
    bottom = ref[half + seq * LANES : half + (seq + 1) * LANES, cols]
    return jnp.concatenate([top, bottom], axis=0)


def put_rows(ref, seq, cols, half, value):
    ref[seq * LANES : (seq + 1) * LANES, cols] = value[:LANES]
    ref[half + seq * LANES : half + (seq + 1) * LANES, cols] = value[LANES:]


def attend_kernel(k, order, own, peer, seg, bias, *refs):
    shards, outs, refs = refs[:9], refs[9:14], refs[14:]
    qkv_out, probs_out, ctx, ctx_out, x_out = outs
    qkv, probs, x, w, sems, out_sems = refs
    half, width = own.shape
    seqs = half // LANES
    copies = attention_copies(order, shards, 3 * 256, w, sems)
    start_all(copies)
    x[:half] = own[...]
    x[half:] = peer[...]
    leaving = [begin(x, x_out, out_sems.at[0])]
    wait_all(copies)
    for i in range(3):
        cols = slice(256 * i, 256 * (i + 1))
        qkv[:, cols] = (dot_nn(x[...], w[:, cols]) + bias[k : k + 1, cols]).astype(bf16)
    leaving.append(begin(qkv, qkv_out, out_sems.at[1]))
    factor = 1.0 / math.sqrt(HEAD_DIM)
    masks = lane_masks(2 * LANES)
    for seq in range(seqs):
        key_seg = jnp.broadcast_to(seg[seq : seq + 1, :], (2 * LANES, 2 * LANES))
        allowed = key_seg == key_seg.T
        for group in range(2):
            q, k, v = [
                seq_rows(qkv, seq, slice(256 * i + LANES * group, 256 * i + LANES * (group + 1)), half)
                for i in range(3)
            ]
            parts = []
            for h in range(2):
                scores = dot_nt(jnp.where(masks[h], q, jnp.zeros_like(q)), k) * factor
                scores = jnp.where(allowed, scores, masked_score)
                peaks = jnp.max(scores, axis=1, keepdims=True)
                exponent = jnp.exp(scores - peaks)
                totals = jnp.sum(exponent, axis=1, keepdims=True)
                weights = exponent * (1.0 / totals)
                at = (seq * 2 + group) * 2 + h
                weights = weights.astype(bf16)
                probs[at] = weights
                leaving.append(begin(probs.at[at], probs_out.at[at], out_sems.at[3 + at]))
                parts.append(dot_nn(weights, v))
            put_rows(
                ctx,
                seq,
                slice(LANES * group, LANES * (group + 1)),
                half,
                jnp.where(masks[0], parts[0], parts[1]).astype(bf16),
            )
    leaving.append(begin(ctx, ctx_out, out_sems.at[2]))
    wait_all(leaving)


def attend(k, order, own, peer, seg, bias, shards, after):
    half, width = own.shape
    seqs = half // LANES
    return kernel_call(
        functools.partial(attend_kernel, k),
        [SMEM] + [VMEM] * 2 + [KEEP] * 2 + [HBM] * 9,
        [
            Stored((2 * half, 768), bf16),
            Stored((4 * seqs, 2 * LANES, 2 * LANES), bf16),
            shape_of((2 * half, 256), bf16),
            Stored((2 * half, 256), bf16),
            Stored((2 * half, width), bf16),
        ],
        (order, own, peer, seg, bias, *shards),
        [
            pltpu.VMEM((2 * half, 768), bf16),
            pltpu.VMEM((4 * seqs, 2 * LANES, 2 * LANES), bf16),
            pltpu.VMEM((2 * half, width), bf16),
            pltpu.VMEM((width, 768), bf16),
            pltpu.SemaphoreType.DMA((9,)),
            pltpu.SemaphoreType.DMA((3 + 4 * seqs,)),
        ],
        after=after,
    )


def out_blocks(s):
    return slice(LANES * s, LANES * (s + 1)), slice(512 + LANES * s, 512 + LANES * (s + 1))


def gather_parts(ids, parts, target, sems):
    return [
        begin(parts[r], target.at[ids[0] ^ r], sems.at[r]) for r in range(SECTIONS)
    ]


def project_kernel(ids, ctx, *refs):
    parts, (p_own, p_send, wo, sems) = refs[:4], refs[4:]
    half = p_own.shape[0]
    wait_all(gather_parts(ids, parts, wo, sems))
    for s in range(SECTIONS):
        result = dot_nn(ctx[...], wo[s].reshape(2 * LANES, 2 * LANES))
        for g, cols in enumerate(out_blocks(s)):
            part = result[:, LANES * g : LANES * (g + 1)]
            p_own[:, cols] = part[:half]
            p_send[:, cols] = part[half:].astype(bf16)


def project(ids, ctx, wo, width, after):
    half = ctx.shape[0] // 2
    return kernel_call(
        project_kernel,
        [SMEM, VMEM] + [HBM] * 4,
        [shape_of((half, width), f32), shape_of((half, width), bf16)],
        (ids, ctx, *wo),
        [
            pltpu.VMEM((SECTIONS, 2, LANES, 256), bf16),
            pltpu.SemaphoreType.DMA((SECTIONS,)),
        ],
        after=after,
    )


def pack_kernel(ids, order, *refs):
    shards, outs, (packed, sems) = refs[:9], refs[9:13], refs[13:]
    half = LANES // 2
    copies = []
    for j in range(9):
        b = order[min(j, 7)]
        first, count = ((0, LANES) if j < 7 else (half * (j - 7), half))
        copies.append(
            pltpu.make_async_copy(
                shards[j].at[pl.ds(0, count), pl.ds(768, 256)],
                packed.at[b % SECTIONS, b // SECTIONS, pl.ds(first, count)],
                sems.at[j],
            )
        )
    start_all(copies)
    wait_all(copies)
    for r in range(SECTIONS):
        outs[r][...] = packed[ids[0] ^ r]


def pack_out(ids, order, shards, after):
    return kernel_call(
        pack_kernel,
        [SMEM] * 2 + [HBM] * 9,
        [shape_of((2, LANES, 256), bf16)] * SECTIONS,
        (ids, order, *shards),
        [
            pltpu.VMEM((SECTIONS, 2, LANES, 256), bf16),
            pltpu.SemaphoreType.DMA((9,)),
        ],
        after=after,
    )


def out_grad_kernel(ids, own, peer, ctx, *outs):
    for r in range(SECTIONS):
        cols = jnp.concatenate(
            [
                jnp.concatenate(
                    [
                        part[:, pl.ds(pl.multiple_of(512 * g + LANES * (ids[0] ^ r), LANES), LANES)]
                        for part in (own, peer)
                    ],
                    axis=0,
                )
                for g in range(2)
            ],
            axis=1,
        )
        outs[r][...] = dot_tn(ctx[...], cols).astype(bf16).reshape(2, LANES, 256)


def out_grad(ids, own, peer, ctx, after):
    return kernel_call(
        out_grad_kernel,
        [SMEM, VMEM, VMEM, KEEP],
        [shape_of((2, LANES, 256), bf16)] * SECTIONS,
        (ids, own, peer, ctx),
        after=after,
    )


def attend_back_kernel(timed, ids, order, own, peer, qkv_in, probs_in, *refs):
    parts, shards, refs = refs[:4], refs[4:13], refs[13:]
    scale, refs = (refs[0], refs[1:]) if timed else (None, refs)
    p_own, p_send, grads, sums, wo, qkv, probs, w, gctx, sems, in_sems = refs
    half, width = own.shape
    seqs = half // LANES
    first = gather_parts(ids, parts, wo, in_sems)
    arriving = [begin(qkv_in, qkv, in_sems.at[4]), begin(probs_in, probs, in_sems.at[5])]
    copies = attention_copies(order, shards, 3 * 256, w, sems)
    start_all(copies)
    wait_all(first)
    for part, rows in ((own, slice(0, half)), (peer, slice(half, 2 * half))):
        total = None
        for s in range(SECTIONS):
            cols = jnp.concatenate([part[:, c] for c in out_blocks(s)], axis=1)
            term = dot_nt(cols, wo[s].reshape(2 * LANES, 2 * LANES))
            total = term if total is None else total + term
        gctx[rows, :] = total.astype(bf16)
    wait_all(arriving)
    factor = 1.0 / math.sqrt(HEAD_DIM)
    masks = lane_masks(2 * LANES)
    for seq in range(seqs):
        for group in range(2):
            lanes = slice(LANES * group, LANES * (group + 1))
            q, k, v = [
                seq_rows(qkv, seq, slice(256 * i + LANES * group, 256 * i + LANES * (group + 1)), half)
                for i in range(3)
            ]
            grad = seq_rows(gctx, seq, lanes, half)
            parts = []
            for h in range(2):
                low = probs[(seq * 2 + group) * 2 + h]
                weights = low.astype(f32)
                grad_probs = dot_nt(jnp.where(masks[h], grad, jnp.zeros_like(grad)), v)
                inner = jnp.sum(grad_probs * weights, axis=1, keepdims=True)
                grad_scores = (weights * (grad_probs - inner)).astype(bf16)
                parts.append(
                    (
                        dot_nn(grad_scores, k) * factor,
                        dot_tn(grad_scores, q) * factor,
                        dot_tn(low, grad),
                    )
                )
            for i in range(3):
                value = jnp.where(masks[0], parts[0][i], parts[1][i]).astype(bf16)
                put_rows(
                    grads,
                    seq,
                    slice(256 * i + LANES * group, 256 * i + LANES * (group + 1)),
                    half,
                    value,
                )
    sums[0:1, :768] = jnp.sum(grads[...].astype(f32), axis=0, keepdims=True)
    wait_all(copies)
    for i in range(width // 256):
        cols = slice(256 * i, 256 * (i + 1))
        result = dot_nt(grads[...], w[cols, :])
        if timed:
            plain, scaled = None, None
            for seq in range(seqs):
                rows = slice(seq * LANES, (seq + 1) * LANES)
                part = jnp.sum(result[:half][rows] + result[half:][rows], axis=0, keepdims=True)
                plain = part if plain is None else plain + part
                scaled = part * scale[seq] if scaled is None else scaled + part * scale[seq]
            sums[1:2, cols] = scaled
            sums[2:3, cols] = plain
        p_own[:, cols] = result[:half]
        p_send[:, cols] = result[half:].astype(bf16)


def attend_back(ids, order, own, peer, wo, qkv, probs, shards, scale, after):
    half, width = own.shape
    timed = scale is not None
    return kernel_call(
        functools.partial(attend_back_kernel, timed),
        [SMEM] * 2 + [VMEM] * 2 + [HBM] * 15 + [SMEM] * timed,
        [
            shape_of((half, width), f32),
            shape_of((half, width), bf16),
            shape_of((2 * half, 768), bf16),
            kept((8, width), f32),
        ],
        (ids, order, own, peer, qkv, probs, *wo, *shards) + ((scale,) if timed else ()),
        [
            pltpu.VMEM((SECTIONS, 2, LANES, 256), bf16),
            pltpu.VMEM(qkv.shape, bf16),
            pltpu.VMEM(probs.shape, bf16),
            pltpu.VMEM((width, 768), bf16),
            pltpu.VMEM((2 * half, 256), bf16),
            pltpu.SemaphoreType.DMA((9,)),
            pltpu.SemaphoreType.DMA((6,)),
        ],
        after=after,
    )


def pair_cols(x, first, second):
    blocks = [x[:, pl.ds(pl.multiple_of(b * LANES, LANES), LANES)] for b in (first, second)]
    return jnp.concatenate(blocks, axis=1)


def weight_kernel(pairs, parts, slots, *refs):
    sources = []
    for part in parts:
        count = {"feed": 5, "attend": 7}.get(part, 1 + 2 * len(part))
        sources.append(refs[:count])
        refs = refs[count:]
    refs, (wo_grad, terms) = refs[:-2], refs[-2:]
    targets, buffers, sems = refs[: len(refs) // 2], refs[len(refs) // 2 : -1], refs[-1]
    for part, source in zip(parts, sources):
        if part == "attend":
            for r in range(SECTIONS):
                wo_grad[source[2][0] ^ r] = source[3 + r][...]
        if isinstance(part, tuple):
            for n, k in enumerate(part):
                fill_terms(source[0][0], k, source[1 + 2 * n], source[2 + 2 * n], terms.at[n])
    outs, places, at, leaving = {}, {}, 0, []
    for pair in pairs:
        for slot in (pair, pair + 1):
            count = 2 if slot == 4 else 1
            outs[slot] = buffers[at : at + count]
            places[slot] = range(at, at + count)
            at += count

    def put(slot, row, cols, value):
        start = 0
        for out in outs[slot]:
            stop = start + out.shape[0]
            low, high = max(row, start), min(row + value.shape[0], stop)
            if low < high:
                out[low - start : high - start, cols] = value[low - row : high - row]
            start = stop

    whole = [
        jnp.concatenate([source[2][...], source[3][...]], axis=0) if part == "feed" else None
        for part, source in zip(parts, sources)
    ]
    for pair in pairs:
        blocks = slots[pair], slots[pair + 1]
        row = 0
        for part, source, g in zip(parts, sources, whole):
            width = terms.shape[2]
            if isinstance(part, tuple):
                for i, b in enumerate(blocks):
                    cols = pl.ds(pl.multiple_of(b * LANES, LANES), LANES)
                    lines = [
                        jnp.concatenate(
                            [terms[n, j : j + 1, cols] for j in range(7)]
                            + [jnp.zeros((1, width - 7 * LANES), f32)],
                            axis=1,
                        )
                        for n in range(len(part))
                    ]
                    lines.append(jnp.zeros((16 - len(part), width), f32))
                    lines = jnp.concatenate(lines, axis=0).astype(bf16)
                    put(pair + i, row, slice(0, width), lines)
                row += 16
                continue
            x, grads = source[:2]
            first = dot_tn(pair_cols(x, *blocks), grads[...]).astype(bf16)
            if part == "feed":
                second = dot_tn(pair_cols(source[4], *blocks), g).astype(bf16)
            for i, b in enumerate(blocks):
                rows = slice(LANES * i, LANES * (i + 1))
                if part == "feed":
                    put(pair + i, row, slice(0, width), first[rows])
                    put(pair + i, row + LANES, slice(0, width), second[rows])
                else:
                    put(pair + i, row, slice(0, 768), first[rows])
                    put(pair + i, row, slice(768, width), wo_grad[b % SECTIONS, b // SECTIONS])
            row += 2 * LANES if part == "feed" else LANES
        for n in (*places[pair], *places[pair + 1]):
            leaving.append(begin(buffers[n], targets[n], sems.at[n]))
    wait_all(leaving)


def weight_grads(slots, work, after, split):
    parts = tuple(part for part, _ in work)
    rows = sum({"feed": 2 * LANES, "attend": LANES}.get(part, 16) for part in parts)
    first = rows // 32 * 16
    width = [group[0].shape[1] for part, group in work if isinstance(part, str)][0]
    args = [a for _, group in work for a in group]
    specs = []
    for part in parts:
        if part == "feed":
            specs += [KEEP, VMEM, VMEM, VMEM, KEEP]
        elif part == "attend":
            specs += [KEEP, KEEP, SMEM] + [KEEP] * 4
        else:
            specs += [SMEM] + [KEEP] * (2 * len(part))
    found = [None] * 9
    for pairs in ((4,), (0, 2, 6)) if split else ((4, 0, 2, 6),):
        shapes, names = [], []
        for pair in pairs:
            for slot in (pair, pair + 1):
                names += [4, 8] if slot == 4 else [slot]
                shapes += [(first, width), (rows - first, width)] if slot == 4 else [(rows, width)]
        made = kernel_call(
            functools.partial(weight_kernel, pairs, parts),
            [SMEM] + specs,
            [Stored(dims, bf16) for dims in shapes],
            (slots, *args),
            [pltpu.VMEM(dims, bf16) for dims in shapes]
            + [
                pltpu.SemaphoreType.DMA((len(shapes),)),
                pltpu.VMEM((SECTIONS, 2, LANES, 256), bf16),
                pltpu.VMEM((3, 8, width), f32),
            ],
            limit=24,
            after=after if found[5] is None else (found[5],),
        )
        for name, value in zip(names, made):
            found[name] = value
    return found


def feed_kernel(k, order, own, peer, bias, *refs):
    shards, outs, refs = refs[:9], refs[9:14], refs[14:]
    p_own, p_send, active_out, slope_out, x_out = outs
    active, slope, x, up, down, sems, out_sems = refs
    half, width = own.shape
    first, second = feed_copies(order, shards, width, up, down, sems)
    start_all(first)
    start_all(second)
    x[:half] = own[...]
    x[half:] = peer[...]
    leaving = [begin(x, x_out, out_sems.at[8])]
    wait_all(first)
    for i in range(width // 256):
        cols = slice(256 * i, 256 * (i + 1))
        upper = dot_nn(x[...], up[:, cols]) + bias[k : k + 1, cols]
        cumulative = 0.5 * (1.0 + lax.erf(upper * (1.0 / math.sqrt(2.0))))
        density = jnp.exp(-0.5 * upper * upper) * (1.0 / math.sqrt(2.0 * math.pi))
        active[:, cols] = (upper * cumulative).astype(bf16)
        slope[:, cols] = (cumulative + upper * density).astype(bf16)
        for j, (part, out) in enumerate(((active, active_out), (slope, slope_out))):
            leaving.append(begin(part.at[:, cols], out.at[:, cols], out_sems.at[4 * j + i]))
    wait_all(second)
    for i in range(width // 256):
        cols = slice(256 * i, 256 * (i + 1))
        result = dot_nn(active[...], down[:, cols])
        p_own[:, cols] = result[:half]
        p_send[:, cols] = result[half:].astype(bf16)
    wait_all(leaving)


def feed(k, order, own, peer, bias, shards, after):
    half, width = own.shape
    return kernel_call(
        functools.partial(feed_kernel, k),
        [SMEM] + [VMEM] * 2 + [KEEP] + [HBM] * 9,
        [
            shape_of((half, width), f32),
            shape_of((half, width), bf16),
            Stored((2 * half, width), bf16),
            Stored((2 * half, width), bf16),
            Stored((2 * half, width), bf16),
        ],
        (order, own, peer, bias, *shards),
        [
            pltpu.VMEM((2 * half, width), bf16),
            pltpu.VMEM((2 * half, width), bf16),
            pltpu.VMEM((2 * half, width), bf16),
            pltpu.VMEM((width, width), bf16),
            pltpu.VMEM((width, width), bf16),
            pltpu.SemaphoreType.DMA((2, 9)),
            pltpu.SemaphoreType.DMA((9,)),
        ],
        after=after,
    )


def feed_back_kernel(order, own, peer, slope_in, *refs):
    shards, (p_own, p_send, grads, sums, slope, g, up, down, sems, slope_sem) = refs[:9], refs[9:]
    half, width = own.shape
    first, second = feed_copies(order, shards, width, up, down, sems)
    start_all(second[:2])
    arriving = begin(slope_in, slope, slope_sem.at[0])
    start_all(second[2:])
    start_all(first)
    g[:half] = own[...]
    g[half:] = peer[...]
    for j in range(0, BLOCKS, 2):
        wait_all(second[j : j + 2])
        if j == 0:
            arriving.wait()
        places = [pl.ds(pl.multiple_of(order[j + i] * LANES, LANES), LANES) for i in range(2)]
        rows = jnp.concatenate([down[p, :] for p in places], axis=0)
        slopes = jnp.concatenate([slope[:, p] for p in places], axis=1)
        grad = (dot_nt(g[...], rows) * slopes.astype(f32)).astype(bf16)
        total = jnp.sum(grad.astype(f32), axis=0, keepdims=True)
        for i, p in enumerate(places):
            grads[:, p] = grad[:, LANES * i : LANES * (i + 1)]
            sums[0:1, p] = total[:, LANES * i : LANES * (i + 1)]
    wait_all(first)
    for i in range(width // 256):
        cols = slice(256 * i, 256 * (i + 1))
        result = dot_nt(grads[...], up[cols, :])
        p_own[:, cols] = result[:half]
        p_send[:, cols] = result[half:].astype(bf16)


def feed_back(order, own, peer, slope, shards, after):
    half, width = own.shape
    return kernel_call(
        feed_back_kernel,
        [SMEM] + [VMEM] * 2 + [HBM] * 10,
        [
            shape_of((half, width), f32),
            shape_of((half, width), bf16),
            shape_of((2 * half, width), bf16),
            kept((8, width), f32),
        ],
        (order, own, peer, slope, *shards),
        [
            pltpu.VMEM((2 * half, width), bf16),
            pltpu.VMEM((2 * half, width), bf16),
            pltpu.VMEM((width, width), bf16),
            pltpu.VMEM((width, width), bf16),
            pltpu.SemaphoreType.DMA((2, 9)),
            pltpu.SemaphoreType.DMA((4,)),
        ],
        after=after,
    )


def norm_rows(resid):
    average = jnp.mean(resid, axis=1, keepdims=True)
    centred = resid - average
    variance = jnp.mean(centred * centred, axis=1, keepdims=True)
    inverse = lax.rsqrt(variance + norm_eps)
    return centred * inverse, inverse


def norm_back_rows(grad_out, normed, inverse, gain):
    scaled = grad_out * gain
    return inverse * (
        scaled
        - jnp.mean(scaled, axis=1, keepdims=True)
        - normed * jnp.mean(scaled * normed, axis=1, keepdims=True)
    )


def add_sums(sums, first, grad_branch, grad_out, normed):
    terms = [grad_branch.astype(f32), grad_out * normed, grad_out]
    for row, term in enumerate(terms):
        total = jnp.sum(term, axis=0, keepdims=True)
        sums[row : row + 1, :] = total if first else sums[row : row + 1, :] + total


def fetch_kernel(k, with_cot, prev, tails, *refs):
    base, tail = refs[with_cot : with_cot + 2]
    tail[...] = tails[k]
    base[...] = prev[: base.shape[0]].astype(f32) + tails[k, 0:1, :]
    if with_cot:
        refs[3][...] = refs[0][...]


def fetch(k, prev, tails, cot, half, after):
    width = prev.shape[1]
    with_cot = cot is not None
    outs = [shape_of((half, width), f32), shape_of((8, width), f32)]
    return kernel_call(
        functools.partial(fetch_kernel, k, int(with_cot)),
        [KEEP] * (2 + with_cot),
        outs + [shape_of((half, width), bf16)] * with_cot,
        (prev, tails) + ((cot,) if with_cot else ()),
        after=after,
    )


def norm_kernel(base, tail, mine, theirs, out, normed_out, inverse_out, normed, inverse, sems):
    step = LANES
    leaving = []
    for r in range(mine.shape[0] // step):
        rows = slice(step * r, step * (r + 1))
        branch = mine[rows].astype(f32) + theirs[rows].astype(f32)
        value, inv = norm_rows(base[rows] + branch)
        normed[rows] = value.astype(bf16)
        inverse[rows] = jnp.broadcast_to(inv, (step, LANES))
        leaving.append(begin(normed.at[rows], normed_out.at[rows], sems.at[0, r]))
        leaving.append(begin(inverse.at[rows], inverse_out.at[rows], sems.at[1, r]))
        out[rows] = (value * tail[1:2] + tail[2:3]).astype(bf16)
    wait_all(leaving)


def norm(base, tail, mine, theirs, after):
    half, width = mine.shape
    return kernel_call(
        norm_kernel,
        [VMEM] * 4,
        [shape_of((half, width), bf16), Stored((half, width), bf16), Stored((half, LANES), f32)],
        (base, tail, mine, theirs),
        [
            pltpu.VMEM((half, width), bf16),
            pltpu.VMEM((half, LANES), f32),
            pltpu.SemaphoreType.DMA((2, half // LANES)),
        ],
        after=after,
    )


def turn_kernel(ids, base, tail, cot, mine, theirs, picked, grad_out_resid, grad_branch, sums, *scratch):
    out, grad_resid, sems = scratch
    step = LANES
    leaving = []
    for r in range(mine.shape[0] // step):
        rows = slice(step * r, step * (r + 1))
        branch = mine[rows].astype(f32) + theirs[rows].astype(f32)
        value, inv = norm_rows(base[rows] + branch)
        out[rows] = (value * tail[1:2] + tail[2:3]).astype(bf16)
        grad_out = cot[rows].astype(f32)
        grad = norm_back_rows(grad_out, value, inv, tail[1:2])
        low = grad.astype(bf16)
        grad_resid[rows] = grad
        leaving.append(begin(grad_resid.at[rows], grad_out_resid.at[rows], sems.at[r]))
        grad_branch[rows] = low
        add_sums(sums, r == 0, low, grad_out, value)
    pick_rows(ids, out, picked)
    wait_all(leaving)


def pick_rows(ids, value, picked):
    count = picked.shape[1]
    for seq in range(picked.shape[0]):
        start = pl.multiple_of(2 * count * seq + count * (ids[0] // 2), count)
        picked[seq] = value[pl.ds(start, count), :]


def turn(ids, base, tail, cot, mine, theirs, seqs, after):
    half, width = mine.shape
    return kernel_call(
        turn_kernel,
        [SMEM] + [VMEM] * 5,
        [
            kept((seqs, half // seqs // 2, width), bf16),
            Stored((half, width), f32),
            shape_of((half, width), bf16),
            kept((8, width), f32),
        ],
        (ids, base, tail, cot, mine, theirs),
        [
            pltpu.VMEM((half, width), bf16),
            pltpu.VMEM((half, width), f32),
            pltpu.SemaphoreType.DMA((half // LANES,)),
        ],
        after=after,
    )


def fetch_back_kernel(k, above_in, normed_in, inverse_in, tails, above, normed, inverse, tail):
    above[...] = above_in[...]
    normed[...] = normed_in[...]
    inverse[...] = inverse_in[...]
    tail[...] = tails[k]


def fetch_back(k, above, normed, inverse, tails, after):
    half, width = above.shape
    return kernel_call(
        functools.partial(fetch_back_kernel, k),
        [KEEP] * 4,
        [
            shape_of((half, width), f32),
            shape_of((half, width), bf16),
            shape_of((half, LANES), f32),
            shape_of((8, width), f32),
        ],
        (above, normed, inverse, tails),
        after=after,
    )


def norm_back_kernel(timed, above, normed, inverse, tail, mine, theirs, *refs):
    scale, refs = (refs[0], refs[1:]) if timed else (None, refs)
    resid_out, grad_branch, sums, grad_resid, sems = refs
    step = LANES
    leaving = []
    for r in range(above.shape[0] // step):
        rows = slice(step * r, step * (r + 1))
        grad_in = above[rows] + (mine[rows].astype(f32) + theirs[rows].astype(f32))
        grad_out = grad_in.astype(bf16).astype(f32)
        value = normed[rows].astype(f32)
        grad = norm_back_rows(grad_out, value, inverse[rows, 0:1], tail[1:2])
        low = grad.astype(bf16)
        grad_resid[rows] = grad
        leaving.append(begin(grad_resid.at[rows], resid_out.at[rows], sems.at[r]))
        grad_branch[rows] = low
        add_sums(sums, r == 0, low, grad_out, value)
        if timed:
            part = jnp.sum(grad, axis=0, keepdims=True)
            for row, term in ((3, part * scale[r]), (4, part)):
                sums[row : row + 1, :] = term if r == 0 else sums[row : row + 1, :] + term
    wait_all(leaving)


def norm_back(above, normed, inverse, tail, mine, theirs, scale, after):
    half, width = above.shape
    timed = scale is not None
    return kernel_call(
        functools.partial(norm_back_kernel, timed),
        [VMEM] * 6 + [SMEM] * timed,
        [Stored((half, width), f32), shape_of((half, width), bf16), kept((8, width), f32)],
        (above, normed, inverse, tail, mine, theirs) + ((scale,) if timed else ()),
        [pltpu.VMEM((half, width), f32), pltpu.SemaphoreType.DMA((half // LANES,))],
        after=after,
    )


def finish_kernel(ids, above, mine, theirs, picked, grad_in):
    grad_in[...] = above[...] + (mine[...].astype(f32) + theirs[...].astype(f32))
    pick_rows(ids, grad_in, picked)


def finish(ids, above, mine, theirs, seqs, after):
    half, width = above.shape
    (picked,) = kernel_call(
        finish_kernel,
        [SMEM, KEEP, VMEM, VMEM],
        [kept((seqs, half // seqs // 2, width), f32)],
        (ids, above, mine, theirs),
        [pltpu.VMEM((half, width), f32)],
        after=after,
    )
    return picked


def join_kernel(own, other, out):
    out[...] = (own[...] + other[...].astype(f32)).astype(bf16)


def join(own, other, after):
    (out,) = kernel_call(
        join_kernel, [VMEM] * 2, [shape_of(own.shape, bf16)], (own, other), after=after
    )
    return out


def prepare_kernel(ids, scale, inputs, cot, vec, hidden, own, peer, cot_own, tails, bias):
    section = ids[0]
    core = section % 2
    seqs, length, width = inputs.shape
    quarter = length // 4
    mul, add = vec[0, 2:3, :], vec[0, 3:4, :]
    for seq in range(seqs):
        embedding = scale[seq] * mul + add
        for y in range(2):
            at = slice((2 * seq + y) * quarter, (2 * seq + y + 1) * quarter)
            mine = pl.ds(pl.multiple_of((2 * y + core) * quarter, quarter), quarter)
            other = pl.ds(pl.multiple_of((2 * y + 1 - core) * quarter, quarter), quarter)
            value = inputs[seq, mine, :].astype(f32) + embedding
            hidden[at] = value
            own[at] = value.astype(bf16)
            peer[at] = (inputs[seq, other, :].astype(f32) + embedding).astype(bf16)
            cot_own[at] = cot[seq, mine, :]
    for k in range(SECTIONS):
        tails[k, 0:3, :] = vec[k, 4:7, :]
        if k % 2 == 0:
            bias[k : k + 1, :] = jnp.zeros((1, width), f32)
            for g in range(2):
                cols = pl.ds(pl.multiple_of(512 * g + LANES * section, LANES), LANES)
                for i in range(2):
                    at = 512 * i + LANES * g
                    bias[k : k + 1, at : at + LANES] = vec[k, i : i + 1, cols]
        else:
            for g in range(8):
                cols = pl.ds(pl.multiple_of(512 * (g % 2) + LANES * section, LANES), LANES)
                bias[k : k + 1, LANES * g : LANES * (g + 1)] = vec[k, g // 2 : g // 2 + 1, cols]


def prepare(ids, scale, inputs, cot, vec, after):
    seqs, length, width = inputs.shape
    half = seqs * length // 2
    return kernel_call(
        prepare_kernel,
        [SMEM] * 2 + [KEEP] * 3,
        [
            kept((half, width), f32),
            shape_of((half, width), bf16),
            shape_of((half, width), bf16),
            kept((half, width), bf16),
            kept((SECTIONS, 8, width), f32),
            kept((SECTIONS, width), f32),
        ],
        (ids, scale, inputs, cot, vec),
        after=after,
    )


def open_kernel(order, *refs):
    shards, (vec, parts, sems) = refs[:8], refs[8:]
    copies = []
    for j in range(BLOCKS):
        first = LANES if j < BLOCKS - 1 else LANES // 2
        copies.append(
            pltpu.make_async_copy(shards[j].at[pl.ds(first, 16), :], parts.at[j], sems.at[j])
        )
    start_all(copies)
    wait_all(copies)
    for j in range(BLOCKS):
        value = parts[j].astype(f32)
        cols = pl.ds(pl.multiple_of(order[j] * LANES, LANES), LANES)
        for k in range(SECTIONS):
            for i in range(7):
                vec[k, i : i + 1, cols] = value[k : k + 1, LANES * i : LANES * (i + 1)]


def open_vectors(order, shards, after):
    width = shards[0].shape[1]
    (vec,) = kernel_call(
        open_kernel,
        [SMEM] + [HBM] * 8,
        [kept((SECTIONS, 8, width), f32)],
        (order, *shards[:7], shards[8]),
        [pltpu.VMEM((BLOCKS, 16, width), bf16), pltpu.SemaphoreType.DMA((BLOCKS,))],
        after=after,
    )
    return vec


def fill_terms(section, k, head, tail, terms):
    terms[...] = jnp.zeros_like(terms)
    if k % 2 == 0:
        for g in range(2):
            cols = pl.ds(pl.multiple_of(512 * g + LANES * section, LANES), LANES)
            for i in range(2):
                at = 512 * i + LANES * g
                terms[i : i + 1, cols] = head[0:1, at : at + LANES]
        if k == 0:
            terms[2:4, :] = head[1:3, :] + 0.5 * tail[3:5, :]
    else:
        for g in range(8):
            cols = pl.ds(pl.multiple_of(512 * (g % 2) + LANES * section, LANES), LANES)
            terms[g // 2 : g // 2 + 1, cols] = head[0:1, LANES * g : LANES * (g + 1)]
    terms[4:7, :] = 0.5 * tail[0:3, :]


def cut_kernel(kind, ids, first, second, *outs):
    sems = outs[4]
    section = ids[0]
    rows = first.shape[0]

    @pl.when(section % 2 == kind)
    def _():
        copies = []
        for r in range(SECTIONS):
            at = section ^ r
            for g in range(8):
                cols = pl.ds(pl.multiple_of(512 * g + LANES * at, LANES), LANES)
                copies.append(
                    pltpu.make_async_copy(
                        first.at[:, cols],
                        outs[r].at[pl.ds(0, rows), pl.ds(LANES * g, LANES)],
                        sems.at[r, g],
                    )
                )
            if kind:
                piece = pl.ds(pl.multiple_of(LANES * at, LANES), LANES)
                copies.append(
                    pltpu.make_async_copy(
                        second.at[piece, :], outs[r].at[pl.ds(rows, LANES), :], sems.at[r, 8]
                    )
                )
        start_all(copies)
        wait_all(copies)


def cut(kind, ids, first, second, after):
    rows, width = first.shape[0], second.shape[1]
    return kernel_call(
        functools.partial(cut_kernel, kind),
        [SMEM] + [HBM] * 2,
        [shape_of((rows + LANES * kind, width), bf16)] * 4,
        (ids, first, second),
        [pltpu.SemaphoreType.DMA((SECTIONS, 9))],
        after=after,
    )


def choose_kernel(base, joined, ids, *refs):
    pieces, refs = refs[:4], refs[4:]
    vectors, refs = (refs[0], refs[1:]) if joined else (None, refs)
    outs, sems = refs[:2], refs[2]
    rows = pieces[0].shape[0]
    for i in range(2):
        at = ids[0] ^ (base + 2 * i)
        for r in range(SECTIONS):

            @pl.when(at == r)
            def _():
                target = outs[i].at[pl.ds(0, rows), :]
                pltpu.make_async_copy(pieces[r], target, sems.at[i]).start()

    if joined:
        width = outs[0].shape[1]
        value = vectors[...].astype(f32)
        lines = [
            jnp.concatenate(
                [value[k, i : i + 1, :] for i in range(7)] + [jnp.zeros((1, width - 7 * LANES), f32)],
                axis=1,
            )
            for k in range(SECTIONS)
        ]
        lines.append(jnp.zeros((16 - SECTIONS, width), f32))
        outs[0][rows:, :] = jnp.concatenate(lines, axis=0).astype(bf16)

    for i in range(2):
        target = outs[i].at[pl.ds(0, rows), :]
        pltpu.make_async_copy(pieces[0], target, sems.at[i]).wait()


def choose(ids, base, pieces, vectors, after):
    rows, width = pieces[0].shape
    joined = vectors is not None
    return kernel_call(
        functools.partial(choose_kernel, base, joined),
        [SMEM] + [ANY] * 4 + [VMEM] * joined,
        [shape_of((rows + 16 * joined, width), bf16), shape_of((rows, width), bf16)],
        (ids, *pieces) + ((vectors,) if joined else ()),
        [pltpu.SemaphoreType.DMA((2,))],
        after=after,
    )


def step_kernel(kind, right, left, ahead, behind, *outs):
    if kind == "last":
        total = ahead[...].astype(f32) + right[...].astype(f32) + left[...].astype(f32)
        outs[0][...] = total.astype(bf16)
    elif kind == "first":
        mid = right.shape[0]
        outs[0][:mid] = ahead[:mid] + right[...]
        outs[0][mid:] = ahead[mid:]
        outs[1][:mid] = behind[:mid]
        outs[1][mid:] = behind[mid:] + left[...]
    else:
        outs[0][...] = ahead[...] + right[...]
        outs[1][...] = behind[...] + left[...]


def ring_step(kind, right, left, ahead, behind, after):
    count = 1 if kind == "last" else 2
    return kernel_call(
        functools.partial(step_kernel, kind),
        [VMEM, VMEM, KEEP, KEEP],
        [shape_of(ahead.shape, bf16)] * count,
        (right, left, ahead, behind),
        after=after,
    )


def place_kernel(ids, *refs):
    feed_pieces, attn_pieces, (first, second, vec) = refs[:4], refs[4:8], refs[8:]
    section = ids[0]
    rows, width = first.shape[0], second.shape[1]

    def columns(r, piece, start):
        at = section ^ r
        for g in range(8):
            cols = pl.ds(pl.multiple_of(512 * g + LANES * at, LANES), LANES)
            first[:, cols] = piece[start : start + rows, LANES * g : LANES * (g + 1)].astype(f32)

    def vector_rows(pieces, start, low, high, pick_high):
        total = None
        for piece in pieces:
            extra = piece[start : start + 16, :].astype(f32)
            total = extra if total is None else total + extra
        line = jnp.where(pick_high, total[high : high + 1, :], total[low : low + 1, :])
        for j in range(7):
            vec[j] = line[:, LANES * j : LANES * (j + 1)]

    @pl.when(section % 2 == 1)
    def _():
        for r in range(SECTIONS):
            columns(r, feed_pieces[r], 0)
            at = pl.ds(pl.multiple_of((section ^ r) * LANES, LANES), LANES)
            second[at, :] = feed_pieces[r][rows : rows + LANES, :].astype(f32)
        vector_rows(feed_pieces, rows + LANES, 0, 2, section == 3)

    @pl.when(section % 2 == 0)
    def _():
        for r in range(SECTIONS):
            columns(r, attn_pieces[r], 16)
        vector_rows(attn_pieces, 0, 0, 1, section == 2)
        second[...] = jnp.zeros_like(second)


def place(ids, feed_pieces, attn_pieces):
    width = attn_pieces[0].shape[1]
    return kernel_call(
        place_kernel,
        [SMEM] + [VMEM] * 8,
        [
            kept((LANES, 4 * width), f32),
            kept((SECTIONS * LANES, width), f32),
            kept((7, 1, LANES), f32),
        ],
        (ids, *feed_pieces, *attn_pieces),
        limit=20,
    )


def over_section(value, r, sources=range(SECTIONS), targets=range(SECTIONS)):
    route = [(i, i ^ r) for i in range(SECTIONS) if i in sources and (i ^ r) in targets]
    return lax.ppermute(value, "section", route)


def ring_of(n):
    return list(range(0, n, 2)) + list(range(n - 1, 0, -2))


def around(value, way):
    ring = ring_of(lax.axis_size("batch"))
    n = len(ring)
    return lax.ppermute(value, "batch", [(ring[i], ring[(i + way) % n]) for i in range(n)])


def ring_gather(shard, name, after=()):
    with jax.named_scope(name):
        return ring_gather_steps(shard, after)


def ring_gather_steps(shard, after):
    out, right, left = [shard], shard, shard
    for i in range(3):
        right, left = around(right, 1), around(left, -1)
        if i == 0 and after:
            right, left = gate((right, left), after)
        out += [right, left]
    mid = shard.shape[0] // 32 * 16
    return out + [around(right[:mid], 1), around(left[mid:], -1)]


class Reduction:
    def __init__(self, chunks, name):
        self.chunks, self.name, self.at = chunks, name, 0
        self.sending = (chunks[4], chunks[8])

    def step(self, after):
        chunks, at = self.chunks, self.at
        with jax.named_scope(self.name):
            right, left = around(self.sending[0], 1), around(self.sending[1], -1)
            kind = ("first", "middle", "middle", "last")[at]
            ahead, behind = ((3, 5), (2, 6), (1, 7), (0, 0))[at]
            self.sending = tuple(
                ring_step(kind, right, left, chunks[ahead], chunks[behind], tuple(after))
            )
        self.at += 1
        return self.sending


class Gathering:
    def __init__(self, shard, name):
        self.name = name
        self.blocks = [shard]
        with jax.named_scope(name):
            right, left = shard, shard
            for _ in range(2):
                right, left = around(right, 1), around(left, -1)
                self.blocks += [right, left]

    def finish(self, after):
        with jax.named_scope(self.name):
            right, left = gate(tuple(self.blocks[3:5]), after)
            self.blocks[3:5] = [right, left]
            right, left = around(right, 1), around(left, -1)
            mid = right.shape[0] // 32 * 16
            self.blocks += [right, left, around(right[:mid], 1), around(left[mid:], -1)]
        return self.blocks


def ring_tables():
    ring = ring_of(BLOCKS)
    place = [ring.index(b) for b in range(BLOCKS)]
    steps = [0, -1, 1, -2, 2, -3, 3, 4]
    order = [[ring[(place[b] + k) % BLOCKS] for k in steps] for b in range(BLOCKS)]
    slots = [[ring[(place[b] + j) % BLOCKS] for j in range(BLOCKS)] for b in range(BLOCKS)]
    return order, slots


def double_gather(value, axis, dim):
    size, index = lax.axis_size(axis), lax.axis_index(axis)
    step = 1
    while step < size:
        other = lax.ppermute(value, axis, [(i, i ^ step) for i in range(size)])
        lower = (index // step) % 2 == 0
        value = jnp.where(
            lower,
            jnp.concatenate([value, other], axis=dim),
            jnp.concatenate([other, value], axis=dim),
        )
        step *= 2
    return value


def halve_reduce(value, axis, dim):
    size, index = lax.axis_size(axis), lax.axis_index(axis)
    step = size // 2
    while step >= 1:
        low, high = jnp.split(value, 2, axis=dim)
        lower = (index // step) % 2 == 0
        send, keep = jnp.where(lower, high, low), jnp.where(lower, low, high)
        value = keep + lax.ppermute(send, axis, [(i, i ^ step) for i in range(size)])
        step //= 2
    return value


def spread(parts, section_id, first):
    stacked = parts
    sources = (first, first + 2)
    pieces = [lax.dynamic_index_in_dim(stacked, section_id, 0, keepdims=False)]
    for r in (1, 2, 3):
        piece = lax.dynamic_index_in_dim(stacked, section_id ^ r, 0, keepdims=False)
        pieces.append(over_section(piece, r, sources=sources))
    return [lax.select_n(section_id ^ k, *pieces) for k in sources]


def local(inputs, segments, timestep, weight_in, weight_out, vectors, cotangent):
    section_id = lax.axis_index("section")
    batch_id = lax.axis_index("batch")
    batch = lax.axis_size("batch")
    ringed = batch == BLOCKS
    core_id = section_id % 2
    seqs, length, width = inputs.shape
    half = seqs * length // 2
    hidden_width = weight_in.shape[2]
    rows = weight_in.shape[1]
    unit = hidden_width // batch // SECTIONS
    ids = jnp.stack([section_id, batch_id]).astype(jnp.int32)
    scale = timestep.astype(f32) / STEPS

    if ringed:
        place_id = jnp.where(batch_id % 2 == 0, batch_id // 2, BLOCKS - 1 - batch_id // 2)

        def neighbours(steps):
            at = (place_id + BLOCKS + jnp.asarray(steps, jnp.int32)) % BLOCKS
            return jnp.where(at < BLOCKS // 2, 2 * at, 2 * BLOCKS - 1 - 2 * at).astype(jnp.int32)

        order, slots = neighbours([0, -1, 1, -2, 2, -3, 3, 4]), neighbours(list(range(BLOCKS)))
    else:
        order = slots = jnp.arange(BLOCKS, dtype=jnp.int32)

    if ringed:

        def sent(group, sources):
            with jax.named_scope(f"spread_{sources[0]}"):
                return [group[0]] + [over_section(group[r], r, sources=sources) for r in (1, 2, 3)]

        with jax.named_scope("vectors"):
            section_vectors = double_gather(vectors, "section", 0)
        attn_pieces = sent(cut(0, ids, weight_in[0], weight_out[0], ()), (0, 2))
        attn_shards = choose(ids, 0, attn_pieces, section_vectors, ())
        first_weights = ring_gather(attn_shards[0], "gather_0")
        feed_pieces = sent(cut(1, ids, weight_in[0], weight_out[0], (attn_shards[1],)), (1, 3))
    else:
        by_head = weight_in[0].reshape(rows, -1, SECTIONS, LANES).transpose(2, 0, 1, 3)
        by_head = by_head.reshape(SECTIONS, rows, width)
        by_unit = weight_in[0].reshape(rows, -1, SECTIONS, unit).transpose(2, 0, 1, 3)
        by_unit = by_unit.reshape(SECTIONS, rows, width)
        down_parts = weight_out[0].reshape(SECTIONS, unit, width)
        attn_shards = spread(by_head, section_id, 0)
        feed_shards = spread(jnp.concatenate([by_unit, down_parts], axis=1), section_id, 1)

    def gather_attn(shard, k):
        if ringed:
            return ring_gather(shard, f"gather_{k}")
        full = lax.all_gather(shard, "batch", axis=0, tiled=True)
        blocks = list(full.reshape(BLOCKS, LANES, width))
        return blocks[:7] + [blocks[7][: LANES // 2], blocks[7][LANES // 2 :]]

    def gather_feed(shard, k, after=()):
        if ringed:
            return ring_gather(shard, f"gather_{k}", after)
        up = lax.all_gather(shard[:rows], "batch", axis=0, tiled=True).reshape(BLOCKS, LANES, width)
        down = lax.all_gather(shard[rows:], "batch", axis=0, tiled=True).reshape(BLOCKS, LANES, width)
        blocks = [jnp.concatenate([up[j], down[j]], axis=0) for j in range(7)]
        return blocks + [up[7], down[7]]

    if ringed:
        vec = open_vectors(order, first_weights, (first_weights[7],))
    else:
        vec = double_gather(double_gather(vectors, "section", 0), "batch", 2).astype(f32)
        vec = jnp.pad(vec, ((0, 0), (0, 1), (0, 0)))
    hidden, own, peer, cot, tails, bias = prepare(ids, scale, inputs, cotangent, vec, ())
    if ringed:
        first_packed = pack_out(ids, order, first_weights, (own,))
        feed_shards = choose(ids, 1, feed_pieces, None, (first_weights[7], first_weights[8]))
    else:
        first_weights = gather_attn(attn_shards[0], 0)
        first_packed = pack_out(ids, order, first_weights, ())

    weights = [
        first_weights,
        gather_feed(feed_shards[0], 1, (first_packed[0],)),
        gather_attn(attn_shards[1], 2),
        None,
    ]
    if ringed:
        last_ring = Gathering(feed_shards[1], "gather_3")
        weights[3] = last_ring.blocks
    else:
        weights[3] = gather_feed(feed_shards[1], 3)

    def step_of(k, *steps):
        if not ringed:
            return ()
        return tuple(weights[k][2 * i - 1 + j] for i in steps for j in range(2))

    if unit != LANES:
        rest = [
            lax.dynamic_index_in_dim(
                vec[k, 0:4].reshape(-1, SECTIONS, unit), section_id, 1, keepdims=False
            ).reshape(width)
            for k in (1, 3)
        ]
        bias = jnp.stack([bias[0], rest[0], bias[2], rest[1]])

    quarters = jnp.moveaxis(segments.reshape(seqs, 2, 2, length // 4), 2, 0)
    quarters = quarters.reshape(2, seqs, length // 2).astype(f32)
    seg = jnp.where(
        core_id == 0,
        jnp.concatenate([quarters[0], quarters[1]], axis=1),
        jnp.concatenate([quarters[1], quarters[0]], axis=1),
    )

    def exchange(p_own, p_send, after):
        with jax.named_scope("sum_cores"):
            mine = join(p_own, over_section(p_send, 1), after)
        with jax.named_scope("sum_chips"):
            return mine, over_section(mine, 2)

    def to_all(parts):
        with jax.named_scope("turn_out_slices"):
            return (parts[0],) + tuple(over_section(parts[r], r) for r in (1, 2, 3))

    saved = []
    prev = hidden
    for k in range(SECTIONS):
        if k % 2 == 0:
            packed = first_packed if k == 0 else pack_out(ids, order, weights[k], ())
            if k == 2 and ringed:
                weights[3] = last_ring.finish((packed[0],))
            wo = to_all(packed)
            qkv, probs, ctx, ctx_kept, x = attend(
                k, order, own, peer, seg, bias, weights[k], ()
            )
            p_own, p_send = project(ids, ctx, wo, width, step_of(1, 2) if k == 0 else step_of(3, 3))
            held = (x, wo, qkv, probs, ctx_kept)
        else:
            p_own, p_send, active, slope, x = feed(
                k, order, own, peer, bias, weights[k], step_of(2, 1) if k == 1 else ()
            )
            held = (x, active, slope)
        mine, theirs = exchange(p_own, p_send, (step_of(2, 2) + step_of(3, 1)) if k == 1 else ())
        prev = hidden if k == 0 else x
        ahead = fetch(k, prev, tails, cot if k == 3 else None, half, (mine,))
        if k < SECTIONS - 1:
            numbers = (((1, 3),), ((2, 3), (3, 2)), ((3, 4),))[k]
            late = sum((step_of(*n) for n in numbers), ())
            own, normed, inverse = norm(*ahead, mine, theirs, late)
            saved.append((held, normed, inverse))
            with jax.named_scope("other_half"):
                peer = over_section(own, 1)
        else:
            output_part, grad_resid, grad_own, tail_sums = turn(
                ids, *ahead, mine, theirs, seqs, ()
            )
            saved.append((held, None, None))

    def scatter(parts):
        return lax.psum_scatter(
            jnp.concatenate(parts, axis=0), "batch", scatter_dimension=0, tiled=True
        )

    def whole_reduce(k, chunks):
        chunks = list(chunks)
        if k % 2 == 0:
            return scatter(chunks[:4] + [chunks[4], chunks[8]] + chunks[5:8])
        up = [c[:LANES] for c in chunks[:4]] + [chunks[4]] + [c[:LANES] for c in chunks[5:8]]
        down = [c[LANES:] for c in chunks[:4]] + [chunks[8]] + [c[LANES:] for c in chunks[5:8]]
        return jnp.concatenate([scatter(up), scatter(down)], axis=0)

    rings, reduced = [None] * 4, [None] * 4
    heads, tail_list = [None] * 4, [None] * 4

    def steps(numbers, after):
        if not ringed:
            return ()
        found = []
        for k in numbers:
            found += rings[k].step(after)
        return tuple(found)

    def weight_ring(k, chunks):
        if ringed:
            rings[k] = Reduction(chunks, f"reduce_{k}")
        else:
            reduced[k] = whole_reduce(k, chunks)

    waiting = []
    for k in range(SECTIONS - 1, -1, -1):
        held, _, _ = saved[k]
        tail_list[k] = tail_sums
        with jax.named_scope("other_half"):
            grad_peer = over_section(grad_own, 1)
        before_join, before_norm = (((1,), (1,)), ((3,), (3,)), ((), (3,)), ((), (3,)))[k]
        early = steps((1,), (grad_own,)) if k == 0 else ()
        if k % 2 == 0:
            x, wo, qkv, probs, ctx = held
            if k == 0:
                packed = out_grad(ids, grad_own, grad_peer, ctx, ())
                wo_grad = to_all(packed)
            p_own, p_send, grads, sums = attend_back(
                ids,
                order,
                grad_own,
                grad_peer,
                wo,
                qkv,
                probs,
                weights[k],
                scale if k == 0 else None,
                (packed[0], *early) if k == 0 else (),
            )
            late = steps(before_join, (p_send,))
            if k == 0:
                late = (*late, *wo_grad[1:])
            mine, theirs = exchange(p_own, p_send, late)
            if k != 0:
                packed = out_grad(ids, grad_own, grad_peer, ctx, (mine,))
                wo_grad = to_all(packed)
            work = [("attend", (x, grads, ids, *wo_grad))]
        else:
            x, active, slope = held
            p_own, p_send, grads, sums = feed_back(
                order, grad_own, grad_peer, slope, weights[k], wo_grad[1:] if k == 1 else ()
            )
            late = steps(before_join, (p_send,))
            mine, theirs = exchange(p_own, p_send, late)
            work = [("feed", (x, grads, grad_own, grad_peer, active))]
        heads[k] = sums

        def shares(numbers):
            if not ringed:
                return []
            return [(numbers, (ids, *[a for n in numbers for a in (heads[n], tail_list[n])]))]

        fence = (mine,)
        if k == 2 and ringed:
            waiting = work
        else:
            if k == 1:
                work = work + shares((1, 2, 3))
            elif k == 0:
                work = shares((0,)) + work
            chunks = weight_grads(slots, work + waiting, (mine,), k != 1)
            weight_ring(k, chunks)
            waiting = []
            if k == 0:
                fence = (mine, chunks[0])
        if k == 0:
            first_step = steps((0,), fence)
            fence = (mine, *first_step[:1])
        late = steps(before_norm, fence)
        if k == 2:
            late = (*late, packed[0])
        if k > 0:
            _, normed, inverse = saved[k - 1]
            ahead = fetch_back(k - 1, grad_resid, normed, inverse, tails, (mine,))
            grad_resid, grad_own, tail_sums = norm_back(
                *ahead, mine, theirs, scale if k == 1 else None, late
            )
        else:
            input_part = finish(ids, grad_resid, mine, theirs, seqs, late)
    if ringed:
        last = (input_part,)
        for k in (1, 0, 0, 0):
            last = steps((k,), (last[0],))
        both = rings[1].sending[0]
        cut_at = 2 * rows + 16
        upper = jnp.concatenate([rings[3].sending[0], both[2 * rows : cut_at]], axis=0)
        reduced = [rings[0].sending[0], both[:cut_at], both[2 * rows :], upper]

    def to_owner(k, r):
        return jnp.where((section_id ^ r) == k, reduced[k], reduced[k + 2])

    def pieces_of(k):
        found = [to_owner(k, 0)]
        return found + [over_section(to_owner(k, r), r, targets=(k, k + 2)) for r in (1, 2, 3)]

    with jax.named_scope("collect"):
        feed_pieces, attn_pieces = pieces_of(1), pieces_of(0)
    if unit == LANES:
        first, second, terms = place(ids, feed_pieces, attn_pieces)
        terms = terms.transpose(1, 0, 2)
    else:
        odd = section_id % 2 == 1
        first_pieces = [jnp.where(odd, f[:rows], a) for f, a in zip(feed_pieces, attn_pieces)]
        slices = [lax.select_n(section_id ^ s, *first_pieces) for s in range(SECTIONS)]
        first = jnp.stack([p.reshape(rows, -1, LANES) for p in slices], axis=2)
        first = first.reshape(rows, hidden_width)
        if unit != LANES:
            other = jnp.stack([p.reshape(rows, -1, unit) for p in slices], axis=2)
            first = jnp.where(odd, other.reshape(rows, hidden_width), first)
        second = jnp.stack(
            [lax.select_n(section_id ^ s, *[f[rows:] for f in feed_pieces]) for s in range(SECTIONS)]
        )
        second = jnp.where(odd, second.reshape(SECTIONS * unit, width).astype(f32), 0.0)

    if unit != LANES:
        empty_row = jnp.zeros((2, width), f32)
        time_sums = heads[0][1:3] + 0.5 * tail_list[0][3:5]
        terms = []
        for k in range(SECTIONS):
            if k % 2 == 0:

                def placed(piece):
                    empty = jnp.zeros((2, SECTIONS, LANES), f32)
                    piece = piece.reshape(2, 1, LANES)
                    full = lax.dynamic_update_slice_in_dim(empty, piece, section_id, 1)
                    return full.reshape(1, width)

                head = [placed(heads[k][0, :256]), placed(heads[k][0, 512:768])]
                head.append(time_sums if k == 0 else empty_row)
            else:
                empty = jnp.zeros((width // unit, SECTIONS, unit), f32)
                piece = heads[k][0].reshape(width // unit, 1, unit)
                full = lax.dynamic_update_slice_in_dim(empty, piece, section_id, 1)
                head = [full.reshape(4, width)]
            terms.append(jnp.concatenate(head + [0.5 * tail_list[k][:3]], axis=0))
        with jax.named_scope("vectors_back"):
            terms = halve_reduce(halve_reduce(jnp.stack(terms), "section", 0), "batch", 2)
    return (output_part, input_part, first.astype(f32)[None], second[None], terms)


def solution(mesh):
    return jax.shard_map(
        local,
        mesh=mesh,
        in_specs=(
            P("batch", None, None),
            P("batch", None),
            P("batch"),
            P("section", "batch", None),
            P("section", "batch", None),
            P("section", None, "batch"),
            P("batch", None, None),
        ),
        out_specs=(
            P("batch", "section", None),
            P("batch", "section", None),
            P("section", "batch", None),
            P("section", "batch", None),
            P("section", None, "batch"),
        ),
        check_vma=False,
    )
```
